32 devices in a mesh: rep: 2 (over y), dp: 4 (over z), tensor: 4 (over x, core).
Axes of the slice: x: 2, y: 2, z: 4, core: 2. Of those that a mesh axis runs over, the one named last changes fastest.
Arguments:
- tokens: bfloat16 [3, 1536, 8192], P(None, ('rep', 'dp'), 'tensor'), parts along dimension 1, may hold values from -6 to 6
- query_weight: bfloat16 [8192, 4096], P(None, 'tensor'), may hold values from -0.0625 to 0.0625
- adapter_down_weight: bfloat16 [32, 8192, 64], P('dp', 'tensor'), may hold values from -0.0625 to 0.0625
- adapter_up_weight: bfloat16 [32, 64, 4096], P('dp', None, 'tensor'), may hold values from -0.75 to 0.75
- cached_key_rows: bfloat16 [1536, 4, 48, 128], P(('rep', 'dp'), None, 'tensor'), parts along dimension 0, may hold values from -110 to 110
- cached_value_rows: bfloat16 [1536, 4, 48, 128], P(('rep', 'dp'), None, 'tensor'), parts along dimension 0, may hold values from -6 to 6
- incoming_key_rows: bfloat16 [3, 1536, 4, 128], P(None, ('rep', 'dp')), parts along dimension 1, may hold values from -6 to 6
- incoming_value_rows: bfloat16 [3, 1536, 4, 128], P(None, ('rep', 'dp')), parts along dimension 1, may hold values from -6 to 6
- cached_length_rows: int32 [1536], P(('rep', 'dp')), parts along dimension 0, may hold values from 1 to 48, as said below
- row_adapter_index: int32 [1536], P(('rep', 'dp')), parts along dimension 0, may hold values from 0 to 31, as said below
Outputs:
- attended: bfloat16 [3, 1536, 4096], P(None, ('rep', 'dp'), 'tensor'), parts along dimension 1
The draws below stay inside these ranges and needn't reach their ends.
There are 2 independent parts, one for each index of `rep`. The reference program is written for one: setup_inputs(seed, part) draws one part's arguments, and reference() takes and returns one part's arrays. A program takes and returns all parts, laid end to end along the dimension named above; an argument that names none is the same for every part. Nothing has to cross between parts.
Inputs may be any that keep to these rules, and one draw needn't show every extreme that they name: `cached_length_rows`: group g (rows g * 192 to (g + 1) * 192 - 1) has lengths up to 48 * (g + 1) * 192 // 768, reached by its first row. `row_adapter_index`: adapter a belongs to owner a // 8. Among the 192 rows of one group at most 96 name adapters of one owner, and in every group some owner is named exactly 96 times.
All inputs are finite; a program needn't handle non-finite values.
Results may differ from the reference program's by a relative error of at most 0.011.
Values may be sent and summed in bfloat16 or wider, within the bound.
No kernel may reach another device: no remote copies, remote signals or barrier semaphores. Data moves between devices by JAX's collectives and lax.ppermute only.
A program may use at most 384 MiB of HBM per device.

```python
import jax
import jax.numpy as jnp
from jax import lax

MODEL_WIDTH = 8192
QUERY_HEADS_HALF = 32
KVH = 4
HEAD_WIDTH = 128
ADAPTER_RANK = 64
STEPS = 3
CACHE = 48
ROWS_GRP = 192
ADAPT_DEV = 8
ROWS = 768
ADAPTER_POOL = 32
CAP = 96
N_TENSOR = 4


def draw_cached_key_rows(key, part):
    key = jax.random.fold_in(key, 11)
    return jnp.clip(jax.random.normal(key, (ROWS, KVH, CACHE, HEAD_WIDTH), jnp.float32), -4.0, 4.0).astype(jnp.bfloat16)


def draw_cached_length_rows(key, part):
    key = jax.random.fold_in(key, 5)
    row_index = jnp.arange(ROWS)
    group = row_index // ROWS_GRP
    ceiling = jnp.maximum(1, CACHE * (group + 1) * ROWS_GRP // ROWS)
    drawn = jax.random.randint(key, (ROWS,), 1, ceiling + 1)
    return jnp.where(row_index % ROWS_GRP == 0, ceiling, drawn).astype(jnp.int32)


def draw_row_adapter_index(key, part):
    key = jax.random.fold_in(key, 7)
    groups = ROWS // ROWS_GRP
    first_key, second_key, third_key, fourth_key = jax.random.split(key, 4)
    hottest = jax.random.randint(first_key, (groups,), 0, groups)
    rotation = jax.random.randint(second_key, (groups,), 0, groups - 1)
    counter = jnp.arange(ROWS_GRP)
    others = (hottest[:, None] + 1 + (counter[None, :] - CAP + rotation[:, None]) % (groups - 1)) % groups
    owner_of = jnp.where(counter[None, :] < CAP, hottest[:, None], others)
    ordering = jax.vmap(lambda single: jax.random.permutation(single, ROWS_GRP))(jax.random.split(third_key, groups))
    owner_of = jnp.take_along_axis(owner_of, ordering, axis=1)
    within = jax.random.randint(fourth_key, (groups, ROWS_GRP), 0, ADAPT_DEV)
    return (owner_of * ADAPT_DEV + within).reshape(ROWS).astype(jnp.int32)


def block_scale(rng, dims, cuts, low, high):
    factor_of = 1.0
    for dim, shards_of in cuts:
        draws = jax.random.uniform(jax.random.fold_in(jax.random.fold_in(rng, 6), dim), (shards_of,), jnp.float32, low / len(cuts), high / len(cuts))
        factor_of = factor_of * jnp.repeat(jnp.exp(draws), dims[dim] // shards_of).reshape((-1,) + (1,) * (len(dims) - 1 - dim))
    return factor_of


def bell_draw(rng, shape, spread, bound, pieces=(), held_as=jnp.bfloat16):
    gain = block_scale(rng, shape, pieces, -0.22, 0.18) if pieces else 1.0
    values = jax.random.normal(rng, shape, jnp.float32) * spread * gain
    return jnp.minimum(jnp.maximum(values, -bound), bound).astype(held_as)


def setup_inputs(seed: int = 0, part: int = 0) -> dict:
    keys = jax.random.split(jax.random.key(seed), 11)
    own_keys = jax.random.split(jax.random.fold_in(keys[10], part), 11)
    tokens = bell_draw(own_keys[0], (STEPS, ROWS, MODEL_WIDTH), 1.0, 6.0, ((1, 4), (2, 4)))
    query_weight = bell_draw(keys[1], (MODEL_WIDTH, QUERY_HEADS_HALF * HEAD_WIDTH), MODEL_WIDTH ** -0.5, 0.0625, ((1, 4),))
    adapter_down_weight = bell_draw(keys[2], (ADAPTER_POOL, MODEL_WIDTH, ADAPTER_RANK), MODEL_WIDTH ** -0.5, 0.0625, ((0, 4), (1, 4)))
    adapter_up_weight = bell_draw(keys[3], (ADAPTER_POOL, ADAPTER_RANK, QUERY_HEADS_HALF * HEAD_WIDTH), ADAPTER_RANK ** -0.5, 0.75, ((0, 4), (2, 4)))
    cached_key_rows = draw_cached_key_rows(jax.random.fold_in(jax.random.fold_in(keys[10], part), 71), part)
    cached_value_rows = bell_draw(own_keys[5], (ROWS, KVH, CACHE, HEAD_WIDTH), 1.0, 6.0, ((0, 4), (2, 4)))
    incoming_key_rows = bell_draw(own_keys[6], (STEPS, ROWS, KVH, HEAD_WIDTH), 1.0, 6.0, ((1, 4),))
    incoming_value_rows = bell_draw(own_keys[7], (STEPS, ROWS, KVH, HEAD_WIDTH), 1.0, 6.0, ((1, 4),))
    cached_length_rows = draw_cached_length_rows(jax.random.fold_in(jax.random.fold_in(keys[10], part), 71), part)
    row_adapter_index = draw_row_adapter_index(jax.random.fold_in(jax.random.fold_in(keys[10], part), 71), part)
    return {"tokens": tokens, "query_weight": query_weight, "adapter_down_weight": adapter_down_weight, "adapter_up_weight": adapter_up_weight, "cached_key_rows": cached_key_rows, "cached_value_rows": cached_value_rows, "incoming_key_rows": incoming_key_rows, "incoming_value_rows": incoming_value_rows, "cached_length_rows": cached_length_rows, "row_adapter_index": row_adapter_index}


def head_attention(query_head, key_head, value_head, fresh_keys, fresh_values, visible, block_size):
    step_count = query_head.shape[0]
    row_count = query_head.shape[1]
    group_size = query_head.shape[2]
    head_size = query_head.shape[3]
    block_count = key_head.shape[1] // block_size
    score_scale = head_size ** -0.5
    query_wide = query_head.astype(jnp.float32)
    scores = jnp.einsum("srgd,rpd->srgp", query_wide, key_head.astype(jnp.float32)) * score_scale
    scores = scores.reshape(step_count, row_count, group_size, block_count, block_size)
    visible_blocks = visible.reshape(row_count, block_count, block_size)[None, :, None, :, :]
    block_max = jnp.max(jnp.where(visible_blocks, scores, -jnp.inf), axis=-1)
    safe_max = jnp.where(block_max > -jnp.inf, block_max, 0.0)
    raised = jnp.where(visible_blocks, jnp.exp(scores - safe_max[..., None]), 0.0)
    block_weights = raised.astype(jnp.bfloat16)
    value_blocks = value_head.reshape(row_count, block_count, block_size, head_size).astype(jnp.float32)
    block_numerator = jnp.einsum("srgbp,rbpd->srgbd", block_weights.astype(jnp.float32), value_blocks)
    block_total = jnp.sum(raised, axis=-1)
    fresh_scores = jnp.einsum("srgd,trd->srgt", query_wide, fresh_keys.astype(jnp.float32)) * score_scale
    earlier = jnp.arange(step_count)[None, :] <= jnp.arange(step_count)[:, None]
    step_mask = earlier[:, None, None, :]
    fresh_max = jnp.max(jnp.where(step_mask, fresh_scores, -jnp.inf), axis=-1)
    fresh_raised = jnp.where(step_mask, jnp.exp(fresh_scores - fresh_max[..., None]), 0.0)
    fresh_weights = fresh_raised.astype(jnp.bfloat16)
    fresh_numerator = jnp.einsum("srgt,trd->srgd", fresh_weights.astype(jnp.float32), fresh_values.astype(jnp.float32))
    fresh_total = jnp.sum(fresh_raised, axis=-1)
    overall = jnp.maximum(jnp.max(block_max, axis=-1), fresh_max)
    factor = jnp.exp(block_max - overall[..., None])
    fresh_factor = jnp.exp(fresh_max - overall)
    numerator = jnp.sum(factor[..., None] * block_numerator, axis=3) + fresh_factor[..., None] * fresh_numerator
    total_sum = jnp.sum(factor * block_total, axis=3) + fresh_factor * fresh_total
    return (numerator / total_sum[..., None]).astype(jnp.bfloat16)


def reference(tokens, query_weight, adapter_down_weight, adapter_up_weight, cached_key_rows, cached_value_rows, incoming_key_rows, incoming_value_rows, cached_length_rows, row_adapter_index):
    flat_tokens = tokens.reshape(STEPS * ROWS, MODEL_WIDTH)
    base_query = jnp.dot(flat_tokens, query_weight, preferred_element_type=jnp.float32).reshape(STEPS, ROWS, QUERY_HEADS_HALF * HEAD_WIDTH)

    def row_delta(inputs):
        token_inputs, adapter_choice = inputs
        down_projected = jnp.dot(token_inputs, adapter_down_weight[adapter_choice], preferred_element_type=jnp.float32).astype(jnp.bfloat16)
        return jnp.dot(down_projected, adapter_up_weight[adapter_choice], preferred_element_type=jnp.float32).astype(jnp.bfloat16)

    deltas = lax.map(row_delta, (jnp.transpose(tokens, (1, 0, 2)), row_adapter_index))
    query_rows = (base_query + jnp.transpose(deltas, (1, 0, 2)).astype(jnp.float32)).astype(jnp.bfloat16)
    group_size = QUERY_HEADS_HALF // KVH
    query_heads = query_rows.reshape(STEPS, ROWS, KVH, group_size, HEAD_WIDTH)
    position = jnp.arange(CACHE)
    visible = position[None, :] < cached_length_rows[:, None]
    block_size = CACHE // N_TENSOR

    def one_head(inputs):
        query_head, key_head, value_head, fresh_keys, fresh_values = inputs
        return head_attention(query_head, key_head, value_head, fresh_keys, fresh_values, visible, block_size)

    outputs = lax.map(one_head, (jnp.transpose(query_heads, (2, 0, 1, 3, 4)), jnp.transpose(cached_key_rows, (1, 0, 2, 3)), jnp.transpose(cached_value_rows, (1, 0, 2, 3)), jnp.transpose(incoming_key_rows, (2, 0, 1, 3)), jnp.transpose(incoming_value_rows, (2, 0, 1, 3))))
    return jnp.transpose(outputs, (1, 2, 0, 3, 4)).reshape(STEPS, ROWS, QUERY_HEADS_HALF * HEAD_WIDTH)
```

```python
import functools

import jax
import jax.numpy as jnp
from jax import lax
from jax.experimental import pallas as pl
from jax.experimental.pallas import tpu as pltpu
from jax.sharding import PartitionSpec as P

QUERY_HEADS_HALF = 32
KVH = 4
VMEM_LIMIT = 56 * 1024 * 1024


def general_body(
    tokens,
    query_weight,
    adapter_down_weight,
    adapter_up_weight,
    cached_key_rows,
    cached_value_rows,
    incoming_key_rows,
    incoming_value_rows,
    cached_length_rows,
    row_adapter_index,
):
    step_count = tokens.shape[0]
    row_count = tokens.shape[1]
    width_local = query_weight.shape[1]
    head_size = cached_key_rows.shape[3]
    flat_tokens = tokens.reshape(step_count * row_count, tokens.shape[2])
    base_query = jnp.dot(
        lax.all_gather(flat_tokens, "tensor", axis=1, tiled=True),
        query_weight,
        preferred_element_type=jnp.float32,
    )
    owner_count = lax.axis_size("dp")
    adapter_count = adapter_down_weight.shape[0]
    capacity = 2 * row_count // owner_count
    owner_of = row_adapter_index // adapter_count
    within = row_adapter_index % adapter_count
    member = (owner_of[:, None] == jnp.arange(owner_count)[None, :]).astype(jnp.int32)
    position = jnp.sum(jnp.cumsum(member, axis=0) * member, axis=1) - 1
    slot_index = owner_of * capacity + position
    placing = slot_index[:, None] == jnp.arange(owner_count * capacity)[None, :]
    place_matrix = placing.astype(jnp.bfloat16).reshape(row_count, owner_count, capacity)
    outgoing = jnp.einsum(
        "rok,srd->oskd", place_matrix, tokens, preferred_element_type=jnp.float32
    ).astype(jnp.bfloat16)
    slot_adapter = jnp.sum(placing.astype(jnp.int32) * (within[:, None] + 1), axis=0) - 1
    slot_adapter = jnp.broadcast_to(
        slot_adapter.reshape(owner_count, 1, capacity), (owner_count, step_count, capacity)
    )
    incoming = lax.all_to_all(outgoing, "dp", split_axis=0, concat_axis=0, tiled=True)
    incoming_ids = lax.all_to_all(slot_adapter, "dp", split_axis=0, concat_axis=0, tiled=True)
    sources = incoming.shape[0]
    slot_ids = jnp.maximum(incoming_ids[:, 0], 0).reshape(-1)
    slot_down = jnp.take(adapter_down_weight, slot_ids, axis=0).reshape(
        sources, capacity, adapter_down_weight.shape[1], adapter_down_weight.shape[2]
    )
    partial_rank = jnp.einsum(
        "oskd,okdr->oskr", incoming, slot_down, preferred_element_type=jnp.float32
    )
    summed_rank = lax.psum(partial_rank, "tensor").astype(jnp.bfloat16)
    slot_up = jnp.take(adapter_up_weight, slot_ids, axis=0).reshape(
        sources, capacity, adapter_up_weight.shape[1], adapter_up_weight.shape[2]
    )
    corrections = jnp.einsum(
        "oskr,okrc->oskc", summed_rank, slot_up, preferred_element_type=jnp.float32
    ).astype(jnp.bfloat16)
    returned = lax.all_to_all(corrections, "dp", split_axis=0, concat_axis=0, tiled=True)
    delta_rows = jnp.einsum(
        "rok,oskc->src", place_matrix, returned, preferred_element_type=jnp.float32
    ).astype(jnp.bfloat16)
    delta_rows = delta_rows.reshape(step_count * row_count, width_local)
    query_rows = (base_query + delta_rows.astype(jnp.float32)).astype(jnp.bfloat16)
    query_rows = query_rows.reshape(step_count, row_count, width_local)
    full_query = lax.all_gather(query_rows, "tensor", axis=2, tiled=True)
    group_size = QUERY_HEADS_HALF // KVH
    heads_local = width_local // head_size
    full_heads = full_query.reshape(step_count, row_count, KVH, group_size, head_size)
    score_scale = head_size ** (-0.5)
    block_size = cached_key_rows.shape[2]
    scores = (
        jnp.einsum(
            "srkgd,rkpd->srkgp", full_heads, cached_key_rows, preferred_element_type=jnp.float32
        )
        * score_scale
    )
    cache_position = lax.axis_index("tensor") * block_size + jnp.arange(block_size)
    visible = cache_position[None, :] < cached_length_rows[:, None]
    visible_wide = visible[None, :, None, None, :]
    block_max = jnp.max(jnp.where(visible_wide, scores, -jnp.inf), axis=-1)
    safe_max = jnp.where(block_max > -jnp.inf, block_max, 0.0)
    raised = jnp.where(visible_wide, jnp.exp(scores - safe_max[..., None]), 0.0)
    block_weights = raised.astype(jnp.bfloat16)
    block_numerator = jnp.einsum(
        "srkgp,rkpd->srkgd", block_weights, cached_value_rows, preferred_element_type=jnp.float32
    )
    block_numerator = block_numerator.reshape(step_count, row_count, QUERY_HEADS_HALF, head_size)
    block_total = jnp.sum(raised, axis=-1).reshape(step_count, row_count, QUERY_HEADS_HALF)
    block_max = block_max.reshape(step_count, row_count, QUERY_HEADS_HALF)
    numerator_in, total_in, max_in = (
        lax.all_to_all(block_numerator[None], "tensor", split_axis=3, concat_axis=0, tiled=True),
        lax.all_to_all(block_total[None], "tensor", split_axis=3, concat_axis=0, tiled=True),
        lax.all_to_all(block_max[None], "tensor", split_axis=3, concat_axis=0, tiled=True),
    )
    head_index = lax.axis_index("tensor") * heads_local + jnp.arange(heads_local)
    kv_index = head_index // group_size
    own_keys = jnp.take(incoming_key_rows, kv_index, axis=2)
    own_values = jnp.take(incoming_value_rows, kv_index, axis=2)
    own_query = query_rows.reshape(step_count, row_count, heads_local, head_size)
    fresh_scores = (
        jnp.einsum("srhd,trhd->srht", own_query, own_keys, preferred_element_type=jnp.float32)
        * score_scale
    )
    earlier = jnp.arange(step_count)[None, :] <= jnp.arange(step_count)[:, None]
    step_mask = earlier[:, None, None, :]
    fresh_max = jnp.max(jnp.where(step_mask, fresh_scores, -jnp.inf), axis=-1)
    fresh_raised = jnp.where(step_mask, jnp.exp(fresh_scores - fresh_max[..., None]), 0.0)
    fresh_weights = fresh_raised.astype(jnp.bfloat16)
    fresh_numerator = jnp.einsum(
        "srht,trhd->srhd", fresh_weights, own_values, preferred_element_type=jnp.float32
    )
    fresh_total = jnp.sum(fresh_raised, axis=-1)
    overall = jnp.maximum(jnp.max(max_in, axis=0), fresh_max)
    factor = jnp.exp(max_in - overall[None])
    fresh_factor = jnp.exp(fresh_max - overall)
    numerator = (
        jnp.sum(factor[..., None] * numerator_in, axis=0)
        + fresh_factor[..., None] * fresh_numerator
    )
    total_sum = jnp.sum(factor * total_in, axis=0) + fresh_factor * fresh_total
    attended = (numerator / total_sum[..., None]).astype(jnp.bfloat16)
    return attended.reshape(step_count, row_count, width_local)


def swap(array, bit, count):
    return lax.ppermute(array, "tensor", [(i, i ^ bit) for i in range(count)])


def project_pair(tensor_ids, first, second, weight, earlier=None):
    rows, depth = first.shape
    columns = weight.shape[1]
    chunk = 512
    chunks = depth // chunk

    def kernel(ids_ref, *refs):
        first_ref, first_weight, second_ref, second_weight = refs[:4]
        out_ref = refs[-1]
        product = jnp.dot(
            first_ref[...], first_weight[...], preferred_element_type=jnp.float32
        ) + jnp.dot(second_ref[...], second_weight[...], preferred_element_type=jnp.float32)

        @pl.when(pl.program_id(0) == 0)
        def _():
            out_ref[...] = product if earlier is None else product + refs[4][...]

        @pl.when(pl.program_id(0) > 0)
        def _():
            out_ref[...] += product

    whole = pl.BlockSpec((rows, columns), lambda k, ids: (0, 0))
    in_specs = [
        pl.BlockSpec((rows, chunk), lambda k, ids: (0, k)),
        pl.BlockSpec((chunk, columns), lambda k, ids: (ids[0] * chunks + k, 0)),
        pl.BlockSpec((rows, chunk), lambda k, ids: (0, k)),
        pl.BlockSpec((chunk, columns), lambda k, ids: (ids[1] * chunks + k, 0)),
    ]
    operands = [first, weight, second, weight]
    if earlier is not None:
        in_specs.append(whole)
        operands.append(earlier)
    return pl.pallas_call(
        kernel,
        out_shape=jax.ShapeDtypeStruct((rows, columns), jnp.float32),
        grid_spec=pltpu.PrefetchScalarGridSpec(
            num_scalar_prefetch=1, grid=(chunks,), in_specs=in_specs, out_specs=whole
        ),
        compiler_params=pltpu.CompilerParams(vmem_limit_bytes=VMEM_LIMIT),
        cost_estimate=pl.CostEstimate(
            flops=4 * rows * depth * columns,
            bytes_accessed=4 * depth * (rows + columns) + 4 * rows * columns,
            transcendentals=0,
        ),
        name="project",
    )(tensor_ids, *operands)


def adapter_rank(tokens, row_adapters, gathered_down, owners, per_block):
    rows, depth = tokens.shape
    halves = gathered_down.shape[0]
    rank = gathered_down.shape[3]
    blocks = halves * owners
    width = per_block * rank
    down = gathered_down.reshape(blocks, width, depth)

    def kernel(tokens_ref, adapter_ref, down_ref, out_ref, acc_ref):
        block = pl.program_id(0)
        half, owner = block // owners, block % owners
        product = lax.dot_general(
            tokens_ref[...],
            down_ref[0],
            (((1,), (1,)), ((), ())),
            preferred_element_type=jnp.float32,
        )
        start = owner * (halves * per_block) + half * per_block
        column = lax.broadcasted_iota(jnp.int32, (rows, width), 1) // rank + start
        kept = jnp.where(column == adapter_ref[...], product, 0.0)

        @pl.when(block == 0)
        def _():
            acc_ref[...] = kept

        @pl.when(block > 0)
        def _():
            acc_ref[...] += kept

        @pl.when(block == blocks - 1)
        def _():
            total = acc_ref[:, :128]
            for i in range(1, width // 128):
                total = total + acc_ref[:, i * 128 : (i + 1) * 128]
            out_ref[...] = total[:, :rank] + total[:, rank:]

    return pl.pallas_call(
        kernel,
        out_shape=jax.ShapeDtypeStruct((rows, rank), jnp.float32),
        grid=(blocks,),
        in_specs=[
            pl.BlockSpec((rows, depth), lambda b: (0, 0)),
            pl.BlockSpec((rows, 1), lambda b: (0, 0)),
            pl.BlockSpec((1, width, depth), lambda b: (b, 0, 0)),
        ],
        out_specs=pl.BlockSpec((rows, rank), lambda b: (0, 0)),
        scratch_shapes=[pltpu.VMEM((rows, width), jnp.float32)],
        compiler_params=pltpu.CompilerParams(vmem_limit_bytes=VMEM_LIMIT),
        cost_estimate=pl.CostEstimate(
            flops=2 * rows * depth * width * blocks,
            bytes_accessed=2 * depth * (rows + width * blocks),
            transcendentals=0,
        ),
        name="rank",
    )(tokens, row_adapters, down)


def finish_query(base, ranks, row_adapters, gathered_up, owners, per_block):
    rows, columns = base.shape
    halves = gathered_up.shape[0]
    rank = gathered_up.shape[3]
    blocks = halves * owners
    width = per_block * rank
    up = gathered_up.reshape(blocks, width, columns)

    def kernel(base_ref, rank_ref, adapter_ref, up_ref, out_ref, acc_ref):
        block = pl.program_id(0)
        half, owner = block // owners, block % owners
        start = owner * (halves * per_block) + half * per_block
        column = lax.broadcasted_iota(jnp.int32, (rows, width), 1) // rank + start
        own = rank_ref[...]
        wide = jnp.concatenate([own] * per_block, axis=1)
        kept = jnp.where(column == adapter_ref[...], wide, 0.0).astype(jnp.bfloat16)
        product = jnp.dot(kept, up_ref[0], preferred_element_type=jnp.float32)

        @pl.when(block == 0)
        def _():
            acc_ref[...] = product

        @pl.when(block > 0)
        def _():
            acc_ref[...] += product

        @pl.when(block == blocks - 1)
        def _():
            delta = acc_ref[...].astype(jnp.bfloat16).astype(jnp.float32)
            out_ref[...] = (base_ref[...] + delta).astype(jnp.bfloat16)

    return pl.pallas_call(
        kernel,
        out_shape=jax.ShapeDtypeStruct((rows, columns), jnp.bfloat16),
        grid=(blocks,),
        in_specs=[
            pl.BlockSpec((rows, columns), lambda b: (0, 0)),
            pl.BlockSpec((rows, rank), lambda b: (0, 0)),
            pl.BlockSpec((rows, 1), lambda b: (0, 0)),
            pl.BlockSpec((1, width, columns), lambda b: (b, 0, 0)),
        ],
        out_specs=pl.BlockSpec((rows, columns), lambda b: (0, 0)),
        scratch_shapes=[pltpu.VMEM((rows, columns), jnp.float32)],
        compiler_params=pltpu.CompilerParams(vmem_limit_bytes=VMEM_LIMIT),
        cost_estimate=pl.CostEstimate(
            flops=2 * rows * columns * width * blocks,
            bytes_accessed=2 * columns * (3 * rows + width * blocks),
            transcendentals=0,
        ),
        name="query",
    )(base, ranks, row_adapters, up)


def attend(block_ids, query, lengths, key_values, fresh_keys, fresh_values):
    steps, rows, width = query.shape
    head_size = fresh_keys.shape[2]
    heads = width // head_size
    blocks = len(key_values)
    positions = key_values[0].shape[1] // rows
    group = 8
    bundle = 16
    cached = blocks * group * positions
    scale = head_size ** (-0.5)

    def kernel(ids_ref, query_ref, length_ref, *refs):
        key_refs = refs[:blocks]
        fresh_key_ref, fresh_value_ref, out_ref = refs[blocks:]
        column = lax.broadcasted_iota(jnp.int32, (group, group * positions), 1)
        own_row = lax.broadcasted_iota(jnp.int32, (group, group * positions), 0)
        on_row = column // positions == own_row
        offset = column % positions
        fresh_column = lax.broadcasted_iota(jnp.int32, (steps, group, steps * group), 2)
        fresh_row = lax.broadcasted_iota(jnp.int32, (steps, group, steps * group), 1)
        fresh_step = lax.broadcasted_iota(jnp.int32, (steps, group, steps * group), 0)
        fresh_seen = (fresh_column % group == fresh_row) & (fresh_column // group <= fresh_step)
        fresh_seen = jnp.broadcast_to(
            fresh_seen[:, None], (steps, heads, group, steps * group)
        ).reshape(steps * heads, group, steps * group)
        query_all = query_ref[...].astype(jnp.float32)
        fresh_key_all = fresh_key_ref[...].astype(jnp.float32)
        fresh_value_all = fresh_value_ref[...].astype(jnp.float32)
        outputs = []
        for part in range(bundle // group):
            here = slice(part * group, (part + 1) * group)
            there = slice(part * group * positions, (part + 1) * group * positions)
            queries = jnp.concatenate(
                [
                    query_all[s, here, h * head_size : (h + 1) * head_size]
                    for s in range(steps)
                    for h in range(heads)
                ],
                axis=0,
            ).astype(jnp.bfloat16)
            keys = jnp.concatenate([ref[0, there, :] for ref in key_refs], axis=0)
            values = jnp.concatenate([ref[1, there, :] for ref in key_refs], axis=0)
            new_keys = fresh_key_all[:, here].reshape(steps * group, head_size)
            new_values = fresh_value_all[:, here].reshape(steps * group, head_size)
            contract = (((1,), (1,)), ((), ()))
            scores = lax.dot_general(
                queries, keys, contract, preferred_element_type=jnp.float32
            ).reshape(steps * heads, group, cached)
            new_scores = lax.dot_general(
                queries,
                new_keys.astype(jnp.bfloat16),
                contract,
                preferred_element_type=jnp.float32,
            ).reshape(steps * heads, group, steps * group)
            seen = jnp.concatenate(
                [
                    (on_row & (offset + ids_ref[b] * positions < length_ref[here])).astype(
                        jnp.float32
                    )
                    for b in range(blocks)
                ],
                axis=1,
            )
            scores = jnp.where(seen[None] > 0.0, scores * scale, -1e30)
            new_scores = jnp.where(fresh_seen, new_scores * scale, -1e30)
            top = jnp.maximum(
                jnp.max(scores, axis=-1, keepdims=True), jnp.max(new_scores, axis=-1, keepdims=True)
            )
            raised = jnp.exp(scores - top)
            new_raised = jnp.exp(new_scores - top)
            total = jnp.sum(raised, axis=-1, keepdims=True) + jnp.sum(
                new_raised, axis=-1, keepdims=True
            )
            numerator = jnp.dot(
                raised.reshape(steps * heads * group, cached).astype(jnp.bfloat16),
                values,
                preferred_element_type=jnp.float32,
            ) + jnp.dot(
                new_raised.reshape(steps * heads * group, steps * group).astype(jnp.bfloat16),
                new_values.astype(jnp.bfloat16),
                preferred_element_type=jnp.float32,
            )
            outputs.append(numerator.reshape(steps * heads, group, head_size) / total)
        for s in range(steps):
            for h in range(heads):
                out_ref[s, :, h * head_size : (h + 1) * head_size] = jnp.concatenate(
                    [out[s * heads + h] for out in outputs], axis=0
                ).astype(jnp.bfloat16)

    key_spec = pl.BlockSpec((2, bundle * positions, head_size), lambda g, ids: (0, g, 0))
    fresh_spec = pl.BlockSpec((steps, bundle, head_size), lambda g, ids: (0, g, 0))
    wide_spec = pl.BlockSpec((steps, bundle, width), lambda g, ids: (0, g, 0))
    return pl.pallas_call(
        kernel,
        out_shape=jax.ShapeDtypeStruct(query.shape, jnp.bfloat16),
        grid_spec=pltpu.PrefetchScalarGridSpec(
            num_scalar_prefetch=1,
            grid=(rows // bundle,),
            in_specs=[wide_spec, pl.BlockSpec((bundle, 1), lambda g, ids: (g, 0))]
            + [key_spec] * blocks
            + [fresh_spec] * 2,
            out_specs=wide_spec,
        ),
        compiler_params=pltpu.CompilerParams(vmem_limit_bytes=VMEM_LIMIT),
        cost_estimate=pl.CostEstimate(
            flops=4 * steps * rows * width * group * (blocks * positions + steps),
            bytes_accessed=4 * steps * rows * width + 4 * blocks * rows * positions * head_size,
            transcendentals=steps * rows * heads * 512,
        ),
        name="attend",
    )(block_ids, query, lengths, *key_values, fresh_keys, fresh_values)


def body(
    tokens,
    query_weight,
    adapter_down_weight,
    adapter_up_weight,
    cached_key_rows,
    cached_value_rows,
    incoming_key_rows,
    incoming_value_rows,
    cached_length_rows,
    row_adapter_index,
):
    steps, rows, features = tokens.shape
    width = query_weight.shape[1]
    positions, head_size = cached_key_rows.shape[2:]
    count = lax.axis_size("tensor")
    owners = lax.axis_size("dp")
    replicas = lax.axis_size("rep")
    me = lax.axis_index("tensor")
    ids = jnp.stack([me ^ j for j in range(count)]).astype(jnp.int32)
    adapters = adapter_down_weight.shape[0]
    per_block = adapters // replicas

    start = lax.axis_index("rep") * per_block
    own_down = lax.dynamic_slice_in_dim(
        jnp.swapaxes(adapter_down_weight, 1, 2), start, per_block, axis=0
    )
    own_up = lax.dynamic_slice_in_dim(adapter_up_weight, start, per_block, axis=0)
    all_down = lax.all_gather(own_down, ("rep", "dp"))
    all_up = lax.all_gather(own_up, ("rep", "dp"))
    all_down = all_down.reshape((replicas, owners) + own_down.shape)
    all_up = all_up.reshape((replicas, owners) + own_up.shape)

    near = swap(tokens, 1, count)
    far = [swap(tokens[s], 2, count) for s in range(steps)]
    far_near = [swap(part, 1, count) for part in far]
    flat = (steps * rows, features)

    key_heads = jnp.transpose(cached_key_rows, (1, 0, 2, 3)).reshape(KVH, rows * positions, head_size)
    value_heads = jnp.transpose(cached_value_rows, (1, 0, 2, 3)).reshape(
        KVH, rows * positions, head_size
    )
    both = jnp.stack([key_heads, value_heads], axis=1)
    parcels = [lax.dynamic_index_in_dim(both, ids[j], 0, keepdims=False) for j in range(count)]
    far_parcels = lax.optimization_barrier((parcels[2], parcels[3], far[steps - 1]))
    key_values = [
        parcels[0],
        swap(parcels[1], 1, count),
        swap(far_parcels[0], 2, count),
        swap(far_parcels[1], 3, count),
    ]

    base = project_pair(ids[:2], tokens.reshape(flat), near.reshape(flat), query_weight)
    base = project_pair(
        ids[2:], jnp.stack(far).reshape(flat), jnp.stack(far_near).reshape(flat), query_weight, base
    )

    row_adapters = jnp.tile(row_adapter_index, steps).reshape(steps * rows, 1)
    ranks = adapter_rank(tokens.reshape(flat), row_adapters, all_down, owners, per_block)
    ranks = ranks + swap(ranks, 1, count)
    ranks = ranks + swap(ranks, 2, count)
    query = finish_query(base, ranks, row_adapters, all_up, owners, per_block)

    fresh_keys = lax.dynamic_index_in_dim(incoming_key_rows, me, 2, keepdims=False)
    fresh_values = lax.dynamic_index_in_dim(incoming_value_rows, me, 2, keepdims=False)
    return attend(
        ids,
        query.reshape(steps, rows, width),
        cached_length_rows.reshape(rows, 1),
        key_values,
        fresh_keys,
        fresh_values,
    )


def solution(mesh):
    in_specs = (
        P(None, ("rep", "dp"), "tensor"),
        P(None, "tensor"),
        P("dp", "tensor", None),
        P("dp", None, "tensor"),
        P(("rep", "dp"), None, "tensor", None),
        P(("rep", "dp"), None, "tensor", None),
        P(None, ("rep", "dp"), None, None),
        P(None, ("rep", "dp"), None, None),
        P(("rep", "dp")),
        P(("rep", "dp")),
    )
    out_specs = P(None, ("rep", "dp"), "tensor")
    chosen = body if mesh.shape["tensor"] == KVH else general_body
    return jax.shard_map(chosen, mesh=mesh, in_specs=in_specs, out_specs=out_specs, check_vma=False)
```

```python
import jax
import jax.numpy as jnp
from jax import lax
from jax.experimental import pallas as pl
from jax.experimental.pallas import tpu as pltpu
from jax.sharding import PartitionSpec as P

KVH = 4
VMEM_LIMIT = 56 * 1024 * 1024


def swap(array, bit, count):
    return lax.ppermute(array, "tensor", [(i, i ^ bit) for i in range(count)])


def project_pair(tensor_ids, first, second, weight, earlier=None):
    depth = first[0].shape[1]
    rows = sum(part.shape[0] for part in first)
    columns = weight.shape[1]
    chunk = 512
    chunks = depth // chunk
    parts = len(first)

    def kernel(ids_ref, *refs):
        first_weight, second_weight = refs[2 * parts : 2 * parts + 2]
        out_ref = refs[-1]
        left = jnp.concatenate([ref[...] for ref in refs[:parts]], axis=0)
        right = jnp.concatenate([ref[...] for ref in refs[parts : 2 * parts]], axis=0)
        product = jnp.dot(
            left, first_weight[...], preferred_element_type=jnp.float32
        ) + jnp.dot(right, second_weight[...], preferred_element_type=jnp.float32)

        @pl.when(pl.program_id(0) == 0)
        def _():
            out_ref[...] = product if earlier is None else product + refs[2 * parts + 2][...]

        @pl.when(pl.program_id(0) > 0)
        def _():
            out_ref[...] += product

    whole = pl.BlockSpec((rows, columns), lambda k, ids: (0, 0))
    in_specs = [
        pl.BlockSpec((part.shape[0], chunk), lambda k, ids: (0, k)) for part in first + second
    ] + [
        pl.BlockSpec((chunk, columns), lambda k, ids: (ids[0] * chunks + k, 0)),
        pl.BlockSpec((chunk, columns), lambda k, ids: (ids[1] * chunks + k, 0)),
    ]
    operands = first + second + [weight, weight]
    if earlier is not None:
        in_specs.append(whole)
        operands.append(earlier)
    return pl.pallas_call(
        kernel,
        out_shape=jax.ShapeDtypeStruct((rows, columns), jnp.float32),
        grid_spec=pltpu.PrefetchScalarGridSpec(
            num_scalar_prefetch=1, grid=(chunks,), in_specs=in_specs, out_specs=whole
        ),
        compiler_params=pltpu.CompilerParams(vmem_limit_bytes=VMEM_LIMIT),
        cost_estimate=pl.CostEstimate(
            flops=4 * rows * depth * columns,
            bytes_accessed=4 * depth * (rows + columns) + 4 * rows * columns,
            transcendentals=0,
        ),
        name="project",
    )(tensor_ids, *operands)


def all_ranks(starts, tokens, row_adapters, groups, rank):
    rows, depth = tokens.shape
    width = sum(part.shape[0] for part in groups[0])
    sizes = [len(group) for group in groups]
    flat = [part for group in groups for part in group]

    def kernel(starts_ref, tokens_ref, adapter_ref, *refs):
        down_refs, out_ref = refs[:-1], refs[-1]
        lane = lax.broadcasted_iota(jnp.int32, (rows, width), 1) // rank
        total = jnp.zeros((rows, width), jnp.float32)
        used = 0
        for i, size in enumerate(sizes):
            down = jnp.concatenate([ref[...] for ref in down_refs[used : used + size]], axis=0)
            used += size
            product = lax.dot_general(
                tokens_ref[...],
                down,
                (((1,), (1,)), ((), ())),
                preferred_element_type=jnp.float32,
            )
            total = total + jnp.where(lane + starts_ref[i] == adapter_ref[...], product, 0.0)
        folded = total[:, :128]
        for i in range(1, width // 128):
            folded = folded + total[:, i * 128 : (i + 1) * 128]
        out_ref[...] = folded[:, :rank] + folded[:, rank:]

    operands = [tokens, row_adapters] + flat
    return pl.pallas_call(
        kernel,
        out_shape=jax.ShapeDtypeStruct((rows, rank), jnp.float32),
        grid_spec=pltpu.PrefetchScalarGridSpec(
            num_scalar_prefetch=1,
            grid=(1,),
            in_specs=[pl.BlockSpec(op.shape, lambda g, starts: (0, 0)) for op in operands],
            out_specs=pl.BlockSpec((rows, rank), lambda g, starts: (0, 0)),
        ),
        compiler_params=pltpu.CompilerParams(vmem_limit_bytes=VMEM_LIMIT),
        cost_estimate=pl.CostEstimate(
            flops=2 * rows * depth * width * len(groups),
            bytes_accessed=2 * depth * (rows + width * len(groups)),
            transcendentals=0,
        ),
        name="rank",
    )(starts, *operands)


def part_delta(starts_ref, ranks, held, up_refs, sizes):
    rows, rank = ranks.shape
    width = sum(ref.shape[0] for ref in up_refs[: sizes[0]])
    lane = lax.broadcasted_iota(jnp.int32, (rows, width), 1) // rank
    wide = jnp.concatenate([ranks] * (width // rank), axis=1)
    kept = [
        jnp.where(lane + starts_ref[i] == held, wide, 0.0).astype(jnp.bfloat16)
        for i in range(len(sizes))
    ]
    return jnp.dot(
        jnp.concatenate(kept, axis=1),
        jnp.concatenate([ref[...] for ref in up_refs], axis=0),
        preferred_element_type=jnp.float32,
    )


def early_delta(starts, ranks, row_adapters, groups):
    rows = ranks.shape[0]
    columns = groups[0][0].shape[1]
    sizes = [len(group) for group in groups]
    flat = [part for group in groups for part in group]
    depth = sum(part.shape[0] for part in flat)

    def kernel(starts_ref, rank_ref, adapter_ref, *refs):
        refs[-1][...] = part_delta(starts_ref, rank_ref[...], adapter_ref[...], refs[:-1], sizes)

    operands = [ranks, row_adapters] + flat
    return pl.pallas_call(
        kernel,
        out_shape=jax.ShapeDtypeStruct((rows, columns), jnp.float32),
        grid_spec=pltpu.PrefetchScalarGridSpec(
            num_scalar_prefetch=1,
            grid=(1,),
            in_specs=[pl.BlockSpec(op.shape, lambda g, starts: (0, 0)) for op in operands],
            out_specs=pl.BlockSpec((rows, columns), lambda g, starts: (0, 0)),
        ),
        compiler_params=pltpu.CompilerParams(vmem_limit_bytes=VMEM_LIMIT),
        cost_estimate=pl.CostEstimate(
            flops=2 * rows * columns * depth,
            bytes_accessed=4 * columns * rows + 2 * columns * depth,
            transcendentals=0,
        ),
        name="delta",
    )(starts, *operands)


def attend(
    scalars,
    base,
    delta,
    ranks,
    row_adapters,
    groups,
    lengths,
    key_values,
    fresh_keys,
    fresh_values,
):
    steps, rows, head_size = fresh_keys.shape
    width = base.shape[1]
    heads = width // head_size
    blocks = len(key_values)
    sizes = [len(group) for group in groups]
    ups = [part for group in groups for part in group]
    positions = key_values[0].shape[1] // rows
    bundle = 16
    group = 8 if 8 * positions % 16 == 0 else 16
    cached = blocks * group * positions
    fresh = steps * group
    columns = -(-(cached + fresh) // 128) * 128
    scale = head_size ** (-0.5)

    def kernel(scalars_ref, *refs):
        base_ref, delta_ref, rank_ref, adapter_ref = refs[:4]
        up_refs = refs[4 : 4 + len(ups)]
        length_ref = refs[4 + len(ups)]
        cache_refs = refs[5 + len(ups) : 5 + len(ups) + blocks]
        fresh_key_ref, fresh_value_ref, out_ref, query_ref = refs[5 + len(ups) + blocks :]
        step = pl.program_id(0)

        @pl.when(step == 0)
        def _():
            whole_delta = delta_ref[...] + part_delta(
                scalars_ref, rank_ref[...], adapter_ref[...], up_refs, sizes
            )
            query_ref[...] = base_ref[...] + whole_delta.astype(jnp.bfloat16).astype(jnp.float32)

        column = lax.broadcasted_iota(jnp.int32, (group, group * positions), 1)
        own_row = lax.broadcasted_iota(jnp.int32, (group, group * positions), 0)
        on_row = column // positions == own_row
        place = column % positions
        fresh_column = lax.broadcasted_iota(jnp.int32, (group, columns - cached), 1)
        fresh_row = lax.broadcasted_iota(jnp.int32, (group, columns - cached), 0)
        fresh_own = fresh_column % group == fresh_row
        fresh_key_all = fresh_key_ref[...].astype(jnp.float32)
        fresh_value_all = fresh_value_ref[...].astype(jnp.float32)
        padding = jnp.zeros((columns - cached - fresh, head_size), jnp.float32)
        ones = jnp.ones((columns, head_size), jnp.bfloat16)
        for part in range(bundle // group):
            here = slice(part * group, (part + 1) * group)
            there = slice(part * group * positions, (part + 1) * group * positions)
            queries = jnp.concatenate(
                [
                    query_ref[
                        pl.ds(
                            pl.multiple_of(s * rows + step * bundle + part * group, group), group
                        ),
                        h * head_size : (h + 1) * head_size,
                    ]
                    for s in range(steps)
                    for h in range(heads)
                ],
                axis=0,
            ).astype(jnp.bfloat16)
            new_keys = jnp.concatenate(
                [fresh_key_all[t, here] for t in range(steps)] + [padding], axis=0
            ).astype(jnp.bfloat16)
            new_values = jnp.concatenate(
                [fresh_value_all[t, here] for t in range(steps)] + [padding], axis=0
            ).astype(jnp.bfloat16)
            keys = jnp.concatenate(
                [ref[0, there, :] for ref in cache_refs] + [new_keys], axis=0
            )
            values = jnp.concatenate(
                [ref[1, there, :] for ref in cache_refs] + [new_values], axis=0
            )
            values = jnp.concatenate([values, ones], axis=1)
            scores = lax.dot_general(
                queries, keys, (((1,), (1,)), ((), ())), preferred_element_type=jnp.float32
            ).reshape(steps, heads, group, columns)
            cached_bias = [
                jnp.where(
                    on_row & (place + scalars_ref[len(sizes) + b] * positions < length_ref[here]),
                    0.0,
                    -1e30,
                )
                for b in range(blocks)
            ]
            raised = []
            for s in range(steps):
                bias = jnp.concatenate(
                    cached_bias
                    + [jnp.where(fresh_own & (fresh_column // group <= s), 0.0, -1e30)],
                    axis=1,
                )
                shifted = scores[s] * scale + bias[None]
                shifted = shifted - jnp.max(shifted, axis=-1, keepdims=True)
                raised.append(jnp.exp(shifted).reshape(heads * group, columns))
            sums = jnp.dot(
                jnp.concatenate(raised, axis=0).astype(jnp.bfloat16),
                values,
                preferred_element_type=jnp.float32,
            )
            result = sums[:, :head_size] / sums[:, head_size:]
            for s in range(steps):
                for h in range(heads):
                    start = (s * heads + h) * group
                    out_ref[s, here, h * head_size : (h + 1) * head_size] = result[
                        start : start + group
                    ].astype(jnp.bfloat16)

    def whole(array):
        return pl.BlockSpec(array.shape, lambda g, scalars: (0,) * array.ndim)

    cache_spec = pl.BlockSpec((2, bundle * positions, head_size), lambda g, scalars: (0, g, 0))
    fresh_spec = pl.BlockSpec((steps, bundle, head_size), lambda g, scalars: (0, g, 0))
    wide_spec = pl.BlockSpec((steps, bundle, width), lambda g, scalars: (0, g, 0))
    first = [base, delta, ranks, row_adapters, *ups]
    return pl.pallas_call(
        kernel,
        out_shape=jax.ShapeDtypeStruct((steps, rows, width), jnp.bfloat16),
        grid_spec=pltpu.PrefetchScalarGridSpec(
            num_scalar_prefetch=1,
            grid=(rows // bundle,),
            in_specs=[whole(op) for op in first]
            + [pl.BlockSpec((bundle, 1), lambda g, scalars: (g, 0))]
            + [cache_spec] * blocks
            + [fresh_spec] * 2,
            out_specs=wide_spec,
            scratch_shapes=[pltpu.VMEM((steps * rows, width), jnp.float32)],
        ),
        compiler_params=pltpu.CompilerParams(vmem_limit_bytes=VMEM_LIMIT),
        cost_estimate=pl.CostEstimate(
            flops=4 * steps * rows * width * group * (blocks * positions + steps),
            bytes_accessed=4 * steps * rows * width + 4 * blocks * rows * positions * head_size,
            transcendentals=steps * rows * heads * columns,
        ),
        name="attend",
    )(scalars, *first, lengths, *key_values, fresh_keys, fresh_values)


def ring_hop(array, step, owners):
    size = 2 * owners
    device = [place if place < owners else 3 * owners - 1 - place for place in range(size)]
    pairs = [(device[place], device[(place + step) % size]) for place in range(size)]
    return lax.ppermute(array, ("rep", "dp"), pairs)


def ring_gather(own, owners, gates):
    before, after = own, own
    rows = own.shape[0] // 2
    arrivals = []
    for k in range(1, owners + 1):
        if k in gates:
            before, after, _ = lax.optimization_barrier((before, after, gates[k]))
        if k == owners:
            before, after = before[:rows], after[rows:]
        before, after = ring_hop(before, 1, owners), ring_hop(after, -1, owners)
        arrivals.append((before, after))
    return arrivals


def body(
    tokens,
    query_weight,
    adapter_down_weight,
    adapter_up_weight,
    cached_key_rows,
    cached_value_rows,
    incoming_key_rows,
    incoming_value_rows,
    cached_length_rows,
    row_adapter_index,
):
    steps, rows, features = tokens.shape
    width = query_weight.shape[1]
    positions, head_size = cached_key_rows.shape[2:]
    count = lax.axis_size("tensor")
    owners = lax.axis_size("dp")
    me = lax.axis_index("tensor")
    owner = lax.axis_index("dp")
    replica = lax.axis_index("rep")
    adapters, _, rank = adapter_down_weight.shape
    half = adapters // 2
    flat_tokens = tokens.reshape(steps * rows, features)

    key_heads = jnp.transpose(cached_key_rows, (1, 0, 2, 3)).reshape(KVH, rows * positions, head_size)
    value_heads = jnp.transpose(cached_value_rows, (1, 0, 2, 3)).reshape(
        KVH, rows * positions, head_size
    )
    both = jnp.stack([key_heads, value_heads], axis=1)
    if count == 4:
        ids = jnp.stack([me ^ j for j in range(count)]).astype(jnp.int32)
        near = swap(flat_tokens, 1, count)
        far = swap(flat_tokens, 2, count)
        far_near = swap(far, 1, count)
        base = project_pair(ids[:2], [flat_tokens], [near], query_weight)
        base = project_pair(ids[2:], [far], [far_near], query_weight, base)
        parcels = lax.optimization_barrier(
            [lax.dynamic_index_in_dim(both, ids[j], 0, keepdims=False) for j in range(count)]
        )
        parcel, _ = lax.optimization_barrier((parcels[2], (near, far)))
        second = swap(parcel, 2, count)
        parcel, _ = lax.optimization_barrier((parcels[3], (second, far_near)))
        third = swap(parcel, 3, count)
        key_values = [parcels[0], swap(parcels[1], 1, count), second, third]
        gates = [{2: near, owners: far}, {}, {}]
    else:
        all_tokens = lax.all_gather(flat_tokens, "tensor", axis=1, tiled=True)
        base = jnp.dot(all_tokens, query_weight, preferred_element_type=jnp.float32)
        ids = jnp.arange(count, dtype=jnp.int32)
        key_values = lax.all_to_all(
            jnp.repeat(both, count // KVH, axis=0),
            "tensor",
            split_axis=0,
            concat_axis=0,
            tiled=True,
        )
        key_values = [key_values[b] for b in range(count)]
        gates = [{}, {}, {}]

    down_rows = jnp.swapaxes(adapter_down_weight, 1, 2).reshape(adapters * rank, features)
    up_rows = adapter_up_weight.reshape(adapters * rank, width)
    own_down = lax.dynamic_slice_in_dim(down_rows, replica * half * rank, half * rank, axis=0)
    own_up = lax.dynamic_slice_in_dim(up_rows, replica * half * rank, half * rank, axis=0)
    chunk = half * rank // 2
    down_chunks = [own_down[:chunk], own_down[chunk:]]
    down = [ring_gather(down_chunks[c], owners, gates[c]) for c in range(2)]
    own_up, _ = lax.optimization_barrier((own_up, down[0][owners - 2]))
    up = ring_gather(own_up, owners, gates[2])

    size = 2 * owners
    place = jnp.where(replica == 0, owner, size - 1 - owner)
    steps_round = [d for k in range(1, owners) for d in (-k, k)] + [owners]
    start = []
    for step in [0] + steps_round:
        other = lax.rem(place + step + size, size)
        start.append(
            jnp.where(other < owners, other * adapters, (size - 1 - other) * adapters + half)
        )
    starts = jnp.stack(start).astype(jnp.int32)

    row_adapters = jnp.tile(row_adapter_index, steps).reshape(steps * rows, 1)
    groups = [[own_down]]
    for k in range(owners - 1):
        groups += [[down[c][k][side] for c in range(2)] for side in range(2)]
    groups.append([down[c][owners - 1][side] for c in range(2) for side in range(2)])
    ranks = all_ranks(starts, flat_tokens, row_adapters, groups, rank)
    bit = 1
    while bit < count:
        ranks = ranks + swap(ranks, bit, count)
        bit *= 2
    groups = [[own_up]] + [[part] for pair in up[:-1] for part in pair] + [list(up[-1])]
    early = 2 * (owners - 2) + 1
    delta = early_delta(starts[:early], ranks, row_adapters, groups[:early])

    kv_head = me * KVH // count
    fresh_keys = lax.dynamic_index_in_dim(incoming_key_rows, kv_head, 2, keepdims=False)
    fresh_values = lax.dynamic_index_in_dim(incoming_value_rows, kv_head, 2, keepdims=False)
    return attend(
        jnp.concatenate([starts[early:], ids]),
        base,
        delta,
        ranks,
        row_adapters,
        groups[early:],
        cached_length_rows.reshape(rows, 1),
        key_values,
        fresh_keys,
        fresh_values,
    )


def solution(mesh):
    in_specs = (
        P(None, ("rep", "dp"), "tensor"),
        P(None, "tensor"),
        P("dp", "tensor", None),
        P("dp", None, "tensor"),
        P(("rep", "dp"), None, "tensor", None),
        P(("rep", "dp"), None, "tensor", None),
        P(None, ("rep", "dp"), None, None),
        P(None, ("rep", "dp"), None, None),
        P(("rep", "dp")),
        P(("rep", "dp")),
    )
    out_specs = P(None, ("rep", "dp"), "tensor")
    return jax.shard_map(body, mesh=mesh, in_specs=in_specs, out_specs=out_specs, check_vma=False)
```

```python
import jax
import jax.numpy as jnp
from jax import lax
from jax.experimental import pallas as pl
from jax.experimental.pallas import tpu as pltpu
from jax.sharding import PartitionSpec as P

KVH = 4
VMEM_LIMIT = 56 * 1024 * 1024


def swap(array, bit, count):
    return lax.ppermute(array, "tensor", [(i, i ^ bit) for i in range(count)])


def project_pair(tensor_ids, first, second, weight, earlier=None):
    depth = first[0].shape[1]
    rows = sum(part.shape[0] for part in first)
    columns = weight.shape[1]
    chunk = 512
    chunks = depth // chunk
    parts = len(first)

    def kernel(ids_ref, *refs):
        first_weight, second_weight = refs[2 * parts : 2 * parts + 2]
        out_ref = refs[-1]
        left = jnp.concatenate([ref[...] for ref in refs[:parts]], axis=0)
        right = jnp.concatenate([ref[...] for ref in refs[parts : 2 * parts]], axis=0)
        product = jnp.dot(
            left, first_weight[...], preferred_element_type=jnp.float32
        ) + jnp.dot(right, second_weight[...], preferred_element_type=jnp.float32)

        @pl.when(pl.program_id(0) == 0)
        def _():
            out_ref[...] = product if earlier is None else product + refs[2 * parts + 2][...]

        @pl.when(pl.program_id(0) > 0)
        def _():
            out_ref[...] += product

    whole = pl.BlockSpec((rows, columns), lambda k, ids: (0, 0))
    in_specs = [
        pl.BlockSpec((part.shape[0], chunk), lambda k, ids: (0, k)) for part in first + second
    ] + [
        pl.BlockSpec((chunk, columns), lambda k, ids: (ids[0] * chunks + k, 0)),
        pl.BlockSpec((chunk, columns), lambda k, ids: (ids[1] * chunks + k, 0)),
    ]
    operands = first + second + [weight, weight]
    if earlier is not None:
        in_specs.append(whole)
        operands.append(earlier)
    return pl.pallas_call(
        kernel,
        out_shape=jax.ShapeDtypeStruct((rows, columns), jnp.float32),
        grid_spec=pltpu.PrefetchScalarGridSpec(
            num_scalar_prefetch=1, grid=(chunks,), in_specs=in_specs, out_specs=whole
        ),
        compiler_params=pltpu.CompilerParams(vmem_limit_bytes=VMEM_LIMIT),
        cost_estimate=pl.CostEstimate(
            flops=4 * rows * depth * columns,
            bytes_accessed=4 * depth * (rows + columns) + 4 * rows * columns,
            transcendentals=0,
        ),
        name="project",
    )(tensor_ids, *operands)


def add_ranks(starts, tokens, row_adapters, groups, rank, earlier=None, last=False):
    rows, depth = tokens.shape
    width = sum(part.shape[0] for part in groups[0])
    sizes = [len(group) for group in groups]
    flat = [part for group in groups for part in group]

    def kernel(starts_ref, tokens_ref, adapter_ref, *refs):
        out_ref = refs[-1]
        lane = lax.broadcasted_iota(jnp.int32, (rows, width), 1) // rank
        total = jnp.zeros((rows, width), jnp.float32) if earlier is None else refs[-2][...]
        used = 0
        for i, size in enumerate(sizes):
            down = jnp.concatenate([ref[...] for ref in refs[used : used + size]], axis=0)
            used += size
            product = lax.dot_general(
                tokens_ref[...],
                down,
                (((1,), (1,)), ((), ())),
                preferred_element_type=jnp.float32,
            )
            total = total + jnp.where(lane + starts_ref[i] == adapter_ref[...], product, 0.0)
        if last:
            folded = total[:, :128]
            for i in range(1, width // 128):
                folded = folded + total[:, i * 128 : (i + 1) * 128]
            out_ref[...] = folded[:, :rank] + folded[:, rank:]
        else:
            out_ref[...] = total

    out_width = rank if last else width
    operands = [tokens, row_adapters] + flat + ([] if earlier is None else [earlier])
    return pl.pallas_call(
        kernel,
        out_shape=jax.ShapeDtypeStruct((rows, out_width), jnp.float32),
        grid_spec=pltpu.PrefetchScalarGridSpec(
            num_scalar_prefetch=1,
            grid=(1,),
            in_specs=[pl.BlockSpec(op.shape, lambda g, starts: (0, 0)) for op in operands],
            out_specs=pl.BlockSpec((rows, out_width), lambda g, starts: (0, 0)),
        ),
        compiler_params=pltpu.CompilerParams(vmem_limit_bytes=VMEM_LIMIT),
        cost_estimate=pl.CostEstimate(
            flops=2 * rows * depth * width * len(groups),
            bytes_accessed=2 * depth * (rows + width * len(groups)),
            transcendentals=0,
        ),
        name="rank",
    )(starts, *operands)


def part_delta(starts_ref, ranks, held, up_refs, sizes):
    rows, rank = ranks.shape
    width = sum(ref.shape[0] for ref in up_refs[: sizes[0]])
    lane = lax.broadcasted_iota(jnp.int32, (rows, width), 1) // rank
    wide = jnp.concatenate([ranks] * (width // rank), axis=1)
    kept = [
        jnp.where(lane + starts_ref[i] == held, wide, 0.0).astype(jnp.bfloat16)
        for i in range(len(sizes))
    ]
    return jnp.dot(
        jnp.concatenate(kept, axis=1),
        jnp.concatenate([ref[...] for ref in up_refs], axis=0),
        preferred_element_type=jnp.float32,
    )


def early_query(starts, base, ranks, row_adapters, groups):
    rows, columns = base.shape
    sizes = [len(group) for group in groups]
    flat = [part for group in groups for part in group]
    depth = sum(part.shape[0] for part in flat)

    def kernel(starts_ref, base_ref, rank_ref, adapter_ref, *refs):
        delta = part_delta(starts_ref, rank_ref[...], adapter_ref[...], refs[:-1], sizes)
        refs[-1][...] = base_ref[...] + delta.astype(jnp.bfloat16).astype(jnp.float32)

    operands = [base, ranks, row_adapters] + flat
    return pl.pallas_call(
        kernel,
        out_shape=jax.ShapeDtypeStruct((rows, columns), jnp.float32),
        grid_spec=pltpu.PrefetchScalarGridSpec(
            num_scalar_prefetch=1,
            grid=(1,),
            in_specs=[pl.BlockSpec(op.shape, lambda g, starts: (0, 0)) for op in operands],
            out_specs=pl.BlockSpec((rows, columns), lambda g, starts: (0, 0)),
        ),
        compiler_params=pltpu.CompilerParams(vmem_limit_bytes=VMEM_LIMIT),
        cost_estimate=pl.CostEstimate(
            flops=2 * rows * columns * depth,
            bytes_accessed=8 * columns * rows + 2 * columns * depth,
            transcendentals=0,
        ),
        name="delta",
    )(starts, *operands)


def attend(
    scalars, query, ranks, row_adapters, groups, lengths, key_values, fresh_keys, fresh_values
):
    steps, rows, head_size = fresh_keys.shape
    width = query.shape[1]
    heads = width // head_size
    blocks = len(key_values)
    sizes = [len(group) for group in groups]
    ups = [part for group in groups for part in group]
    positions = key_values[0].shape[1] // rows
    bundle = 32
    sub = 4 if 4 * positions % 16 == 0 and heads % 2 == 0 else 16
    slab = max(sub, 8)
    pack = slab // sub
    span = sub * positions
    cached = blocks * span
    fresh = steps * slab
    columns = -(-(cached + fresh) // 128) * 128
    scale = head_size ** (-0.5)

    def kernel(scalars_ref, *refs):
        given_ref, rank_ref, adapter_ref = refs[:3]
        up_refs = refs[3 : 3 + len(ups)]
        length_ref = refs[3 + len(ups)]
        cache_refs = refs[4 + len(ups) : 4 + len(ups) + blocks]
        fresh_key_ref, fresh_value_ref, out_ref, query_ref = refs[4 + len(ups) + blocks :]
        step = pl.program_id(0)

        @pl.when(step == 0)
        def _():
            delta = part_delta(scalars_ref, rank_ref[...], adapter_ref[...], up_refs, sizes)
            rounded = (given_ref[...] + delta.astype(jnp.bfloat16).astype(jnp.float32)).astype(
                jnp.bfloat16
            )
            query_ref[...] = rounded.astype(jnp.float32)

        column = lax.broadcasted_iota(jnp.int32, (slab, columns), 1)
        own = lax.broadcasted_iota(jnp.int32, (slab, columns), 0) % sub
        on_row = (column % span) // positions == own
        place = jnp.full((slab, columns), 1 << 20, jnp.int32)
        for b in range(blocks):
            here = (column >= b * span) & (column < (b + 1) * span)
            place = jnp.where(
                here & on_row, column % positions + scalars_ref[len(sizes) + b] * positions, place
            )
        fresh_step = (column - cached) // slab
        fresh_row = (column - cached) % slab
        is_fresh = (column >= cached) & (column < cached + fresh)
        padding = jnp.zeros((columns - cached - fresh, head_size), jnp.bfloat16)
        ones = jnp.ones((columns, head_size), jnp.bfloat16)
        fresh_key_all = fresh_key_ref[...].astype(jnp.float32)
        fresh_value_all = fresh_value_ref[...].astype(jnp.float32)
        outputs = []
        for first in range(0, bundle, slab):
            begin = pl.multiple_of(step * bundle + first, slab)
            slabs = [
                [
                    query_ref[pl.ds(s * rows + begin, slab), h * head_size : (h + 1) * head_size]
                    for h in range(heads)
                ]
                for s in range(steps)
            ]
            new = slice(first, first + slab)
            new_keys = jnp.concatenate(
                [fresh_key_all[t, new] for t in range(steps)], axis=0
            ).astype(jnp.bfloat16)
            new_values = jnp.concatenate(
                [fresh_value_all[t, new] for t in range(steps)], axis=0
            ).astype(jnp.bfloat16)
            length_all = length_ref[new]
            for part in range(pack):
                mine = slice(part * sub, (part + 1) * sub)
                there = slice((first + part * sub) * positions, (first + (part + 1) * sub) * positions)
                queries = jnp.concatenate(
                    [slabs[s][h][mine] for s in range(steps) for h in range(heads)], axis=0
                ).astype(jnp.bfloat16)
                keys = jnp.concatenate(
                    [ref[0, there, :] for ref in cache_refs] + [new_keys, padding], axis=0
                )
                values = jnp.concatenate(
                    [ref[1, there, :] for ref in cache_refs] + [new_values, padding], axis=0
                )
                values = jnp.concatenate([values, ones], axis=1)
                scores = lax.dot_general(
                    queries, keys, (((1,), (1,)), ((), ())), preferred_element_type=jnp.float32
                ).reshape(steps, heads // pack, slab, columns)
                length = jnp.concatenate([length_all[mine]] * pack, axis=0)
                cached_seen = place < length
                fresh_seen = is_fresh & (fresh_row == own + part * sub)
                raised = []
                for s in range(steps):
                    seen = cached_seen | (fresh_seen & (fresh_step <= s))
                    bias = jnp.where(seen, 0.0, -1e30)
                    shifted = scores[s] * scale + bias[None]
                    shifted = shifted - jnp.max(shifted, axis=-1, keepdims=True)
                    raised.append(jnp.exp(shifted).reshape(heads // pack * slab, columns))
                sums = jnp.dot(
                    jnp.concatenate(raised, axis=0).astype(jnp.bfloat16),
                    values,
                    preferred_element_type=jnp.float32,
                )
                outputs.append(sums[:, :head_size] / sums[:, head_size:])
        for s in range(steps):
            for h in range(heads):
                start = (s * heads + h) * sub
                out_ref[s, :, h * head_size : (h + 1) * head_size] = jnp.concatenate(
                    [out[start : start + sub] for out in outputs], axis=0
                ).astype(jnp.bfloat16)

    def whole(array):
        return pl.BlockSpec(array.shape, lambda g, scalars: (0,) * array.ndim)

    cache_spec = pl.BlockSpec((2, bundle * positions, head_size), lambda g, scalars: (0, g, 0))
    fresh_spec = pl.BlockSpec((steps, bundle, head_size), lambda g, scalars: (0, g, 0))
    wide_spec = pl.BlockSpec((steps, bundle, width), lambda g, scalars: (0, g, 0))
    first = [query, ranks, row_adapters, *ups]
    return pl.pallas_call(
        kernel,
        out_shape=jax.ShapeDtypeStruct((steps, rows, width), jnp.bfloat16),
        grid_spec=pltpu.PrefetchScalarGridSpec(
            num_scalar_prefetch=1,
            grid=(rows // bundle,),
            in_specs=[whole(op) for op in first]
            + [pl.BlockSpec((bundle, 1), lambda g, scalars: (g, 0))]
            + [cache_spec] * blocks
            + [fresh_spec] * 2,
            out_specs=wide_spec,
            scratch_shapes=[pltpu.VMEM((steps * rows, width), jnp.float32)],
        ),
        compiler_params=pltpu.CompilerParams(vmem_limit_bytes=VMEM_LIMIT),
        cost_estimate=pl.CostEstimate(
            flops=4 * steps * rows * width * sub * (blocks * positions + steps),
            bytes_accessed=4 * steps * rows * width + 4 * blocks * rows * positions * head_size,
            transcendentals=steps * rows * heads * columns,
        ),
        name="attend",
    )(scalars, *first, lengths, *key_values, fresh_keys, fresh_values)


def ring_hop(array, step, owners):
    size = 2 * owners
    device = [place if place < owners else 3 * owners - 1 - place for place in range(size)]
    pairs = [(device[place], device[(place + step) % size]) for place in range(size)]
    return lax.ppermute(array, ("rep", "dp"), pairs)


def gate(array, *others):
    return lax.optimization_barrier((array, others))[0]


def ring_step(k, before, after, owners):
    if k == owners:
        rows = before.shape[0] // 2
        before, after = before[:rows], after[rows:]
    return ring_hop(before, 1, owners), ring_hop(after, -1, owners)


def body(
    tokens,
    query_weight,
    adapter_down_weight,
    adapter_up_weight,
    cached_key_rows,
    cached_value_rows,
    incoming_key_rows,
    incoming_value_rows,
    cached_length_rows,
    row_adapter_index,
):
    steps, rows, features = tokens.shape
    width = query_weight.shape[1]
    positions, head_size = cached_key_rows.shape[2:]
    count = lax.axis_size("tensor")
    owners = lax.axis_size("dp")
    me = lax.axis_index("tensor")
    owner = lax.axis_index("dp")
    replica = lax.axis_index("rep")
    adapters, _, rank = adapter_down_weight.shape
    half = adapters // 2
    flat_tokens = tokens.reshape(steps * rows, features)

    row_adapters = jnp.tile(row_adapter_index, steps).reshape(steps * rows, 1)

    down_rows = jnp.swapaxes(adapter_down_weight, 1, 2).reshape(adapters * rank, features)
    up_rows = adapter_up_weight.reshape(adapters * rank, width)
    own_down = lax.dynamic_slice_in_dim(down_rows, replica * half * rank, half * rank, axis=0)
    own_up = lax.dynamic_slice_in_dim(up_rows, replica * half * rank, half * rank, axis=0)

    size = 2 * owners
    place = jnp.where(replica == 0, owner, size - 1 - owner)
    start = []
    for step in [0] + [d for k in range(1, owners) for d in (-k, k)] + [owners]:
        other = lax.rem(place + step + size, size)
        start.append(
            jnp.where(other < owners, other * adapters, (size - 1 - other) * adapters + half)
        )
    starts = jnp.stack(start).astype(jnp.int32)

    key_heads = jnp.transpose(cached_key_rows, (1, 0, 2, 3)).reshape(KVH, rows * positions, head_size)
    value_heads = jnp.transpose(cached_value_rows, (1, 0, 2, 3)).reshape(
        KVH, rows * positions, head_size
    )
    both = jnp.stack([key_heads, value_heads], axis=1)

    paired = count == 4
    down = [ring_step(1, own_down, own_down, owners)]
    if paired:
        ids = jnp.stack([me ^ j for j in range(count)]).astype(jnp.int32)
        far = swap(flat_tokens, 2, count)
        near = swap(flat_tokens, 1, count)
        parcels = lax.optimization_barrier(
            [lax.dynamic_index_in_dim(both, ids[j], 0, keepdims=False) for j in range(count)]
        )
        base = project_pair(ids[:2], [flat_tokens], [near], query_weight)
        second = swap(gate(parcels[2], near, down[0]), 2, count)
        waits = {2: [near, parcels], 3: [base]}
    else:
        all_tokens = lax.all_gather(flat_tokens, "tensor", axis=1, tiled=True)
        base = jnp.dot(all_tokens, query_weight, preferred_element_type=jnp.float32)
        ids = jnp.arange(count, dtype=jnp.int32)
        gathered = lax.all_to_all(
            jnp.repeat(both, count // KVH, axis=0),
            "tensor",
            split_axis=0,
            concat_axis=0,
            tiled=True,
        )
        key_values = [gathered[b] for b in range(count)]
        waits = {}
    early = 1 + 2 * (owners - 2)
    for k in range(2, owners + 1):
        before, after = down[-1]
        if k == owners:
            groups = [[own_down]] + [[part] for pair in down[: owners - 2] for part in pair]
            ranks = add_ranks(starts[:early], flat_tokens, row_adapters, groups, rank)
        if k in waits:
            before, after = gate((before, after), *waits[k])
        down.append(ring_step(k, before, after, owners))
    if paired:
        far = gate(far, down[owners - 2])
        far_near = swap(far, 1, count)
        third = swap(gate(parcels[3], far), 3, count)
        first = swap(gate(parcels[1], far_near), 1, count)
        key_values = [parcels[0], first, second, third]
        base = project_pair(ids[2:], [far], [far_near], query_weight, base)

    groups = [[part] for part in down[owners - 2]] + [list(down[owners - 1])]
    ranks = add_ranks(
        starts[early:], flat_tokens, row_adapters, groups, rank, earlier=ranks, last=True
    )

    own_up = gate(own_up, down[owners - 2])
    up = [ring_step(1, own_up, own_up, owners)]
    waits = {2: [ranks] + ([second] if paired else [])}
    bit = 1
    while bit < count:
        ranks = ranks + swap(ranks, bit, count)
        bit *= 2
    waits[3] = [ranks, base]
    for k in range(2, owners + 1):
        up.append(ring_step(k, *gate(up[-1], *waits.get(k, [])), owners))

    groups = [[own_up]] + [[part] for pair in up[: owners - 2] for part in pair]
    query = early_query(starts[:early], base, ranks, row_adapters, groups)
    groups = [[part] for part in up[owners - 2]] + [list(up[owners - 1])]

    kv_head = me * KVH // count
    fresh_keys = lax.dynamic_index_in_dim(incoming_key_rows, kv_head, 2, keepdims=False)
    fresh_values = lax.dynamic_index_in_dim(incoming_value_rows, kv_head, 2, keepdims=False)
    return attend(
        jnp.concatenate([starts[early:], ids]),
        query,
        ranks,
        row_adapters,
        groups,
        cached_length_rows.reshape(rows, 1),
        key_values,
        fresh_keys,
        fresh_values,
    )


def solution(mesh):
    in_specs = (
        P(None, ("rep", "dp"), "tensor"),
        P(None, "tensor"),
        P("dp", "tensor", None),
        P("dp", None, "tensor"),
        P(("rep", "dp"), None, "tensor", None),
        P(("rep", "dp"), None, "tensor", None),
        P(None, ("rep", "dp"), None, None),
        P(None, ("rep", "dp"), None, None),
        P(("rep", "dp")),
        P(("rep", "dp")),
    )
    out_specs = P(None, ("rep", "dp"), "tensor")
    return jax.shard_map(body, mesh=mesh, in_specs=in_specs, out_specs=out_specs, check_vma=False)
```

```python
import jax
import jax.numpy as jnp
from jax import lax
from jax.experimental import pallas as pl
from jax.experimental.pallas import tpu as pltpu
from jax.sharding import PartitionSpec as P

KVH = 4
VMEM_LIMIT = 56 * 1024 * 1024


def swap(array, bit, count):
    return lax.ppermute(array, "tensor", [(i, i ^ bit) for i in range(count)])


def project_pair(tensor_ids, first, second, weight, earlier=None):
    depth = first[0].shape[1]
    rows = sum(part.shape[0] for part in first)
    columns = weight.shape[1]
    chunk = 512
    chunks = depth // chunk
    parts = len(first)

    def kernel(ids_ref, *refs):
        first_weight, second_weight = refs[2 * parts : 2 * parts + 2]
        out_ref = refs[-1]
        left = jnp.concatenate([ref[...] for ref in refs[:parts]], axis=0)
        right = jnp.concatenate([ref[...] for ref in refs[parts : 2 * parts]], axis=0)
        product = jnp.dot(
            left, first_weight[...], preferred_element_type=jnp.float32
        ) + jnp.dot(right, second_weight[...], preferred_element_type=jnp.float32)

        @pl.when(pl.program_id(0) == 0)
        def _():
            out_ref[...] = product if earlier is None else product + refs[2 * parts + 2][...]

        @pl.when(pl.program_id(0) > 0)
        def _():
            out_ref[...] += product

    whole = pl.BlockSpec((rows, columns), lambda k, ids: (0, 0))
    in_specs = [
        pl.BlockSpec((part.shape[0], chunk), lambda k, ids: (0, k)) for part in first + second
    ] + [
        pl.BlockSpec((chunk, columns), lambda k, ids: (ids[0] * chunks + k, 0)),
        pl.BlockSpec((chunk, columns), lambda k, ids: (ids[1] * chunks + k, 0)),
    ]
    operands = first + second + [weight, weight]
    if earlier is not None:
        in_specs.append(whole)
        operands.append(earlier)
    return pl.pallas_call(
        kernel,
        out_shape=jax.ShapeDtypeStruct((rows, columns), jnp.float32),
        grid_spec=pltpu.PrefetchScalarGridSpec(
            num_scalar_prefetch=1, grid=(chunks,), in_specs=in_specs, out_specs=whole
        ),
        compiler_params=pltpu.CompilerParams(vmem_limit_bytes=VMEM_LIMIT),
        cost_estimate=pl.CostEstimate(
            flops=4 * rows * depth * columns,
            bytes_accessed=4 * depth * (rows + columns) + 4 * rows * columns,
            transcendentals=0,
        ),
        name="project",
    )(tensor_ids, *operands)


def add_ranks(starts, tokens, row_adapters, groups, rank, earlier=None, last=False):
    rows, depth = tokens.shape
    width = sum(part.shape[0] for part in groups[0])
    sizes = [len(group) for group in groups]
    flat = [part for group in groups for part in group]

    def kernel(starts_ref, tokens_ref, adapter_ref, *refs):
        out_ref = refs[-1]
        lane = lax.broadcasted_iota(jnp.int32, (rows, width), 1) // rank
        total = jnp.zeros((rows, width), jnp.float32) if earlier is None else refs[-2][...]
        used = 0
        for i, size in enumerate(sizes):
            down = jnp.concatenate([ref[...] for ref in refs[used : used + size]], axis=0)
            used += size
            product = lax.dot_general(
                tokens_ref[...],
                down,
                (((1,), (1,)), ((), ())),
                preferred_element_type=jnp.float32,
            )
            total = total + jnp.where(lane + starts_ref[i] == adapter_ref[...], product, 0.0)
        if last:
            folded = total[:, :128]
            for i in range(1, width // 128):
                folded = folded + total[:, i * 128 : (i + 1) * 128]
            out_ref[...] = folded[:, :rank] + folded[:, rank:]
        else:
            out_ref[...] = total

    out_width = rank if last else width
    operands = [tokens, row_adapters] + flat + ([] if earlier is None else [earlier])
    return pl.pallas_call(
        kernel,
        out_shape=jax.ShapeDtypeStruct((rows, out_width), jnp.float32),
        grid_spec=pltpu.PrefetchScalarGridSpec(
            num_scalar_prefetch=1,
            grid=(1,),
            in_specs=[pl.BlockSpec(op.shape, lambda g, starts: (0, 0)) for op in operands],
            out_specs=pl.BlockSpec((rows, out_width), lambda g, starts: (0, 0)),
        ),
        compiler_params=pltpu.CompilerParams(vmem_limit_bytes=VMEM_LIMIT),
        cost_estimate=pl.CostEstimate(
            flops=2 * rows * depth * width * len(groups),
            bytes_accessed=2 * depth * (rows + width * len(groups)),
            transcendentals=0,
        ),
        name="rank",
    )(starts, *operands)


def part_delta(starts_ref, ranks, held, up_refs, sizes):
    rows, rank = ranks.shape
    width = sum(ref.shape[0] for ref in up_refs[: sizes[0]])
    lane = lax.broadcasted_iota(jnp.int32, (rows, width), 1) // rank
    wide = jnp.concatenate([ranks] * (width // rank), axis=1)
    kept = [
        jnp.where(lane + starts_ref[i] == held, wide, 0.0).astype(jnp.bfloat16)
        for i in range(len(sizes))
    ]
    return jnp.dot(
        jnp.concatenate(kept, axis=1),
        jnp.concatenate([ref[...] for ref in up_refs], axis=0),
        preferred_element_type=jnp.float32,
    )


def early_query(starts, base, ranks, row_adapters, groups):
    rows, columns = base.shape
    sizes = [len(group) for group in groups]
    flat = [part for group in groups for part in group]
    depth = sum(part.shape[0] for part in flat)

    def kernel(starts_ref, base_ref, rank_ref, adapter_ref, *refs):
        delta = part_delta(starts_ref, rank_ref[...], adapter_ref[...], refs[:-1], sizes)
        refs[-1][...] = base_ref[...] + delta.astype(jnp.bfloat16).astype(jnp.float32)

    operands = [base, ranks, row_adapters] + flat
    return pl.pallas_call(
        kernel,
        out_shape=jax.ShapeDtypeStruct((rows, columns), jnp.float32),
        grid_spec=pltpu.PrefetchScalarGridSpec(
            num_scalar_prefetch=1,
            grid=(1,),
            in_specs=[pl.BlockSpec(op.shape, lambda g, starts: (0, 0)) for op in operands],
            out_specs=pl.BlockSpec((rows, columns), lambda g, starts: (0, 0)),
        ),
        compiler_params=pltpu.CompilerParams(vmem_limit_bytes=VMEM_LIMIT),
        cost_estimate=pl.CostEstimate(
            flops=2 * rows * columns * depth,
            bytes_accessed=8 * columns * rows + 2 * columns * depth,
            transcendentals=0,
        ),
        name="delta",
    )(starts, *operands)


def attend(
    scalars, query, ranks, row_adapters, groups, lengths, key_values, fresh_keys, fresh_values
):
    steps, rows, head_size = fresh_keys.shape
    width = query.shape[1]
    heads = width // head_size
    blocks = len(key_values)
    sizes = [len(group) for group in groups]
    ups = [part for group in groups for part in group]
    positions = key_values[0].shape[1] // rows
    bundle = 32
    sub = 4 if 4 * positions % 16 == 0 and heads % 2 == 0 else 16
    slab = max(sub, 8)
    pack = slab // sub
    span = sub * positions
    cached = blocks * span
    fresh = steps * slab
    columns = -(-(cached + fresh) // 128) * 128
    scale = head_size ** (-0.5)

    def kernel(scalars_ref, *refs):
        given_ref, rank_ref, adapter_ref = refs[:3]
        up_refs = refs[3 : 3 + len(ups)]
        length_ref = refs[3 + len(ups)]
        cache_refs = refs[4 + len(ups) : 4 + len(ups) + blocks]
        fresh_key_ref, fresh_value_ref, out_ref, query_ref = refs[4 + len(ups) + blocks :]
        step = pl.program_id(0)

        @pl.when(step == 0)
        def _():
            delta = part_delta(scalars_ref, rank_ref[...], adapter_ref[...], up_refs, sizes)
            rounded = (given_ref[...] + delta.astype(jnp.bfloat16).astype(jnp.float32)).astype(
                jnp.bfloat16
            )
            query_ref[...] = rounded.astype(jnp.float32)

        column = lax.broadcasted_iota(jnp.int32, (slab, columns), 1)
        own = lax.broadcasted_iota(jnp.int32, (slab, columns), 0) % sub
        on_row = (column % span) // positions == own
        place = jnp.full((slab, columns), 1 << 20, jnp.int32)
        for b in range(blocks):
            here = (column >= b * span) & (column < (b + 1) * span)
            place = jnp.where(
                here & on_row, column % positions + scalars_ref[len(sizes) + b] * positions, place
            )
        fresh_step = (column - cached) // slab
        fresh_row = (column - cached) % slab
        is_fresh = (column >= cached) & (column < cached + fresh)
        padding = jnp.zeros((columns - cached - fresh, head_size), jnp.bfloat16)
        ones = jnp.ones((columns, head_size), jnp.bfloat16)
        fresh_key_all = fresh_key_ref[...].astype(jnp.float32)
        fresh_value_all = fresh_value_ref[...].astype(jnp.float32)
        scores, values, seen = [], [], []
        for first in range(0, bundle, slab):
            begin = pl.multiple_of(step * bundle + first, slab)
            slabs = [
                [
                    query_ref[pl.ds(s * rows + begin, slab), h * head_size : (h + 1) * head_size]
                    for h in range(heads)
                ]
                for s in range(steps)
            ]
            new = slice(first, first + slab)
            new_keys = jnp.concatenate(
                [fresh_key_all[t, new] for t in range(steps)], axis=0
            ).astype(jnp.bfloat16)
            new_values = jnp.concatenate(
                [fresh_value_all[t, new] for t in range(steps)], axis=0
            ).astype(jnp.bfloat16)
            length_all = length_ref[new]
            for part in range(pack):
                mine = slice(part * sub, (part + 1) * sub)
                there = slice((first + part * sub) * positions, (first + (part + 1) * sub) * positions)
                queries = jnp.concatenate(
                    [slabs[s][h][mine] for s in range(steps) for h in range(heads)], axis=0
                ).astype(jnp.bfloat16)
                keys = jnp.concatenate(
                    [ref[0, there, :] for ref in cache_refs] + [new_keys, padding], axis=0
                )
                own_values = jnp.concatenate(
                    [ref[1, there, :] for ref in cache_refs] + [new_values, padding], axis=0
                )
                values.append(jnp.concatenate([own_values, ones], axis=1))
                scores.append(
                    lax.dot_general(
                        queries, keys, (((1,), (1,)), ((), ())), preferred_element_type=jnp.float32
                    ).reshape(steps, heads // pack, slab, columns)
                )
                length = jnp.concatenate([length_all[mine]] * pack, axis=0)
                cached_seen = place < length
                fresh_seen = is_fresh & (fresh_row == own + part * sub)
                seen.append(
                    [
                        jnp.where(cached_seen | (fresh_seen & (fresh_step <= s)), 0.0, -1e30)
                        for s in range(steps)
                    ]
                )
        shifted = [
            [score[s] * scale + bias[s][None] for s in range(steps)]
            for score, bias in zip(scores, seen)
        ]
        top = [[jnp.max(part, axis=-1, keepdims=True) for part in parts] for parts in shifted]
        raised = [
            jnp.concatenate(
                [
                    jnp.exp(part - most).reshape(heads // pack * slab, columns)
                    for part, most in zip(parts, tops)
                ],
                axis=0,
            ).astype(jnp.bfloat16)
            for parts, tops in zip(shifted, top)
        ]
        sums = [
            jnp.dot(weights, value, preferred_element_type=jnp.float32)
            for weights, value in zip(raised, values)
        ]
        outputs = [both[:, :head_size] / both[:, head_size:] for both in sums]
        for s in range(steps):
            for h in range(heads):
                start = (s * heads + h) * sub
                out_ref[s, :, h * head_size : (h + 1) * head_size] = jnp.concatenate(
                    [out[start : start + sub] for out in outputs], axis=0
                ).astype(jnp.bfloat16)

    def whole(array):
        return pl.BlockSpec(array.shape, lambda g, scalars: (0,) * array.ndim)

    cache_spec = pl.BlockSpec((2, bundle * positions, head_size), lambda g, scalars: (0, g, 0))
    fresh_spec = pl.BlockSpec((steps, bundle, head_size), lambda g, scalars: (0, g, 0))
    wide_spec = pl.BlockSpec((steps, bundle, width), lambda g, scalars: (0, g, 0))
    first = [query, ranks, row_adapters, *ups]
    return pl.pallas_call(
        kernel,
        out_shape=jax.ShapeDtypeStruct((steps, rows, width), jnp.bfloat16),
        grid_spec=pltpu.PrefetchScalarGridSpec(
            num_scalar_prefetch=1,
            grid=(rows // bundle,),
            in_specs=[whole(op) for op in first]
            + [pl.BlockSpec((bundle, 1), lambda g, scalars: (g, 0))]
            + [cache_spec] * blocks
            + [fresh_spec] * 2,
            out_specs=wide_spec,
            scratch_shapes=[pltpu.VMEM((steps * rows, width), jnp.float32)],
        ),
        compiler_params=pltpu.CompilerParams(vmem_limit_bytes=VMEM_LIMIT),
        cost_estimate=pl.CostEstimate(
            flops=4 * steps * rows * width * sub * (blocks * positions + steps),
            bytes_accessed=4 * steps * rows * width + 4 * blocks * rows * positions * head_size,
            transcendentals=steps * rows * heads * columns,
        ),
        name="attend",
    )(scalars, *first, lengths, *key_values, fresh_keys, fresh_values)


def ring_hop(array, step, owners):
    size = 2 * owners
    device = [place if place < owners else 3 * owners - 1 - place for place in range(size)]
    pairs = [(device[place], device[(place + step) % size]) for place in range(size)]
    return lax.ppermute(array, ("rep", "dp"), pairs)


def gate(array, *others):
    return lax.optimization_barrier((array, others))[0]


def ring_step(k, before, after, owners):
    if k == owners:
        rows = before.shape[0] // 2
        before, after = before[:rows], after[rows:]
    return ring_hop(before, 1, owners), ring_hop(after, -1, owners)


def body(
    tokens,
    query_weight,
    adapter_down_weight,
    adapter_up_weight,
    cached_key_rows,
    cached_value_rows,
    incoming_key_rows,
    incoming_value_rows,
    cached_length_rows,
    row_adapter_index,
):
    steps, rows, features = tokens.shape
    width = query_weight.shape[1]
    positions, head_size = cached_key_rows.shape[2:]
    count = lax.axis_size("tensor")
    owners = lax.axis_size("dp")
    me = lax.axis_index("tensor")
    owner = lax.axis_index("dp")
    replica = lax.axis_index("rep")
    adapters, _, rank = adapter_down_weight.shape
    half = adapters // 2
    flat_tokens = tokens.reshape(steps * rows, features)

    row_adapters = jnp.tile(row_adapter_index, steps).reshape(steps * rows, 1)

    down_rows = jnp.swapaxes(adapter_down_weight, 1, 2).reshape(adapters * rank, features)
    up_rows = adapter_up_weight.reshape(adapters * rank, width)
    own_down = lax.dynamic_slice_in_dim(down_rows, replica * half * rank, half * rank, axis=0)
    own_up = lax.dynamic_slice_in_dim(up_rows, replica * half * rank, half * rank, axis=0)

    size = 2 * owners
    place = jnp.where(replica == 0, owner, size - 1 - owner)
    start = []
    for step in [0] + [d for k in range(1, owners) for d in (-k, k)] + [owners]:
        other = lax.rem(place + step + size, size)
        start.append(
            jnp.where(other < owners, other * adapters, (size - 1 - other) * adapters + half)
        )
    starts = jnp.stack(start).astype(jnp.int32)

    key_heads = jnp.transpose(cached_key_rows, (1, 0, 2, 3)).reshape(KVH, rows * positions, head_size)
    value_heads = jnp.transpose(cached_value_rows, (1, 0, 2, 3)).reshape(
        KVH, rows * positions, head_size
    )
    both = jnp.stack([key_heads, value_heads], axis=1)

    paired = count == 4
    down = [ring_step(1, own_down, own_down, owners)]
    if paired:
        ids = jnp.stack([me ^ j for j in range(count)]).astype(jnp.int32)
        far = swap(flat_tokens, 2, count)
        near = swap(flat_tokens, 1, count)
        parcels = lax.optimization_barrier(
            [lax.dynamic_index_in_dim(both, ids[j], 0, keepdims=False) for j in range(count)]
        )
        base = project_pair(ids[:2], [flat_tokens], [near], query_weight)
        waits = {2: [near, parcels, base]}
    else:
        all_tokens = lax.all_gather(flat_tokens, "tensor", axis=1, tiled=True)
        base = jnp.dot(all_tokens, query_weight, preferred_element_type=jnp.float32)
        ids = jnp.arange(count, dtype=jnp.int32)
        gathered = lax.all_to_all(
            jnp.repeat(both, count // KVH, axis=0),
            "tensor",
            split_axis=0,
            concat_axis=0,
            tiled=True,
        )
        key_values = [gathered[b] for b in range(count)]
        waits = {}
    early = 1 + 2 * (owners - 2)
    for k in range(2, owners + 1):
        before, after = down[-1]
        if k == owners:
            groups = [[own_down]] + [[part] for pair in down[: owners - 2] for part in pair]
            ranks = add_ranks(starts[:early], flat_tokens, row_adapters, groups, rank)
            if paired:
                far = gate(far, down[1])
                far_near = swap(far, 1, count)
                second = swap(gate(parcels[2], far), 2, count)
                both_far = gate((far, far_near), ranks)
                base = project_pair(ids[2:], [both_far[0]], [both_far[1]], query_weight, base)
                waits[owners] = [base]
        if k in waits:
            before, after = gate((before, after), *waits[k])
        down.append(ring_step(k, before, after, owners))
    if paired:
        first = swap(gate(parcels[1], far_near), 1, count)
        third = swap(gate(parcels[3], second, first), 3, count)
        key_values = [parcels[0], first, second, third]

    groups = [[part] for part in down[owners - 2]] + [list(down[owners - 1])]
    ranks = add_ranks(
        starts[early:], flat_tokens, row_adapters, groups, rank, earlier=ranks, last=True
    )

    own_up = gate(own_up, down[owners - 2], base)
    up = [ring_step(1, own_up, own_up, owners)]
    waits = {2: [ranks]}
    bit = 1
    while bit < count:
        ranks = ranks + swap(ranks, bit, count)
        bit *= 2
    waits[3] = [ranks]
    if paired:
        waits[owners] = [third]
    for k in range(2, owners + 1):
        up.append(ring_step(k, *gate(up[-1], *waits.get(k, [])), owners))

    groups = [[own_up]] + [[part] for pair in up[: owners - 2] for part in pair]
    query = early_query(starts[:early], base, ranks, row_adapters, groups)
    groups = [[part] for part in up[owners - 2]] + [list(up[owners - 1])]

    kv_head = me * KVH // count
    fresh_keys = lax.dynamic_index_in_dim(incoming_key_rows, kv_head, 2, keepdims=False)
    fresh_values = lax.dynamic_index_in_dim(incoming_value_rows, kv_head, 2, keepdims=False)
    return attend(
        jnp.concatenate([starts[early:], ids]),
        query,
        ranks,
        row_adapters,
        groups,
        cached_length_rows.reshape(rows, 1),
        key_values,
        fresh_keys,
        fresh_values,
    )


def solution(mesh):
    in_specs = (
        P(None, ("rep", "dp"), "tensor"),
        P(None, "tensor"),
        P("dp", "tensor", None),
        P("dp", None, "tensor"),
        P(("rep", "dp"), None, "tensor", None),
        P(("rep", "dp"), None, "tensor", None),
        P(None, ("rep", "dp"), None, None),
        P(None, ("rep", "dp"), None, None),
        P(("rep", "dp")),
        P(("rep", "dp")),
    )
    out_specs = P(None, ("rep", "dp"), "tensor")
    return jax.shard_map(body, mesh=mesh, in_specs=in_specs, out_specs=out_specs, check_vma=False)
```

```python
import jax
import jax.numpy as jnp
from jax import lax
from jax.experimental import pallas as pl
from jax.experimental.pallas import tpu as pltpu
from jax.sharding import PartitionSpec as P

KVH = 4
VMEM_LIMIT = 56 * 1024 * 1024


def swap(array, bit, count):
    return lax.ppermute(array, "tensor", [(i, i ^ bit) for i in range(count)])


def project_pair(tensor_ids, first, second, weight, earlier=None):
    depth = first[0].shape[1]
    rows = sum(part.shape[0] for part in first)
    columns = weight.shape[1]
    chunk = 512
    chunks = depth // chunk
    parts = len(first)

    def kernel(ids_ref, *refs):
        first_weight, second_weight = refs[2 * parts : 2 * parts + 2]
        out_ref = refs[-1]
        left = jnp.concatenate([ref[...] for ref in refs[:parts]], axis=0)
        right = jnp.concatenate([ref[...] for ref in refs[parts : 2 * parts]], axis=0)
        product = jnp.dot(
            left, first_weight[...], preferred_element_type=jnp.float32
        ) + jnp.dot(right, second_weight[...], preferred_element_type=jnp.float32)

        @pl.when(pl.program_id(0) == 0)
        def _():
            out_ref[...] = product if earlier is None else product + refs[2 * parts + 2][...]

        @pl.when(pl.program_id(0) > 0)
        def _():
            out_ref[...] += product

    whole = pl.BlockSpec((rows, columns), lambda k, ids: (0, 0))
    in_specs = [
        pl.BlockSpec((part.shape[0], chunk), lambda k, ids: (0, k)) for part in first + second
    ] + [
        pl.BlockSpec((chunk, columns), lambda k, ids: (ids[0] * chunks + k, 0)),
        pl.BlockSpec((chunk, columns), lambda k, ids: (ids[1] * chunks + k, 0)),
    ]
    operands = first + second + [weight, weight]
    if earlier is not None:
        in_specs.append(whole)
        operands.append(earlier)
    return pl.pallas_call(
        kernel,
        out_shape=jax.ShapeDtypeStruct((rows, columns), jnp.float32),
        grid_spec=pltpu.PrefetchScalarGridSpec(
            num_scalar_prefetch=1, grid=(chunks,), in_specs=in_specs, out_specs=whole
        ),
        compiler_params=pltpu.CompilerParams(vmem_limit_bytes=VMEM_LIMIT),
        cost_estimate=pl.CostEstimate(
            flops=4 * rows * depth * columns,
            bytes_accessed=4 * depth * (rows + columns) + 4 * rows * columns,
            transcendentals=0,
        ),
        name="project",
    )(tensor_ids, *operands)


def add_ranks(starts, tokens, row_adapters, groups, rank, earlier=None, last=False):
    rows, depth = tokens.shape
    width = sum(part.shape[0] for part in groups[0])
    sizes = [len(group) for group in groups]
    flat = [part for group in groups for part in group]

    def kernel(starts_ref, tokens_ref, adapter_ref, *refs):
        out_ref = refs[-1]
        lane = lax.broadcasted_iota(jnp.int32, (rows, width), 1) // rank
        total = jnp.zeros((rows, width), jnp.float32) if earlier is None else refs[-2][...]
        used = 0
        for i, size in enumerate(sizes):
            down = jnp.concatenate([ref[...] for ref in refs[used : used + size]], axis=0)
            used += size
            product = lax.dot_general(
                tokens_ref[...],
                down,
                (((1,), (1,)), ((), ())),
                preferred_element_type=jnp.float32,
            )
            total = total + jnp.where(lane + starts_ref[i] == adapter_ref[...], product, 0.0)
        if last:
            folded = total[:, :128]
            for i in range(1, width // 128):
                folded = folded + total[:, i * 128 : (i + 1) * 128]
            out_ref[...] = folded[:, :rank] + folded[:, rank:]
        else:
            out_ref[...] = total

    out_width = rank if last else width
    operands = [tokens, row_adapters] + flat + ([] if earlier is None else [earlier])
    return pl.pallas_call(
        kernel,
        out_shape=jax.ShapeDtypeStruct((rows, out_width), jnp.float32),
        grid_spec=pltpu.PrefetchScalarGridSpec(
            num_scalar_prefetch=1,
            grid=(1,),
            in_specs=[pl.BlockSpec(op.shape, lambda g, starts: (0, 0)) for op in operands],
            out_specs=pl.BlockSpec((rows, out_width), lambda g, starts: (0, 0)),
        ),
        compiler_params=pltpu.CompilerParams(vmem_limit_bytes=VMEM_LIMIT),
        cost_estimate=pl.CostEstimate(
            flops=2 * rows * depth * width * len(groups),
            bytes_accessed=2 * depth * (rows + width * len(groups)),
            transcendentals=0,
        ),
        name="rank",
    )(starts, *operands)


def part_delta(starts_ref, ranks, held, up_refs, sizes):
    rows, rank = ranks.shape
    width = sum(ref.shape[0] for ref in up_refs[: sizes[0]])
    lane = lax.broadcasted_iota(jnp.int32, (rows, width), 1) // rank
    wide = jnp.concatenate([ranks] * (width // rank), axis=1)
    kept = [
        jnp.where(lane + starts_ref[i] == held, wide, 0.0).astype(jnp.bfloat16)
        for i in range(len(sizes))
    ]
    return jnp.dot(
        jnp.concatenate(kept, axis=1),
        jnp.concatenate([ref[...] for ref in up_refs], axis=0),
        preferred_element_type=jnp.float32,
    )


def early_query(starts, base, ranks, row_adapters, groups):
    rows, columns = base.shape
    sizes = [len(group) for group in groups]
    flat = [part for group in groups for part in group]
    depth = sum(part.shape[0] for part in flat)

    def kernel(starts_ref, base_ref, rank_ref, adapter_ref, *refs):
        delta = part_delta(starts_ref, rank_ref[...], adapter_ref[...], refs[:-1], sizes)
        refs[-1][...] = base_ref[...] + delta.astype(jnp.bfloat16).astype(jnp.float32)

    operands = [base, ranks, row_adapters] + flat
    return pl.pallas_call(
        kernel,
        out_shape=jax.ShapeDtypeStruct((rows, columns), jnp.float32),
        grid_spec=pltpu.PrefetchScalarGridSpec(
            num_scalar_prefetch=1,
            grid=(1,),
            in_specs=[pl.BlockSpec(op.shape, lambda g, starts: (0, 0)) for op in operands],
            out_specs=pl.BlockSpec((rows, columns), lambda g, starts: (0, 0)),
        ),
        compiler_params=pltpu.CompilerParams(vmem_limit_bytes=VMEM_LIMIT),
        cost_estimate=pl.CostEstimate(
            flops=2 * rows * columns * depth,
            bytes_accessed=8 * columns * rows + 2 * columns * depth,
            transcendentals=0,
        ),
        name="delta",
    )(starts, *operands)


def attend(
    scalars, query, ranks, row_adapters, groups, lengths, key_values, fresh_keys, fresh_values
):
    steps, rows, head_size = fresh_keys.shape
    width = query.shape[1]
    heads = width // head_size
    blocks = len(key_values)
    sizes = [len(group) for group in groups]
    ups = [part for group in groups for part in group]
    positions = key_values[0].shape[1] // rows
    bundle = 32
    sub = 4 if 4 * positions % 16 == 0 and heads % 2 == 0 else 16
    slab = max(sub, 8)
    pack = slab // sub
    span = sub * positions
    cached = blocks * span
    fresh = steps * slab
    columns = -(-(cached + fresh) // 128) * 128
    scale = head_size ** (-0.5)

    def kernel(scalars_ref, *refs):
        given_ref, rank_ref, adapter_ref = refs[:3]
        up_refs = refs[3 : 3 + len(ups)]
        length_ref = refs[3 + len(ups)]
        cache_refs = refs[4 + len(ups) : 4 + len(ups) + blocks]
        fresh_key_ref, fresh_value_ref, out_ref, query_ref = refs[4 + len(ups) + blocks :]
        step = pl.program_id(0)

        @pl.when(step == 0)
        def _():
            delta = part_delta(scalars_ref, rank_ref[...], adapter_ref[...], up_refs, sizes)
            rounded = (given_ref[...] + delta.astype(jnp.bfloat16).astype(jnp.float32)).astype(
                jnp.bfloat16
            )
            query_ref[...] = rounded.astype(jnp.float32)

        column = lax.broadcasted_iota(jnp.int32, (slab, columns), 1)
        own = lax.broadcasted_iota(jnp.int32, (slab, columns), 0) % sub
        on_row = (column % span) // positions == own
        place = jnp.full((slab, columns), 1 << 20, jnp.int32)
        for b in range(blocks):
            here = (column >= b * span) & (column < (b + 1) * span)
            place = jnp.where(
                here & on_row, column % positions + scalars_ref[len(sizes) + b] * positions, place
            )
        fresh_step = (column - cached) // slab
        fresh_row = (column - cached) % slab
        is_fresh = (column >= cached) & (column < cached + fresh)
        padding = jnp.zeros((columns - cached - fresh, head_size), jnp.bfloat16)
        ones = jnp.ones((columns, head_size), jnp.bfloat16)
        fresh_key_all = fresh_key_ref[...].astype(jnp.float32)
        fresh_value_all = fresh_value_ref[...].astype(jnp.float32)
        scores, values, seen = [], [], []
        for first in range(0, bundle, slab):
            begin = pl.multiple_of(step * bundle + first, slab)
            slabs = [
                [
                    query_ref[pl.ds(s * rows + begin, slab), h * head_size : (h + 1) * head_size]
                    for h in range(heads)
                ]
                for s in range(steps)
            ]
            new = slice(first, first + slab)
            new_keys = jnp.concatenate(
                [fresh_key_all[t, new] for t in range(steps)], axis=0
            ).astype(jnp.bfloat16)
            new_values = jnp.concatenate(
                [fresh_value_all[t, new] for t in range(steps)], axis=0
            ).astype(jnp.bfloat16)
            length_all = length_ref[new]
            for part in range(pack):
                mine = slice(part * sub, (part + 1) * sub)
                there = slice((first + part * sub) * positions, (first + (part + 1) * sub) * positions)
                queries = jnp.concatenate(
                    [slabs[s][h][mine] for s in range(steps) for h in range(heads)], axis=0
                ).astype(jnp.bfloat16)
                keys = jnp.concatenate(
                    [ref[0, there, :] for ref in cache_refs] + [new_keys, padding], axis=0
                )
                own_values = jnp.concatenate(
                    [ref[1, there, :] for ref in cache_refs] + [new_values, padding], axis=0
                )
                values.append(jnp.concatenate([own_values, ones], axis=1))
                scores.append(
                    lax.dot_general(
                        queries, keys, (((1,), (1,)), ((), ())), preferred_element_type=jnp.float32
                    ).reshape(steps, heads // pack, slab, columns)
                )
                length = jnp.concatenate([length_all[mine]] * pack, axis=0)
                cached_seen = place < length
                fresh_seen = is_fresh & (fresh_row == own + part * sub)
                seen.append(
                    [
                        jnp.where(cached_seen | (fresh_seen & (fresh_step <= s)), 0.0, -1e30)
                        for s in range(steps)
                    ]
                )
        shifted = [
            [score[s] * scale + bias[s][None] for s in range(steps)]
            for score, bias in zip(scores, seen)
        ]
        top = [[jnp.max(part, axis=-1, keepdims=True) for part in parts] for parts in shifted]
        raised = [
            jnp.concatenate(
                [
                    jnp.exp(part - most).reshape(heads // pack * slab, columns)
                    for part, most in zip(parts, tops)
                ],
                axis=0,
            ).astype(jnp.bfloat16)
            for parts, tops in zip(shifted, top)
        ]
        sums = [
            jnp.dot(weights, value, preferred_element_type=jnp.float32)
            for weights, value in zip(raised, values)
        ]
        outputs = [both[:, :head_size] / both[:, head_size:] for both in sums]
        for s in range(steps):
            for h in range(heads):
                start = (s * heads + h) * sub
                out_ref[s, :, h * head_size : (h + 1) * head_size] = jnp.concatenate(
                    [out[start : start + sub] for out in outputs], axis=0
                ).astype(jnp.bfloat16)

    def whole(array):
        return pl.BlockSpec(array.shape, lambda g, scalars: (0,) * array.ndim)

    cache_spec = pl.BlockSpec((2, bundle * positions, head_size), lambda g, scalars: (0, g, 0))
    fresh_spec = pl.BlockSpec((steps, bundle, head_size), lambda g, scalars: (0, g, 0))
    wide_spec = pl.BlockSpec((steps, bundle, width), lambda g, scalars: (0, g, 0))
    first = [query, ranks, row_adapters, *ups]
    return pl.pallas_call(
        kernel,
        out_shape=jax.ShapeDtypeStruct((steps, rows, width), jnp.bfloat16),
        grid_spec=pltpu.PrefetchScalarGridSpec(
            num_scalar_prefetch=1,
            grid=(rows // bundle,),
            in_specs=[whole(op) for op in first]
            + [pl.BlockSpec((bundle, 1), lambda g, scalars: (g, 0))]
            + [cache_spec] * blocks
            + [fresh_spec] * 2,
            out_specs=wide_spec,
            scratch_shapes=[pltpu.VMEM((steps * rows, width), jnp.float32)],
        ),
        compiler_params=pltpu.CompilerParams(vmem_limit_bytes=VMEM_LIMIT),
        cost_estimate=pl.CostEstimate(
            flops=4 * steps * rows * width * sub * (blocks * positions + steps),
            bytes_accessed=4 * steps * rows * width + 4 * blocks * rows * positions * head_size,
            transcendentals=steps * rows * heads * columns,
        ),
        name="attend",
    )(scalars, *first, lengths, *key_values, fresh_keys, fresh_values)


def ring_hop(array, step, owners):
    size = 2 * owners
    device = [place if place < owners else 3 * owners - 1 - place for place in range(size)]
    pairs = [(device[place], device[(place + step) % size]) for place in range(size)]
    return lax.ppermute(array, ("rep", "dp"), pairs)


def gate(array, *others):
    return lax.optimization_barrier((array, others))[0]


def ring_step(before, after, owners):
    return ring_hop(before, 1, owners), ring_hop(after, -1, owners)


def body(
    tokens,
    query_weight,
    adapter_down_weight,
    adapter_up_weight,
    cached_key_rows,
    cached_value_rows,
    incoming_key_rows,
    incoming_value_rows,
    cached_length_rows,
    row_adapter_index,
):
    steps, rows, features = tokens.shape
    width = query_weight.shape[1]
    positions, head_size = cached_key_rows.shape[2:]
    count = lax.axis_size("tensor")
    owners = lax.axis_size("dp")
    me = lax.axis_index("tensor")
    owner = lax.axis_index("dp")
    replica = lax.axis_index("rep")
    adapters, _, rank = adapter_down_weight.shape
    half = adapters // 2
    flat_tokens = tokens.reshape(steps * rows, features)

    row_adapters = jnp.tile(row_adapter_index, steps).reshape(steps * rows, 1)

    down_rows = jnp.swapaxes(adapter_down_weight, 1, 2).reshape(adapters * rank, features)
    up_rows = adapter_up_weight.reshape(adapters * rank, width)
    own_down = lax.dynamic_slice_in_dim(down_rows, replica * half * rank, half * rank, axis=0)
    own_up = lax.dynamic_slice_in_dim(up_rows, replica * half * rank, half * rank, axis=0)

    size = 2 * owners
    place = jnp.where(replica == 0, owner, size - 1 - owner)
    start = []
    for step in [0] + [d for k in range(1, owners) for d in (-k, k)] + [owners]:
        other = lax.rem(place + step + size, size)
        start.append(
            jnp.where(other < owners, other * adapters, (size - 1 - other) * adapters + half)
        )
    starts = jnp.stack(start).astype(jnp.int32)

    key_heads = jnp.transpose(cached_key_rows, (1, 0, 2, 3)).reshape(KVH, rows * positions, head_size)
    value_heads = jnp.transpose(cached_value_rows, (1, 0, 2, 3)).reshape(
        KVH, rows * positions, head_size
    )
    both = jnp.stack([key_heads, value_heads], axis=1)

    paired = count == 4
    down = [ring_step(own_down, own_down, owners)]
    if paired:
        ids = jnp.stack([me ^ j for j in range(count)]).astype(jnp.int32)
        far = swap(flat_tokens, 2, count)
        near = swap(flat_tokens, 1, count)
        parcels = lax.optimization_barrier(
            [lax.dynamic_index_in_dim(both, ids[j], 0, keepdims=False) for j in range(count)]
        )
        base = project_pair(ids[:2], [flat_tokens], [near], query_weight)
        waits = {2: [near, parcels, base]}
    else:
        all_tokens = lax.all_gather(flat_tokens, "tensor", axis=1, tiled=True)
        base = jnp.dot(all_tokens, query_weight, preferred_element_type=jnp.float32)
        ids = jnp.arange(count, dtype=jnp.int32)
        gathered = lax.all_to_all(
            jnp.repeat(both, count // KVH, axis=0),
            "tensor",
            split_axis=0,
            concat_axis=0,
            tiled=True,
        )
        key_values = [gathered[b] for b in range(count)]
        waits = {}
    early = 1 + 2 * (owners - 2)
    for k in range(2, owners):
        down.append(ring_step(*gate(down[-1], *waits.get(k, [])), owners))
    groups = [[own_down]] + [[part] for pair in down[: owners - 2] for part in pair]
    ranks = add_ranks(starts[:early], flat_tokens, row_adapters, groups, rank)
    before, after = gate(down[-1], ranks)
    down.append([ring_hop(before, 1, owners)])
    waits = {1: down[owners - 3]}
    if paired:
        far = gate(far, down[owners - 3])
        far_near = swap(far, 1, count)
        second = swap(gate(parcels[2], far), 2, count)
        third = swap(gate(parcels[3], second), 3, count)
        base = project_pair(ids[2:], [far], [far_near], query_weight, base)
        waits = {1: [down[owners - 3], far]}

    from_after = [ring_hop(gate(own_up, *waits[1]), -1, owners)]
    from_before = [ring_hop(gate(own_up, before, from_after[0], base), 1, owners)]
    if paired:
        first = swap(gate(parcels[1], from_after[0]), 1, count)
        key_values = [parcels[0], first, second, third]
    groups = [[part] for part in down[owners - 2]]
    ranks = add_ranks(
        starts[early : early + 2], flat_tokens, row_adapters, groups, rank, earlier=ranks
    )
    ranks = add_ranks(
        starts[early + 2 :],
        flat_tokens,
        row_adapters,
        [down[owners - 1]],
        rank,
        earlier=ranks,
        last=True,
    )
    for k in range(2, owners + 1):
        from_after.append(ring_hop(gate(from_after[-1], *waits.get(k, [])), -1, owners))
    bits = [1 << i for i in range((count - 1).bit_length())]
    for k in range(2, owners):
        for bit in bits[k - 2 : k - 1]:
            ranks = ranks + swap(ranks, bit, count)
        wait = [third] if paired and k == owners - 1 else []
        from_before.append(ring_hop(gate(from_before[-1], ranks, *wait), 1, owners))
    for bit in bits[owners - 2 :]:
        ranks = ranks + swap(ranks, bit, count)
    up = [part for pair in zip(from_before, from_after) for part in pair] + [from_after[-1]]
    groups = [[own_up]] + [[part] for part in up[: early - 1]]
    query = early_query(starts[:early], base, ranks, row_adapters, groups)
    groups = [[part] for part in up[early - 1 :]]

    kv_head = me * KVH // count
    fresh_keys = lax.dynamic_index_in_dim(incoming_key_rows, kv_head, 2, keepdims=False)
    fresh_values = lax.dynamic_index_in_dim(incoming_value_rows, kv_head, 2, keepdims=False)
    return attend(
        jnp.concatenate([starts[early:], ids]),
        query,
        ranks,
        row_adapters,
        groups,
        cached_length_rows.reshape(rows, 1),
        key_values,
        fresh_keys,
        fresh_values,
    )


def solution(mesh):
    in_specs = (
        P(None, ("rep", "dp"), "tensor"),
        P(None, "tensor"),
        P("dp", "tensor", None),
        P("dp", None, "tensor"),
        P(("rep", "dp"), None, "tensor", None),
        P(("rep", "dp"), None, "tensor", None),
        P(None, ("rep", "dp"), None, None),
        P(None, ("rep", "dp"), None, None),
        P(("rep", "dp")),
        P(("rep", "dp")),
    )
    out_specs = P(None, ("rep", "dp"), "tensor")
    return jax.shard_map(body, mesh=mesh, in_specs=in_specs, out_specs=out_specs, check_vma=False)
```

```python
import jax
import jax.numpy as jnp
from jax import lax
from jax.experimental import pallas as pl
from jax.experimental.pallas import tpu as pltpu
from jax.sharding import PartitionSpec as P

KVH = 4
VMEM_LIMIT = 56 * 1024 * 1024


def swap(array, bit, count):
    return lax.ppermute(array, "tensor", [(i, i ^ bit) for i in range(count)])


def project_pair(tensor_ids, first, second, weight, earlier=None):
    depth = first[0].shape[1]
    rows = sum(part.shape[0] for part in first)
    columns = weight.shape[1]
    chunk = 512
    chunks = depth // chunk
    parts = len(first)

    def kernel(ids_ref, *refs):
        first_weight, second_weight = refs[2 * parts : 2 * parts + 2]
        out_ref = refs[-1]
        left = jnp.concatenate([ref[...] for ref in refs[:parts]], axis=0)
        right = jnp.concatenate([ref[...] for ref in refs[parts : 2 * parts]], axis=0)
        product = jnp.dot(
            left, first_weight[...], preferred_element_type=jnp.float32
        ) + jnp.dot(right, second_weight[...], preferred_element_type=jnp.float32)

        @pl.when(pl.program_id(0) == 0)
        def _():
            out_ref[...] = product if earlier is None else product + refs[2 * parts + 2][...]

        @pl.when(pl.program_id(0) > 0)
        def _():
            out_ref[...] += product

    whole = pl.BlockSpec((rows, columns), lambda k, ids: (0, 0))
    in_specs = [
        pl.BlockSpec((part.shape[0], chunk), lambda k, ids: (0, k)) for part in first + second
    ] + [
        pl.BlockSpec((chunk, columns), lambda k, ids: (ids[0] * chunks + k, 0)),
        pl.BlockSpec((chunk, columns), lambda k, ids: (ids[1] * chunks + k, 0)),
    ]
    operands = first + second + [weight, weight]
    if earlier is not None:
        in_specs.append(whole)
        operands.append(earlier)
    return pl.pallas_call(
        kernel,
        out_shape=jax.ShapeDtypeStruct((rows, columns), jnp.float32),
        grid_spec=pltpu.PrefetchScalarGridSpec(
            num_scalar_prefetch=1, grid=(chunks,), in_specs=in_specs, out_specs=whole
        ),
        compiler_params=pltpu.CompilerParams(vmem_limit_bytes=VMEM_LIMIT),
        cost_estimate=pl.CostEstimate(
            flops=4 * rows * depth * columns,
            bytes_accessed=4 * depth * (rows + columns) + 4 * rows * columns,
            transcendentals=0,
        ),
        name="project",
    )(tensor_ids, *operands)


def add_ranks(starts, tokens, row_adapters, groups, rank, earlier=None, last=False):
    rows, depth = tokens.shape
    width = sum(part.shape[0] for part in groups[0])
    sizes = [len(group) for group in groups]
    flat = [part for group in groups for part in group]

    def kernel(starts_ref, tokens_ref, adapter_ref, *refs):
        out_ref = refs[-1]
        lane = lax.broadcasted_iota(jnp.int32, (rows, width), 1) // rank
        total = jnp.zeros((rows, width), jnp.float32) if earlier is None else refs[-2][...]
        used = 0
        for i, size in enumerate(sizes):
            down = jnp.concatenate([ref[...] for ref in refs[used : used + size]], axis=0)
            used += size
            product = lax.dot_general(
                tokens_ref[...],
                down,
                (((1,), (1,)), ((), ())),
                preferred_element_type=jnp.float32,
            )
            total = total + jnp.where(lane + starts_ref[i] == adapter_ref[...], product, 0.0)
        if last:
            folded = total[:, :128]
            for i in range(1, width // 128):
                folded = folded + total[:, i * 128 : (i + 1) * 128]
            out_ref[...] = folded[:, :rank] + folded[:, rank:]
        else:
            out_ref[...] = total

    out_width = rank if last else width
    operands = [tokens, row_adapters] + flat + ([] if earlier is None else [earlier])
    return pl.pallas_call(
        kernel,
        out_shape=jax.ShapeDtypeStruct((rows, out_width), jnp.float32),
        grid_spec=pltpu.PrefetchScalarGridSpec(
            num_scalar_prefetch=1,
            grid=(1,),
            in_specs=[pl.BlockSpec(op.shape, lambda g, starts: (0, 0)) for op in operands],
            out_specs=pl.BlockSpec((rows, out_width), lambda g, starts: (0, 0)),
        ),
        compiler_params=pltpu.CompilerParams(vmem_limit_bytes=VMEM_LIMIT),
        cost_estimate=pl.CostEstimate(
            flops=2 * rows * depth * width * len(groups),
            bytes_accessed=2 * depth * (rows + width * len(groups)),
            transcendentals=0,
        ),
        name="rank",
    )(starts, *operands)


def part_delta(starts_ref, ranks, held, up_refs, sizes):
    rows, rank = ranks.shape
    width = sum(ref.shape[0] for ref in up_refs[: sizes[0]])
    lane = lax.broadcasted_iota(jnp.int32, (rows, width), 1) // rank
    wide = jnp.concatenate([ranks] * (width // rank), axis=1)
    kept = [
        jnp.where(lane + starts_ref[i] == held, wide, 0.0).astype(jnp.bfloat16)
        for i in range(len(sizes))
    ]
    return jnp.dot(
        jnp.concatenate(kept, axis=1),
        jnp.concatenate([ref[...] for ref in up_refs], axis=0),
        preferred_element_type=jnp.float32,
    )


def early_query(starts, base, ranks, row_adapters, groups):
    rows, columns = base.shape
    sizes = [len(group) for group in groups]
    flat = [part for group in groups for part in group]
    depth = sum(part.shape[0] for part in flat)

    def kernel(starts_ref, base_ref, rank_ref, adapter_ref, *refs):
        delta = part_delta(starts_ref, rank_ref[...], adapter_ref[...], refs[:-1], sizes)
        refs[-1][...] = base_ref[...] + delta.astype(jnp.bfloat16).astype(jnp.float32)

    operands = [base, ranks, row_adapters] + flat
    return pl.pallas_call(
        kernel,
        out_shape=jax.ShapeDtypeStruct((rows, columns), jnp.float32),
        grid_spec=pltpu.PrefetchScalarGridSpec(
            num_scalar_prefetch=1,
            grid=(1,),
            in_specs=[pl.BlockSpec(op.shape, lambda g, starts: (0, 0)) for op in operands],
            out_specs=pl.BlockSpec((rows, columns), lambda g, starts: (0, 0)),
        ),
        compiler_params=pltpu.CompilerParams(vmem_limit_bytes=VMEM_LIMIT),
        cost_estimate=pl.CostEstimate(
            flops=2 * rows * columns * depth,
            bytes_accessed=8 * columns * rows + 2 * columns * depth,
            transcendentals=0,
        ),
        name="delta",
    )(starts, *operands)


def attend(
    scalars, query, ranks, row_adapters, groups, lengths, key_values, fresh_keys, fresh_values
):
    steps, rows, head_size = fresh_keys.shape
    width = query.shape[1]
    heads = width // head_size
    blocks = len(key_values)
    sizes = [len(group) for group in groups]
    ups = [part for group in groups for part in group]
    positions = key_values[0].shape[1] // rows
    bundle = 32
    sub = 4 if 4 * positions % 16 == 0 and heads % 2 == 0 else 16
    slab = max(sub, 8)
    pack = slab // sub
    span = sub * positions
    cached = blocks * span
    fresh = steps * slab
    columns = -(-(cached + fresh) // 128) * 128
    scale = head_size ** (-0.5)

    def kernel(scalars_ref, *refs):
        given_ref, rank_ref, adapter_ref = refs[:3]
        up_refs = refs[3 : 3 + len(ups)]
        length_ref = refs[3 + len(ups)]
        cache_refs = refs[4 + len(ups) : 4 + len(ups) + blocks]
        fresh_key_ref, fresh_value_ref, out_ref, query_ref = refs[4 + len(ups) + blocks :]
        step = pl.program_id(0)

        @pl.when(step == 0)
        def _():
            delta = part_delta(scalars_ref, rank_ref[...], adapter_ref[...], up_refs, sizes)
            rounded = (given_ref[...] + delta.astype(jnp.bfloat16).astype(jnp.float32)).astype(
                jnp.bfloat16
            )
            query_ref[...] = rounded.astype(jnp.float32)

        column = lax.broadcasted_iota(jnp.int32, (slab, columns), 1)
        own = lax.broadcasted_iota(jnp.int32, (slab, columns), 0) % sub
        on_row = (column % span) // positions == own
        place = jnp.full((slab, columns), 1 << 20, jnp.int32)
        for b in range(blocks):
            here = (column >= b * span) & (column < (b + 1) * span)
            place = jnp.where(
                here & on_row, column % positions + scalars_ref[len(sizes) + b] * positions, place
            )
        fresh_step = (column - cached) // slab
        fresh_row = (column - cached) % slab
        is_fresh = (column >= cached) & (column < cached + fresh)
        padding = jnp.zeros((columns - cached - fresh, head_size), jnp.bfloat16)
        ones = jnp.ones((columns, head_size), jnp.bfloat16)
        fresh_key_all = fresh_key_ref[...].astype(jnp.float32)
        fresh_value_all = fresh_value_ref[...].astype(jnp.float32)
        scores, values, seen = [], [], []
        for first in range(0, bundle, slab):
            begin = pl.multiple_of(step * bundle + first, slab)
            slabs = [
                [
                    query_ref[pl.ds(s * rows + begin, slab), h * head_size : (h + 1) * head_size]
                    for h in range(heads)
                ]
                for s in range(steps)
            ]
            new = slice(first, first + slab)
            new_keys = jnp.concatenate(
                [fresh_key_all[t, new] for t in range(steps)], axis=0
            ).astype(jnp.bfloat16)
            new_values = jnp.concatenate(
                [fresh_value_all[t, new] for t in range(steps)], axis=0
            ).astype(jnp.bfloat16)
            length_all = length_ref[new]
            for part in range(pack):
                mine = slice(part * sub, (part + 1) * sub)
                there = slice((first + part * sub) * positions, (first + (part + 1) * sub) * positions)
                queries = jnp.concatenate(
                    [slabs[s][h][mine] for s in range(steps) for h in range(heads)], axis=0
                ).astype(jnp.bfloat16)
                keys = jnp.concatenate(
                    [ref[0, there, :] for ref in cache_refs] + [new_keys, padding], axis=0
                )
                own_values = jnp.concatenate(
                    [ref[1, there, :] for ref in cache_refs] + [new_values, padding], axis=0
                )
                values.append(jnp.concatenate([own_values, ones], axis=1))
                scores.append(
                    lax.dot_general(
                        queries, keys, (((1,), (1,)), ((), ())), preferred_element_type=jnp.float32
                    ).reshape(steps, heads // pack, slab, columns)
                )
                length = jnp.concatenate([length_all[mine]] * pack, axis=0)
                cached_seen = place < length
                fresh_seen = is_fresh & (fresh_row == own + part * sub)
                seen.append(
                    [
                        jnp.where(cached_seen | (fresh_seen & (fresh_step <= s)), 0.0, -1e30)
                        for s in range(steps)
                    ]
                )
        shifted = [
            [score[s] * scale + bias[s][None] for s in range(steps)]
            for score, bias in zip(scores, seen)
        ]
        top = [[jnp.max(part, axis=-1, keepdims=True) for part in parts] for parts in shifted]
        raised = [
            jnp.concatenate(
                [
                    jnp.exp(part - most).reshape(heads // pack * slab, columns)
                    for part, most in zip(parts, tops)
                ],
                axis=0,
            ).astype(jnp.bfloat16)
            for parts, tops in zip(shifted, top)
        ]
        sums = [
            jnp.dot(weights, value, preferred_element_type=jnp.float32)
            for weights, value in zip(raised, values)
        ]
        outputs = [both[:, :head_size] / both[:, head_size:] for both in sums]
        for s in range(steps):
            for h in range(heads):
                start = (s * heads + h) * sub
                out_ref[s, :, h * head_size : (h + 1) * head_size] = jnp.concatenate(
                    [out[start : start + sub] for out in outputs], axis=0
                ).astype(jnp.bfloat16)

    def whole(array):
        return pl.BlockSpec(array.shape, lambda g, scalars: (0,) * array.ndim)

    cache_spec = pl.BlockSpec((2, bundle * positions, head_size), lambda g, scalars: (0, g, 0))
    fresh_spec = pl.BlockSpec((steps, bundle, head_size), lambda g, scalars: (0, g, 0))
    wide_spec = pl.BlockSpec((steps, bundle, width), lambda g, scalars: (0, g, 0))
    first = [query, ranks, row_adapters, *ups]
    return pl.pallas_call(
        kernel,
        out_shape=jax.ShapeDtypeStruct((steps, rows, width), jnp.bfloat16),
        grid_spec=pltpu.PrefetchScalarGridSpec(
            num_scalar_prefetch=1,
            grid=(rows // bundle,),
            in_specs=[whole(op) for op in first]
            + [pl.BlockSpec((bundle, 1), lambda g, scalars: (g, 0))]
            + [cache_spec] * blocks
            + [fresh_spec] * 2,
            out_specs=wide_spec,
            scratch_shapes=[pltpu.VMEM((steps * rows, width), jnp.float32)],
        ),
        compiler_params=pltpu.CompilerParams(vmem_limit_bytes=VMEM_LIMIT),
        cost_estimate=pl.CostEstimate(
            flops=4 * steps * rows * width * sub * (blocks * positions + steps),
            bytes_accessed=4 * steps * rows * width + 4 * blocks * rows * positions * head_size,
            transcendentals=steps * rows * heads * columns,
        ),
        name="attend",
    )(scalars, *first, lengths, *key_values, fresh_keys, fresh_values)


def ring_hop(array, step, owners):
    size = 2 * owners
    device = [place if place < owners else 3 * owners - 1 - place for place in range(size)]
    pairs = [(device[place], device[(place + step) % size]) for place in range(size)]
    return lax.ppermute(array, ("rep", "dp"), pairs)


def gate(array, *others):
    return lax.optimization_barrier((array, others))[0]


def ring_step(before, after, owners):
    return ring_hop(before, 1, owners), ring_hop(after, -1, owners)


def split_rows(before, after):
    rows, columns = before.shape
    cut = rows * 3 // 4

    def kernel(before_ref, after_ref, first_ref, last_ref, sems):
        copies = [
            pltpu.make_async_copy(before_ref.at[pl.ds(0, cut)], first_ref, sems.at[0]),
            pltpu.make_async_copy(after_ref.at[pl.ds(cut, rows - cut)], last_ref, sems.at[1]),
        ]
        for copy in copies:
            copy.start()
        for copy in copies:
            copy.wait()

    return pl.pallas_call(
        kernel,
        out_shape=[
            jax.ShapeDtypeStruct((cut, columns), before.dtype),
            jax.ShapeDtypeStruct((rows - cut, columns), before.dtype),
        ],
        in_specs=[pl.BlockSpec(memory_space=pl.ANY)] * 2,
        out_specs=[pl.BlockSpec(memory_space=pl.ANY)] * 2,
        scratch_shapes=[pltpu.SemaphoreType.DMA((2,))],
        cost_estimate=pl.CostEstimate(
            flops=0, bytes_accessed=4 * rows * columns, transcendentals=0
        ),
        name="split",
    )(before, after)


def body(
    tokens,
    query_weight,
    adapter_down_weight,
    adapter_up_weight,
    cached_key_rows,
    cached_value_rows,
    incoming_key_rows,
    incoming_value_rows,
    cached_length_rows,
    row_adapter_index,
):
    steps, rows, features = tokens.shape
    width = query_weight.shape[1]
    positions, head_size = cached_key_rows.shape[2:]
    count = lax.axis_size("tensor")
    owners = lax.axis_size("dp")
    me = lax.axis_index("tensor")
    owner = lax.axis_index("dp")
    replica = lax.axis_index("rep")
    adapters, _, rank = adapter_down_weight.shape
    half = adapters // 2
    flat_tokens = tokens.reshape(steps * rows, features)

    row_adapters = jnp.tile(row_adapter_index, steps).reshape(steps * rows, 1)

    down_rows = jnp.swapaxes(adapter_down_weight, 1, 2).reshape(adapters * rank, features)
    up_rows = adapter_up_weight.reshape(adapters * rank, width)
    own_down = lax.dynamic_slice_in_dim(down_rows, replica * half * rank, half * rank, axis=0)
    own_up = lax.dynamic_slice_in_dim(up_rows, replica * half * rank, half * rank, axis=0)

    size = 2 * owners
    place = jnp.where(replica == 0, owner, size - 1 - owner)
    start = []
    for step in [0] + [d for k in range(1, owners) for d in (-k, k)] + [owners]:
        other = lax.rem(place + step + size, size)
        start.append(
            jnp.where(other < owners, other * adapters, (size - 1 - other) * adapters + half)
        )
    starts = jnp.stack(start).astype(jnp.int32)

    key_heads = jnp.transpose(cached_key_rows, (1, 0, 2, 3)).reshape(KVH, rows * positions, head_size)
    value_heads = jnp.transpose(cached_value_rows, (1, 0, 2, 3)).reshape(
        KVH, rows * positions, head_size
    )
    both = jnp.stack([key_heads, value_heads], axis=1)

    paired = count == 4
    down = [ring_step(own_down, own_down, owners)]
    if paired:
        ids = jnp.stack([me ^ j for j in range(count)]).astype(jnp.int32)
        far = swap(flat_tokens, 2, count)
        near = swap(flat_tokens, 1, count)
        parcels = lax.optimization_barrier(
            [lax.dynamic_index_in_dim(both, ids[j], 0, keepdims=False) for j in range(count)]
        )
        base = project_pair(ids[:2], [flat_tokens], [near], query_weight)
        waits = {2: [near, parcels, base]}
    else:
        all_tokens = lax.all_gather(flat_tokens, "tensor", axis=1, tiled=True)
        base = jnp.dot(all_tokens, query_weight, preferred_element_type=jnp.float32)
        ids = jnp.arange(count, dtype=jnp.int32)
        gathered = lax.all_to_all(
            jnp.repeat(both, count // KVH, axis=0),
            "tensor",
            split_axis=0,
            concat_axis=0,
            tiled=True,
        )
        key_values = [gathered[b] for b in range(count)]
        waits = {}
    early = 1 + 2 * (owners - 2)
    for k in range(2, owners):
        down.append(ring_step(*gate(down[-1], *waits.get(k, [])), owners))
    groups = [[own_down]] + [[part] for pair in down[: owners - 2] for part in pair]
    ranks = add_ranks(starts[:early], flat_tokens, row_adapters, groups, rank)
    if paired:
        far = gate(far, down[owners - 3])
        far_near = swap(far, 1, count)
        second = swap(gate(parcels[2], far), 2, count)
        third = swap(gate(parcels[3], second), 3, count)
        base = project_pair(ids[2:], [far], [far_near], query_weight, base)
    before, after = gate(down[-1], ranks)
    parts = split_rows(before, after)
    down.append(ring_step(*parts, owners))

    from_after = [ring_hop(gate(own_up, *(down[owners - 3] + (far,) if paired else [])), -1, owners)]
    from_before = [ring_hop(gate(own_up, *parts), 1, owners)]
    if paired:
        first = swap(gate(parcels[1], from_after[0]), 1, count)
        key_values = [parcels[0], first, second, third]
    groups = [[part] for part in down[owners - 2]] + [list(down[owners - 1])]
    ranks = add_ranks(
        starts[early:], flat_tokens, row_adapters, groups, rank, earlier=ranks, last=True
    )
    for k in range(2, owners + 1):
        from_after.append(ring_hop(gate(from_after[-1], *(down[-1] if k == 2 else [])), -1, owners))
    bits = [1 << i for i in range((count - 1).bit_length())]
    ranks = ranks + swap(ranks, bits[0], count)
    for k in range(2, owners):
        wait = [ranks] + ([third, base] if paired else []) if k == owners - 1 else []
        from_before.append(ring_hop(gate(from_before[-1], *wait), 1, owners))
    for bit in bits[1:]:
        ranks = ranks + swap(ranks, bit, count)
    up = [part for pair in zip(from_before, from_after) for part in pair] + [from_after[-1]]
    groups = [[own_up]] + [[part] for part in up[: early - 1]]
    query = early_query(starts[:early], base, ranks, row_adapters, groups)
    groups = [[part] for part in up[early - 1 :]]

    kv_head = me * KVH // count
    fresh_keys = lax.dynamic_index_in_dim(incoming_key_rows, kv_head, 2, keepdims=False)
    fresh_values = lax.dynamic_index_in_dim(incoming_value_rows, kv_head, 2, keepdims=False)
    return attend(
        jnp.concatenate([starts[early:], ids]),
        query,
        ranks,
        row_adapters,
        groups,
        cached_length_rows.reshape(rows, 1),
        key_values,
        fresh_keys,
        fresh_values,
    )


def solution(mesh):
    in_specs = (
        P(None, ("rep", "dp"), "tensor"),
        P(None, "tensor"),
        P("dp", "tensor", None),
        P("dp", None, "tensor"),
        P(("rep", "dp"), None, "tensor", None),
        P(("rep", "dp"), None, "tensor", None),
        P(None, ("rep", "dp"), None, None),
        P(None, ("rep", "dp"), None, None),
        P(("rep", "dp")),
        P(("rep", "dp")),
    )
    out_specs = P(None, ("rep", "dp"), "tensor")
    return jax.shard_map(body, mesh=mesh, in_specs=in_specs, out_specs=out_specs, check_vma=False)
```

```python
import jax
import jax.numpy as jnp
from jax import lax
from jax.experimental import pallas as pl
from jax.experimental.pallas import tpu as pltpu
from jax.sharding import PartitionSpec as P

KVH = 4
VMEM_LIMIT = 56 * 1024 * 1024


def swap(array, bit, count):
    return lax.ppermute(array, "tensor", [(i, i ^ bit) for i in range(count)])


def project_pair(tensor_ids, first, second, weight, earlier=None):
    depth = first[0].shape[1]
    rows = sum(part.shape[0] for part in first)
    columns = weight.shape[1]
    chunk = 512
    chunks = depth // chunk
    parts = len(first)

    def kernel(ids_ref, *refs):
        first_weight, second_weight = refs[2 * parts : 2 * parts + 2]
        out_ref = refs[-1]
        left = jnp.concatenate([ref[...] for ref in refs[:parts]], axis=0)
        right = jnp.concatenate([ref[...] for ref in refs[parts : 2 * parts]], axis=0)
        product = jnp.dot(
            left, first_weight[...], preferred_element_type=jnp.float32
        ) + jnp.dot(right, second_weight[...], preferred_element_type=jnp.float32)

        @pl.when(pl.program_id(0) == 0)
        def _():
            out_ref[...] = product if earlier is None else product + refs[2 * parts + 2][...]

        @pl.when(pl.program_id(0) > 0)
        def _():
            out_ref[...] += product

    whole = pl.BlockSpec((rows, columns), lambda k, ids: (0, 0))
    in_specs = [
        pl.BlockSpec((part.shape[0], chunk), lambda k, ids: (0, k)) for part in first + second
    ] + [
        pl.BlockSpec((chunk, columns), lambda k, ids: (ids[0] * chunks + k, 0)),
        pl.BlockSpec((chunk, columns), lambda k, ids: (ids[1] * chunks + k, 0)),
    ]
    operands = first + second + [weight, weight]
    if earlier is not None:
        in_specs.append(whole)
        operands.append(earlier)
    return pl.pallas_call(
        kernel,
        out_shape=jax.ShapeDtypeStruct((rows, columns), jnp.float32),
        grid_spec=pltpu.PrefetchScalarGridSpec(
            num_scalar_prefetch=1, grid=(chunks,), in_specs=in_specs, out_specs=whole
        ),
        compiler_params=pltpu.CompilerParams(vmem_limit_bytes=VMEM_LIMIT),
        cost_estimate=pl.CostEstimate(
            flops=4 * rows * depth * columns,
            bytes_accessed=4 * depth * (rows + columns) + 4 * rows * columns,
            transcendentals=0,
        ),
        name="project",
    )(tensor_ids, *operands)


def add_ranks(starts, tokens, row_adapters, groups, rank, earlier=None, last=False):
    rows, depth = tokens.shape
    width = sum(part.shape[0] for part in groups[0])
    sizes = [len(group) for group in groups]
    flat = [part for group in groups for part in group]

    def kernel(starts_ref, tokens_ref, adapter_ref, *refs):
        out_ref = refs[-1]
        lane = lax.broadcasted_iota(jnp.int32, (rows, width), 1) // rank
        total = jnp.zeros((rows, width), jnp.float32) if earlier is None else refs[-2][...]
        used = 0
        for i, size in enumerate(sizes):
            down = jnp.concatenate([ref[...] for ref in refs[used : used + size]], axis=0)
            used += size
            product = lax.dot_general(
                tokens_ref[...],
                down,
                (((1,), (1,)), ((), ())),
                preferred_element_type=jnp.float32,
            )
            total = total + jnp.where(lane + starts_ref[i] == adapter_ref[...], product, 0.0)
        if last:
            folded = total[:, :128]
            for i in range(1, width // 128):
                folded = folded + total[:, i * 128 : (i + 1) * 128]
            out_ref[...] = folded[:, :rank] + folded[:, rank:]
        else:
            out_ref[...] = total

    out_width = rank if last else width
    operands = [tokens, row_adapters] + flat + ([] if earlier is None else [earlier])
    return pl.pallas_call(
        kernel,
        out_shape=jax.ShapeDtypeStruct((rows, out_width), jnp.float32),
        grid_spec=pltpu.PrefetchScalarGridSpec(
            num_scalar_prefetch=1,
            grid=(1,),
            in_specs=[pl.BlockSpec(op.shape, lambda g, starts: (0, 0)) for op in operands],
            out_specs=pl.BlockSpec((rows, out_width), lambda g, starts: (0, 0)),
        ),
        compiler_params=pltpu.CompilerParams(vmem_limit_bytes=VMEM_LIMIT),
        cost_estimate=pl.CostEstimate(
            flops=2 * rows * depth * width * len(groups),
            bytes_accessed=2 * depth * (rows + width * len(groups)),
            transcendentals=0,
        ),
        name="rank",
    )(starts, *operands)


def part_delta(starts_ref, ranks, held, up_refs, sizes):
    rows, rank = ranks.shape
    width = sum(ref.shape[0] for ref in up_refs[: sizes[0]])
    lane = lax.broadcasted_iota(jnp.int32, (rows, width), 1) // rank
    wide = jnp.concatenate([ranks] * (width // rank), axis=1)
    kept = [
        jnp.where(lane + starts_ref[i] == held, wide, 0.0).astype(jnp.bfloat16)
        for i in range(len(sizes))
    ]
    return jnp.dot(
        jnp.concatenate(kept, axis=1),
        jnp.concatenate([ref[...] for ref in up_refs], axis=0),
        preferred_element_type=jnp.float32,
    )


def early_query(starts, base, ranks, row_adapters, groups):
    rows, columns = base.shape
    sizes = [len(group) for group in groups]
    flat = [part for group in groups for part in group]
    depth = sum(part.shape[0] for part in flat)

    def kernel(starts_ref, base_ref, rank_ref, adapter_ref, *refs):
        delta = part_delta(starts_ref, rank_ref[...], adapter_ref[...], refs[:-1], sizes)
        refs[-1][...] = base_ref[...] + delta.astype(jnp.bfloat16).astype(jnp.float32)

    operands = [base, ranks, row_adapters] + flat
    return pl.pallas_call(
        kernel,
        out_shape=jax.ShapeDtypeStruct((rows, columns), jnp.float32),
        grid_spec=pltpu.PrefetchScalarGridSpec(
            num_scalar_prefetch=1,
            grid=(1,),
            in_specs=[pl.BlockSpec(op.shape, lambda g, starts: (0, 0)) for op in operands],
            out_specs=pl.BlockSpec((rows, columns), lambda g, starts: (0, 0)),
        ),
        compiler_params=pltpu.CompilerParams(vmem_limit_bytes=VMEM_LIMIT),
        cost_estimate=pl.CostEstimate(
            flops=2 * rows * columns * depth,
            bytes_accessed=8 * columns * rows + 2 * columns * depth,
            transcendentals=0,
        ),
        name="delta",
    )(starts, *operands)


def attend(
    scalars, query, ranks, row_adapters, groups, lengths, key_values, fresh_keys, fresh_values
):
    steps, rows, head_size = fresh_keys.shape
    width = query.shape[1]
    heads = width // head_size
    blocks = len(key_values)
    sizes = [len(group) for group in groups]
    ups = [part for group in groups for part in group]
    positions = key_values[0].shape[1] // rows
    bundle = 32
    sub = 4 if 4 * positions % 16 == 0 and heads % 2 == 0 else 16
    slab = max(sub, 8)
    pack = slab // sub
    span = sub * positions
    cached = blocks * span
    fresh = steps * slab
    columns = -(-(cached + fresh) // 128) * 128
    scale = head_size ** (-0.5)

    def kernel(scalars_ref, *refs):
        given_ref, rank_ref, adapter_ref = refs[:3]
        up_refs = refs[3 : 3 + len(ups)]
        length_ref = refs[3 + len(ups)]
        cache_refs = refs[4 + len(ups) : 4 + len(ups) + blocks]
        fresh_key_ref, fresh_value_ref, out_ref, query_ref = refs[4 + len(ups) + blocks :]
        step = pl.program_id(0)

        @pl.when(step == 0)
        def _():
            delta = part_delta(scalars_ref, rank_ref[...], adapter_ref[...], up_refs, sizes)
            rounded = (given_ref[...] + delta.astype(jnp.bfloat16).astype(jnp.float32)).astype(
                jnp.bfloat16
            )
            query_ref[...] = rounded.astype(jnp.float32)

        column = lax.broadcasted_iota(jnp.int32, (slab, columns), 1)
        own = lax.broadcasted_iota(jnp.int32, (slab, columns), 0) % sub
        on_row = (column % span) // positions == own
        place = jnp.full((slab, columns), 1 << 20, jnp.int32)
        for b in range(blocks):
            here = (column >= b * span) & (column < (b + 1) * span)
            place = jnp.where(
                here & on_row, column % positions + scalars_ref[len(sizes) + b] * positions, place
            )
        fresh_step = (column - cached) // slab
        fresh_row = (column - cached) % slab
        is_fresh = (column >= cached) & (column < cached + fresh)
        padding = jnp.zeros((columns - cached - fresh, head_size), jnp.bfloat16)
        ones = jnp.ones((columns, head_size), jnp.bfloat16)
        fresh_key_all = fresh_key_ref[...].astype(jnp.float32)
        fresh_value_all = fresh_value_ref[...].astype(jnp.float32)
        scores, values, seen = [], [], []
        for first in range(0, bundle, slab):
            begin = pl.multiple_of(step * bundle + first, slab)
            slabs = [
                [
                    query_ref[pl.ds(s * rows + begin, slab), h * head_size : (h + 1) * head_size]
                    for h in range(heads)
                ]
                for s in range(steps)
            ]
            new = slice(first, first + slab)
            new_keys = jnp.concatenate(
                [fresh_key_all[t, new] for t in range(steps)], axis=0
            ).astype(jnp.bfloat16)
            new_values = jnp.concatenate(
                [fresh_value_all[t, new] for t in range(steps)], axis=0
            ).astype(jnp.bfloat16)
            length_all = length_ref[new]
            for part in range(pack):
                mine = slice(part * sub, (part + 1) * sub)
                there = slice((first + part * sub) * positions, (first + (part + 1) * sub) * positions)
                queries = jnp.concatenate(
                    [slabs[s][h][mine] for s in range(steps) for h in range(heads)], axis=0
                ).astype(jnp.bfloat16)
                keys = jnp.concatenate(
                    [ref[0, there, :] for ref in cache_refs] + [new_keys, padding], axis=0
                )
                own_values = jnp.concatenate(
                    [ref[1, there, :] for ref in cache_refs] + [new_values, padding], axis=0
                )
                values.append(jnp.concatenate([own_values, ones], axis=1))
                scores.append(
                    lax.dot_general(
                        queries, keys, (((1,), (1,)), ((), ())), preferred_element_type=jnp.float32
                    ).reshape(steps, heads // pack, slab, columns)
                )
                length = jnp.concatenate([length_all[mine]] * pack, axis=0)
                cached_seen = place < length
                fresh_seen = is_fresh & (fresh_row == own + part * sub)
                seen.append(
                    [
                        jnp.where(cached_seen | (fresh_seen & (fresh_step <= s)), 0.0, -1e30)
                        for s in range(steps)
                    ]
                )
        shifted = [
            [score[s] * scale + bias[s][None] for s in range(steps)]
            for score, bias in zip(scores, seen)
        ]
        top = [[jnp.max(part, axis=-1, keepdims=True) for part in parts] for parts in shifted]
        raised = [
            jnp.concatenate(
                [
                    jnp.exp(part - most).reshape(heads // pack * slab, columns)
                    for part, most in zip(parts, tops)
                ],
                axis=0,
            ).astype(jnp.bfloat16)
            for parts, tops in zip(shifted, top)
        ]
        sums = [
            jnp.dot(weights, value, preferred_element_type=jnp.float32)
            for weights, value in zip(raised, values)
        ]
        outputs = [both[:, :head_size] / both[:, head_size:] for both in sums]
        for s in range(steps):
            for h in range(heads):
                start = (s * heads + h) * sub
                out_ref[s, :, h * head_size : (h + 1) * head_size] = jnp.concatenate(
                    [out[start : start + sub] for out in outputs], axis=0
                ).astype(jnp.bfloat16)

    def whole(array):
        return pl.BlockSpec(array.shape, lambda g, scalars: (0,) * array.ndim)

    cache_spec = pl.BlockSpec((2, bundle * positions, head_size), lambda g, scalars: (0, g, 0))
    fresh_spec = pl.BlockSpec((steps, bundle, head_size), lambda g, scalars: (0, g, 0))
    wide_spec = pl.BlockSpec((steps, bundle, width), lambda g, scalars: (0, g, 0))
    first = [query, ranks, row_adapters, *ups]
    return pl.pallas_call(
        kernel,
        out_shape=jax.ShapeDtypeStruct((steps, rows, width), jnp.bfloat16),
        grid_spec=pltpu.PrefetchScalarGridSpec(
            num_scalar_prefetch=1,
            grid=(rows // bundle,),
            in_specs=[whole(op) for op in first]
            + [pl.BlockSpec((bundle, 1), lambda g, scalars: (g, 0))]
            + [cache_spec] * blocks
            + [fresh_spec] * 2,
            out_specs=wide_spec,
            scratch_shapes=[pltpu.VMEM((steps * rows, width), jnp.float32)],
        ),
        compiler_params=pltpu.CompilerParams(vmem_limit_bytes=VMEM_LIMIT),
        cost_estimate=pl.CostEstimate(
            flops=4 * steps * rows * width * sub * (blocks * positions + steps),
            bytes_accessed=4 * steps * rows * width + 4 * blocks * rows * positions * head_size,
            transcendentals=steps * rows * heads * columns,
        ),
        name="attend",
    )(scalars, *first, lengths, *key_values, fresh_keys, fresh_values)


def ring_hop(array, step, owners):
    size = 2 * owners
    device = [place if place < owners else 3 * owners - 1 - place for place in range(size)]
    pairs = [(device[place], device[(place + step) % size]) for place in range(size)]
    return lax.ppermute(array, ("rep", "dp"), pairs)


def gate(array, *others):
    return lax.optimization_barrier((array, others))[0]


def ring_step(before, after, owners):
    return ring_hop(before, 1, owners), ring_hop(after, -1, owners)


def split_rows(before, after):
    rows, columns = before.shape
    cut = rows * 3 // 4

    def kernel(before_ref, after_ref, first_ref, last_ref):
        first_ref[...] = before_ref[...]
        last_ref[...] = after_ref[...]

    return pl.pallas_call(
        kernel,
        out_shape=[
            jax.ShapeDtypeStruct((cut, columns), before.dtype),
            jax.ShapeDtypeStruct((rows - cut, columns), before.dtype),
        ],
        grid=(1,),
        in_specs=[
            pl.BlockSpec((cut, columns), lambda g: (0, 0)),
            pl.BlockSpec((rows - cut, columns), lambda g: (3, 0)),
        ],
        out_specs=[
            pl.BlockSpec((cut, columns), lambda g: (0, 0)),
            pl.BlockSpec((rows - cut, columns), lambda g: (0, 0)),
        ],
        compiler_params=pltpu.CompilerParams(vmem_limit_bytes=VMEM_LIMIT),
        cost_estimate=pl.CostEstimate(
            flops=0, bytes_accessed=4 * rows * columns, transcendentals=0
        ),
        name="split",
    )(before, after)


def body(
    tokens,
    query_weight,
    adapter_down_weight,
    adapter_up_weight,
    cached_key_rows,
    cached_value_rows,
    incoming_key_rows,
    incoming_value_rows,
    cached_length_rows,
    row_adapter_index,
):
    steps, rows, features = tokens.shape
    width = query_weight.shape[1]
    positions, head_size = cached_key_rows.shape[2:]
    count = lax.axis_size("tensor")
    owners = lax.axis_size("dp")
    me = lax.axis_index("tensor")
    owner = lax.axis_index("dp")
    replica = lax.axis_index("rep")
    adapters, _, rank = adapter_down_weight.shape
    half = adapters // 2
    flat_tokens = tokens.reshape(steps * rows, features)

    row_adapters = jnp.tile(row_adapter_index, steps).reshape(steps * rows, 1)

    down_rows = jnp.swapaxes(adapter_down_weight, 1, 2).reshape(adapters * rank, features)
    up_rows = adapter_up_weight.reshape(adapters * rank, width)
    own_down = lax.dynamic_slice_in_dim(down_rows, replica * half * rank, half * rank, axis=0)
    own_up = lax.dynamic_slice_in_dim(up_rows, replica * half * rank, half * rank, axis=0)

    size = 2 * owners
    place = jnp.where(replica == 0, owner, size - 1 - owner)
    start = []
    for step in [0] + [d for k in range(1, owners) for d in (-k, k)] + [owners]:
        other = lax.rem(place + step + size, size)
        start.append(
            jnp.where(other < owners, other * adapters, (size - 1 - other) * adapters + half)
        )
    starts = jnp.stack(start).astype(jnp.int32)

    key_heads = jnp.transpose(cached_key_rows, (1, 0, 2, 3)).reshape(KVH, rows * positions, head_size)
    value_heads = jnp.transpose(cached_value_rows, (1, 0, 2, 3)).reshape(
        KVH, rows * positions, head_size
    )
    both = jnp.stack([key_heads, value_heads], axis=1)

    paired = count == 4
    down = [ring_step(own_down, own_down, owners)]
    if paired:
        ids = jnp.stack([me ^ j for j in range(count)]).astype(jnp.int32)
        far = swap(flat_tokens, 2, count)
        near = swap(flat_tokens, 1, count)
        parcels = lax.optimization_barrier(
            [lax.dynamic_index_in_dim(both, ids[j], 0, keepdims=False) for j in range(count)]
        )
        base = project_pair(ids[:2], [flat_tokens], [near], query_weight)
        waits = {2: [near, parcels, base]}
    else:
        all_tokens = lax.all_gather(flat_tokens, "tensor", axis=1, tiled=True)
        base = jnp.dot(all_tokens, query_weight, preferred_element_type=jnp.float32)
        ids = jnp.arange(count, dtype=jnp.int32)
        gathered = lax.all_to_all(
            jnp.repeat(both, count // KVH, axis=0),
            "tensor",
            split_axis=0,
            concat_axis=0,
            tiled=True,
        )
        key_values = [gathered[b] for b in range(count)]
        waits = {}
    early = 1 + 2 * (owners - 2)
    for k in range(2, owners):
        down.append(ring_step(*gate(down[-1], *waits.get(k, [])), owners))
    groups = [[own_down]] + [[part] for pair in down[: owners - 2] for part in pair]
    ranks = add_ranks(starts[:early], flat_tokens, row_adapters, groups, rank)
    if paired:
        far = gate(far, down[owners - 3])
        far_near = swap(far, 1, count)
        second = swap(gate(parcels[2], far), 2, count)
        third = swap(gate(parcels[3], second), 3, count)
        base = project_pair(ids[2:], [far], [far_near], query_weight, base)
    before, after = gate(down[-1], ranks)
    parts = split_rows(before, after)
    down.append(ring_step(*parts, owners))

    from_after = [ring_hop(gate(own_up, *(down[owners - 3] + (far,) if paired else [])), -1, owners)]
    from_before = [ring_hop(gate(own_up, *parts), 1, owners)]
    if paired:
        first = swap(gate(parcels[1], from_after[0]), 1, count)
        key_values = [parcels[0], first, second, third]
    groups = [[part] for part in down[owners - 2]] + [list(down[owners - 1])]
    ranks = add_ranks(
        starts[early:], flat_tokens, row_adapters, groups, rank, earlier=ranks, last=True
    )
    for k in range(2, owners + 1):
        from_after.append(ring_hop(gate(from_after[-1], *(down[-1] if k == 2 else [])), -1, owners))
    bits = [1 << i for i in range((count - 1).bit_length())]
    ranks = ranks + swap(ranks, bits[0], count)
    for k in range(2, owners):
        wait = [ranks] + ([third, base] if paired else []) if k == owners - 1 else []
        from_before.append(ring_hop(gate(from_before[-1], *wait), 1, owners))
    for bit in bits[1:]:
        ranks = ranks + swap(ranks, bit, count)
    up = [part for pair in zip(from_before, from_after) for part in pair] + [from_after[-1]]
    groups = [[own_up]] + [[part] for part in up[: early - 1]]
    query = early_query(starts[:early], base, ranks, row_adapters, groups)
    groups = [[part] for part in up[early - 1 :]]

    kv_head = me * KVH // count
    fresh_keys = lax.dynamic_index_in_dim(incoming_key_rows, kv_head, 2, keepdims=False)
    fresh_values = lax.dynamic_index_in_dim(incoming_value_rows, kv_head, 2, keepdims=False)
    return attend(
        jnp.concatenate([starts[early:], ids]),
        query,
        ranks,
        row_adapters,
        groups,
        cached_length_rows.reshape(rows, 1),
        key_values,
        fresh_keys,
        fresh_values,
    )


def solution(mesh):
    in_specs = (
        P(None, ("rep", "dp"), "tensor"),
        P(None, "tensor"),
        P("dp", "tensor", None),
        P("dp", None, "tensor"),
        P(("rep", "dp"), None, "tensor", None),
        P(("rep", "dp"), None, "tensor", None),
        P(None, ("rep", "dp"), None, None),
        P(None, ("rep", "dp"), None, None),
        P(("rep", "dp")),
        P(("rep", "dp")),
    )
    out_specs = P(None, ("rep", "dp"), "tensor")
    return jax.shard_map(body, mesh=mesh, in_specs=in_specs, out_specs=out_specs, check_vma=False)
```

```python
import jax
import jax.numpy as jnp
from jax import lax
from jax.experimental import pallas as pl
from jax.experimental.pallas import tpu as pltpu
from jax.sharding import PartitionSpec as P

KVH = 4
VMEM_LIMIT = 56 * 1024 * 1024


def swap(array, bit, count):
    return lax.ppermute(array, "tensor", [(i, i ^ bit) for i in range(count)])


def project_pair(tensor_ids, first, second, weight, earlier=None):
    depth = first[0].shape[1]
    rows = sum(part.shape[0] for part in first)
    columns = weight.shape[1]
    chunk = 512
    chunks = depth // chunk
    parts = len(first)

    def kernel(ids_ref, *refs):
        first_weight, second_weight = refs[2 * parts : 2 * parts + 2]
        out_ref = refs[-1]
        left = jnp.concatenate([ref[...] for ref in refs[:parts]], axis=0)
        right = jnp.concatenate([ref[...] for ref in refs[parts : 2 * parts]], axis=0)
        product = jnp.dot(
            jnp.concatenate([left, right], axis=1),
            jnp.concatenate([first_weight[...], second_weight[...]], axis=0),
            preferred_element_type=jnp.float32,
        )

        @pl.when(pl.program_id(0) == 0)
        def _():
            out_ref[...] = product if earlier is None else product + refs[2 * parts + 2][...]

        @pl.when(pl.program_id(0) > 0)
        def _():
            out_ref[...] += product

    whole = pl.BlockSpec((rows, columns), lambda k, ids: (0, 0))
    in_specs = [
        pl.BlockSpec((part.shape[0], chunk), lambda k, ids: (0, k)) for part in first + second
    ] + [
        pl.BlockSpec((chunk, columns), lambda k, ids: (ids[0] * chunks + k, 0)),
        pl.BlockSpec((chunk, columns), lambda k, ids: (ids[1] * chunks + k, 0)),
    ]
    operands = first + second + [weight, weight]
    if earlier is not None:
        in_specs.append(whole)
        operands.append(earlier)
    return pl.pallas_call(
        kernel,
        out_shape=jax.ShapeDtypeStruct((rows, columns), jnp.float32),
        grid_spec=pltpu.PrefetchScalarGridSpec(
            num_scalar_prefetch=1, grid=(chunks,), in_specs=in_specs, out_specs=whole
        ),
        compiler_params=pltpu.CompilerParams(vmem_limit_bytes=VMEM_LIMIT),
        cost_estimate=pl.CostEstimate(
            flops=4 * rows * depth * columns,
            bytes_accessed=4 * depth * (rows + columns) + 4 * rows * columns,
            transcendentals=0,
        ),
        name="project",
    )(tensor_ids, *operands)


def add_ranks(starts, tokens, row_adapters, groups, rank, earlier=None, last=False):
    rows, depth = tokens.shape
    width = sum(part.shape[0] for part in groups[0])
    sizes = [len(group) for group in groups]
    flat = [part for group in groups for part in group]

    def kernel(starts_ref, tokens_ref, adapter_ref, *refs):
        out_ref = refs[-1]
        lane = lax.broadcasted_iota(jnp.int32, (rows, width), 1) // rank
        total = jnp.zeros((rows, width), jnp.float32) if earlier is None else refs[-2][...]
        used = 0
        for i, size in enumerate(sizes):
            down = jnp.concatenate([ref[...] for ref in refs[used : used + size]], axis=0)
            used += size
            product = lax.dot_general(
                tokens_ref[...],
                down,
                (((1,), (1,)), ((), ())),
                preferred_element_type=jnp.float32,
            )
            total = total + jnp.where(lane + starts_ref[i] == adapter_ref[...], product, 0.0)
        if last:
            folded = total[:, :128]
            for i in range(1, width // 128):
                folded = folded + total[:, i * 128 : (i + 1) * 128]
            out_ref[...] = folded[:, :rank] + folded[:, rank:]
        else:
            out_ref[...] = total

    out_width = rank if last else width
    operands = [tokens, row_adapters] + flat + ([] if earlier is None else [earlier])
    return pl.pallas_call(
        kernel,
        out_shape=jax.ShapeDtypeStruct((rows, out_width), jnp.float32),
        grid_spec=pltpu.PrefetchScalarGridSpec(
            num_scalar_prefetch=1,
            grid=(1,),
            in_specs=[pl.BlockSpec(op.shape, lambda g, starts: (0, 0)) for op in operands],
            out_specs=pl.BlockSpec((rows, out_width), lambda g, starts: (0, 0)),
        ),
        compiler_params=pltpu.CompilerParams(vmem_limit_bytes=VMEM_LIMIT),
        cost_estimate=pl.CostEstimate(
            flops=2 * rows * depth * width * len(groups),
            bytes_accessed=2 * depth * (rows + width * len(groups)),
            transcendentals=0,
        ),
        name="rank",
    )(starts, *operands)


def part_delta(starts_ref, ranks, held, up_refs, sizes):
    rows, rank = ranks.shape
    width = sum(ref.shape[0] for ref in up_refs[: sizes[0]])
    lane = lax.broadcasted_iota(jnp.int32, (rows, width), 1) // rank
    wide = jnp.concatenate([ranks] * (width // rank), axis=1)
    kept = [
        jnp.where(lane + starts_ref[i] == held, wide, 0.0).astype(jnp.bfloat16)
        for i in range(len(sizes))
    ]
    return jnp.dot(
        jnp.concatenate(kept, axis=1),
        jnp.concatenate([ref[...] for ref in up_refs], axis=0),
        preferred_element_type=jnp.float32,
    )


def early_query(starts, base, ranks, row_adapters, groups):
    rows, columns = base.shape
    sizes = [len(group) for group in groups]
    flat = [part for group in groups for part in group]
    depth = sum(part.shape[0] for part in flat)

    def kernel(starts_ref, base_ref, rank_ref, adapter_ref, *refs):
        delta = part_delta(starts_ref, rank_ref[...], adapter_ref[...], refs[:-1], sizes)
        refs[-1][...] = base_ref[...] + delta.astype(jnp.bfloat16).astype(jnp.float32)

    operands = [base, ranks, row_adapters] + flat
    return pl.pallas_call(
        kernel,
        out_shape=jax.ShapeDtypeStruct((rows, columns), jnp.float32),
        grid_spec=pltpu.PrefetchScalarGridSpec(
            num_scalar_prefetch=1,
            grid=(1,),
            in_specs=[pl.BlockSpec(op.shape, lambda g, starts: (0, 0)) for op in operands],
            out_specs=pl.BlockSpec((rows, columns), lambda g, starts: (0, 0)),
        ),
        compiler_params=pltpu.CompilerParams(vmem_limit_bytes=VMEM_LIMIT),
        cost_estimate=pl.CostEstimate(
            flops=2 * rows * columns * depth,
            bytes_accessed=8 * columns * rows + 2 * columns * depth,
            transcendentals=0,
        ),
        name="delta",
    )(starts, *operands)


def attend(
    scalars, query, ranks, row_adapters, groups, lengths, key_values, fresh_keys, fresh_values
):
    steps, rows, head_size = fresh_keys.shape
    width = query.shape[1]
    heads = width // head_size
    blocks = len(key_values)
    sizes = [len(group) for group in groups]
    ups = [part for group in groups for part in group]
    positions = key_values[0].shape[1] // rows
    bundle = 32
    sub = 4 if 4 * positions % 16 == 0 and heads % 2 == 0 else 16
    slab = max(sub, 8)
    pack = slab // sub
    span = sub * positions
    cached = blocks * span
    fresh = steps * slab
    columns = -(-(cached + fresh) // 128) * 128
    scale = head_size ** (-0.5)

    def kernel(scalars_ref, *refs):
        given_ref, rank_ref, adapter_ref = refs[:3]
        up_refs = refs[3 : 3 + len(ups)]
        length_ref = refs[3 + len(ups)]
        cache_refs = refs[4 + len(ups) : 4 + len(ups) + blocks]
        fresh_key_ref, fresh_value_ref, out_ref, query_ref = refs[4 + len(ups) + blocks :]
        step = pl.program_id(0)

        @pl.when(step == 0)
        def _():
            delta = part_delta(scalars_ref, rank_ref[...], adapter_ref[...], up_refs, sizes)
            rounded = (given_ref[...] + delta.astype(jnp.bfloat16).astype(jnp.float32)).astype(
                jnp.bfloat16
            )
            query_ref[...] = rounded.astype(jnp.float32)

        column = lax.broadcasted_iota(jnp.int32, (slab, columns), 1)
        own = lax.broadcasted_iota(jnp.int32, (slab, columns), 0) % sub
        on_row = (column % span) // positions == own
        place = jnp.full((slab, columns), 1 << 20, jnp.int32)
        for b in range(blocks):
            here = (column >= b * span) & (column < (b + 1) * span)
            place = jnp.where(
                here & on_row, column % positions + scalars_ref[len(sizes) + b] * positions, place
            )
        fresh_step = (column - cached) // slab
        fresh_row = (column - cached) % slab
        is_fresh = (column >= cached) & (column < cached + fresh)
        padding = jnp.zeros((columns - cached - fresh, head_size), jnp.bfloat16)
        ones = jnp.ones((columns, head_size), jnp.bfloat16)
        fresh_key_all = fresh_key_ref[...].astype(jnp.float32)
        fresh_value_all = fresh_value_ref[...].astype(jnp.float32)
        scores, values, seen = [], [], []
        for first in range(0, bundle, slab):
            begin = pl.multiple_of(step * bundle + first, slab)
            slabs = [
                [
                    query_ref[pl.ds(s * rows + begin, slab), h * head_size : (h + 1) * head_size]
                    for h in range(heads)
                ]
                for s in range(steps)
            ]
            new = slice(first, first + slab)
            new_keys = jnp.concatenate(
                [fresh_key_all[t, new] for t in range(steps)], axis=0
            ).astype(jnp.bfloat16)
            new_values = jnp.concatenate(
                [fresh_value_all[t, new] for t in range(steps)], axis=0
            ).astype(jnp.bfloat16)
            length_all = length_ref[new]
            for part in range(pack):
                mine = slice(part * sub, (part + 1) * sub)
                there = slice((first + part * sub) * positions, (first + (part + 1) * sub) * positions)
                queries = jnp.concatenate(
                    [slabs[s][h][mine] for s in range(steps) for h in range(heads)], axis=0
                ).astype(jnp.bfloat16)
                keys = jnp.concatenate(
                    [ref[0, there, :] for ref in cache_refs] + [new_keys, padding], axis=0
                )
                own_values = jnp.concatenate(
                    [ref[1, there, :] for ref in cache_refs] + [new_values, padding], axis=0
                )
                values.append(jnp.concatenate([own_values, ones], axis=1))
                scores.append(
                    lax.dot_general(
                        queries, keys, (((1,), (1,)), ((), ())), preferred_element_type=jnp.float32
                    ).reshape(steps, heads // pack, slab, columns)
                )
                length = jnp.concatenate([length_all[mine]] * pack, axis=0)
                cached_seen = place < length
                fresh_seen = is_fresh & (fresh_row == own + part * sub)
                seen.append(
                    [
                        jnp.where(cached_seen | (fresh_seen & (fresh_step <= s)), 0.0, -1e30)
                        for s in range(steps)
                    ]
                )
        shifted = [
            [score[s] * scale + bias[s][None] for s in range(steps)]
            for score, bias in zip(scores, seen)
        ]
        top = [[jnp.max(part, axis=-1, keepdims=True) for part in parts] for parts in shifted]
        raised = [
            jnp.concatenate(
                [
                    jnp.exp(part - most).reshape(heads // pack * slab, columns)
                    for part, most in zip(parts, tops)
                ],
                axis=0,
            ).astype(jnp.bfloat16)
            for parts, tops in zip(shifted, top)
        ]
        sums = [
            jnp.dot(weights, value, preferred_element_type=jnp.float32)
            for weights, value in zip(raised, values)
        ]
        outputs = [both[:, :head_size] / both[:, head_size:] for both in sums]
        for s in range(steps):
            for h in range(heads):
                start = (s * heads + h) * sub
                out_ref[s, :, h * head_size : (h + 1) * head_size] = jnp.concatenate(
                    [out[start : start + sub] for out in outputs], axis=0
                ).astype(jnp.bfloat16)

    def whole(array):
        return pl.BlockSpec(array.shape, lambda g, scalars: (0,) * array.ndim)

    cache_spec = pl.BlockSpec((2, bundle * positions, head_size), lambda g, scalars: (0, g, 0))
    fresh_spec = pl.BlockSpec((steps, bundle, head_size), lambda g, scalars: (0, g, 0))
    wide_spec = pl.BlockSpec((steps, bundle, width), lambda g, scalars: (0, g, 0))
    first = [query, ranks, row_adapters, *ups]
    return pl.pallas_call(
        kernel,
        out_shape=jax.ShapeDtypeStruct((steps, rows, width), jnp.bfloat16),
        grid_spec=pltpu.PrefetchScalarGridSpec(
            num_scalar_prefetch=1,
            grid=(rows // bundle,),
            in_specs=[whole(op) for op in first]
            + [pl.BlockSpec((bundle, 1), lambda g, scalars: (g, 0))]
            + [cache_spec] * blocks
            + [fresh_spec] * 2,
            out_specs=wide_spec,
            scratch_shapes=[pltpu.VMEM((steps * rows, width), jnp.float32)],
        ),
        compiler_params=pltpu.CompilerParams(vmem_limit_bytes=VMEM_LIMIT),
        cost_estimate=pl.CostEstimate(
            flops=4 * steps * rows * width * sub * (blocks * positions + steps),
            bytes_accessed=4 * steps * rows * width + 4 * blocks * rows * positions * head_size,
            transcendentals=steps * rows * heads * columns,
        ),
        name="attend",
    )(scalars, *first, lengths, *key_values, fresh_keys, fresh_values)


def ring_hop(array, step, owners):
    size = 2 * owners
    device = [place if place < owners else 3 * owners - 1 - place for place in range(size)]
    pairs = [(device[place], device[(place + step) % size]) for place in range(size)]
    return lax.ppermute(array, ("rep", "dp"), pairs)


def gate(array, *others):
    return lax.optimization_barrier((array, others))[0]


def ring_step(before, after, owners):
    return ring_hop(before, 1, owners), ring_hop(after, -1, owners)


def split_rows(before, after):
    rows, columns = before.shape
    cut = rows * 3 // 4

    def kernel(before_ref, after_ref, first_ref, last_ref):
        first_ref[...] = before_ref[...]
        last_ref[...] = after_ref[...]

    return pl.pallas_call(
        kernel,
        out_shape=[
            jax.ShapeDtypeStruct((cut, columns), before.dtype),
            jax.ShapeDtypeStruct((rows - cut, columns), before.dtype),
        ],
        grid=(1,),
        in_specs=[
            pl.BlockSpec((cut, columns), lambda g: (0, 0)),
            pl.BlockSpec((rows - cut, columns), lambda g: (3, 0)),
        ],
        out_specs=[
            pl.BlockSpec((cut, columns), lambda g: (0, 0)),
            pl.BlockSpec((rows - cut, columns), lambda g: (0, 0)),
        ],
        compiler_params=pltpu.CompilerParams(vmem_limit_bytes=VMEM_LIMIT),
        cost_estimate=pl.CostEstimate(
            flops=0, bytes_accessed=4 * rows * columns, transcendentals=0
        ),
        name="split",
    )(before, after)


def body(
    tokens,
    query_weight,
    adapter_down_weight,
    adapter_up_weight,
    cached_key_rows,
    cached_value_rows,
    incoming_key_rows,
    incoming_value_rows,
    cached_length_rows,
    row_adapter_index,
):
    steps, rows, features = tokens.shape
    width = query_weight.shape[1]
    positions, head_size = cached_key_rows.shape[2:]
    count = lax.axis_size("tensor")
    owners = lax.axis_size("dp")
    me = lax.axis_index("tensor")
    owner = lax.axis_index("dp")
    replica = lax.axis_index("rep")
    adapters, _, rank = adapter_down_weight.shape
    half = adapters // 2
    flat_tokens = tokens.reshape(steps * rows, features)

    row_adapters = jnp.tile(row_adapter_index, steps).reshape(steps * rows, 1)

    down_rows = jnp.swapaxes(adapter_down_weight, 1, 2).reshape(adapters * rank, features)
    up_rows = adapter_up_weight.reshape(adapters * rank, width)
    own_down = lax.dynamic_slice_in_dim(down_rows, replica * half * rank, half * rank, axis=0)
    own_up = lax.dynamic_slice_in_dim(up_rows, replica * half * rank, half * rank, axis=0)

    size = 2 * owners
    place = jnp.where(replica == 0, owner, size - 1 - owner)
    start = []
    for step in [0] + [d for k in range(1, owners) for d in (-k, k)] + [owners]:
        other = lax.rem(place + step + size, size)
        start.append(
            jnp.where(other < owners, other * adapters, (size - 1 - other) * adapters + half)
        )
    starts = jnp.stack(start).astype(jnp.int32)

    key_heads = jnp.transpose(cached_key_rows, (1, 0, 2, 3)).reshape(KVH, rows * positions, head_size)
    value_heads = jnp.transpose(cached_value_rows, (1, 0, 2, 3)).reshape(
        KVH, rows * positions, head_size
    )
    both = jnp.stack([key_heads, value_heads], axis=1)

    paired = count == 4
    down = [ring_step(own_down, own_down, owners)]
    if paired:
        ids = jnp.stack([me ^ j for j in range(count)]).astype(jnp.int32)
        far = swap(flat_tokens, 2, count)
        near = swap(flat_tokens, 1, count)
        parcels = lax.optimization_barrier(
            [lax.dynamic_index_in_dim(both, ids[j], 0, keepdims=False) for j in range(count)]
        )
        base = project_pair(ids[:2], [flat_tokens], [near], query_weight)
        waits = {2: [near, parcels, base]}
    else:
        all_tokens = lax.all_gather(flat_tokens, "tensor", axis=1, tiled=True)
        base = jnp.dot(all_tokens, query_weight, preferred_element_type=jnp.float32)
        ids = jnp.arange(count, dtype=jnp.int32)
        gathered = lax.all_to_all(
            jnp.repeat(both, count // KVH, axis=0),
            "tensor",
            split_axis=0,
            concat_axis=0,
            tiled=True,
        )
        key_values = [gathered[b] for b in range(count)]
        waits = {}
    early = 1 + 2 * (owners - 2)
    for k in range(2, owners):
        down.append(ring_step(*gate(down[-1], *waits.get(k, [])), owners))
    groups = [[own_down]] + [[part] for pair in down[: owners - 2] for part in pair]
    ranks = add_ranks(starts[:early], flat_tokens, row_adapters, groups, rank)
    if paired:
        far = gate(far, down[owners - 3])
        far_near = swap(far, 1, count)
        second = swap(gate(parcels[2], far), 2, count)
        third = swap(gate(parcels[3], second), 3, count)
        base = project_pair(ids[2:], [far], [far_near], query_weight, base)
    before, after = gate(down[-1], ranks)
    parts = split_rows(before, after)
    down.append(ring_step(*parts, owners))

    from_after = [ring_hop(gate(own_up, *(down[owners - 3] + (far,) if paired else [])), -1, owners)]
    from_before = [ring_hop(gate(own_up, *parts), 1, owners)]
    if paired:
        first = swap(gate(parcels[1], from_after[0]), 1, count)
        key_values = [parcels[0], first, second, third]
    groups = [[part] for part in down[owners - 2]] + [list(down[owners - 1])]
    ranks = add_ranks(
        starts[early:], flat_tokens, row_adapters, groups, rank, earlier=ranks, last=True
    )
    for k in range(2, owners + 1):
        from_after.append(ring_hop(gate(from_after[-1], *(down[-1] if k == 2 else [])), -1, owners))
    bits = [1 << i for i in range((count - 1).bit_length())]
    ranks = ranks + swap(ranks, bits[0], count)
    for k in range(2, owners):
        wait = [ranks] + ([third, base] if paired else []) if k == owners - 1 else []
        from_before.append(ring_hop(gate(from_before[-1], *wait), 1, owners))
    for bit in bits[1:]:
        ranks = ranks + swap(ranks, bit, count)
    up = [part for pair in zip(from_before, from_after) for part in pair] + [from_after[-1]]
    groups = [[own_up]] + [[part] for part in up[: early - 1]]
    query = early_query(starts[:early], base, ranks, row_adapters, groups)
    groups = [[part] for part in up[early - 1 :]]

    kv_head = me * KVH // count
    fresh_keys = lax.dynamic_index_in_dim(incoming_key_rows, kv_head, 2, keepdims=False)
    fresh_values = lax.dynamic_index_in_dim(incoming_value_rows, kv_head, 2, keepdims=False)
    return attend(
        jnp.concatenate([starts[early:], ids]),
        query,
        ranks,
        row_adapters,
        groups,
        cached_length_rows.reshape(rows, 1),
        key_values,
        fresh_keys,
        fresh_values,
    )


def solution(mesh):
    in_specs = (
        P(None, ("rep", "dp"), "tensor"),
        P(None, "tensor"),
        P("dp", "tensor", None),
        P("dp", None, "tensor"),
        P(("rep", "dp"), None, "tensor", None),
        P(("rep", "dp"), None, "tensor", None),
        P(None, ("rep", "dp"), None, None),
        P(None, ("rep", "dp"), None, None),
        P(("rep", "dp")),
        P(("rep", "dp")),
    )
    out_specs = P(None, ("rep", "dp"), "tensor")
    return jax.shard_map(body, mesh=mesh, in_specs=in_specs, out_specs=out_specs, check_vma=False)
```

```python
import jax
import jax.numpy as jnp
from jax import lax
from jax.experimental import pallas as pl
from jax.experimental.pallas import tpu as pltpu
from jax.sharding import PartitionSpec as P

KVH = 4
VMEM_LIMIT = 56 * 1024 * 1024


def swap(array, bit, count):
    return lax.ppermute(array, "tensor", [(i, i ^ bit) for i in range(count)])


def project_pair(tensor_ids, first, second, weight, earlier=None):
    depth = first[0].shape[1]
    rows = sum(part.shape[0] for part in first)
    columns = weight.shape[1]
    chunk = 512
    chunks = depth // chunk
    parts = len(first)

    def kernel(ids_ref, *refs):
        first_weight, second_weight = refs[2 * parts : 2 * parts + 2]
        out_ref = refs[-1]
        left = jnp.concatenate([ref[...] for ref in refs[:parts]], axis=0)
        right = jnp.concatenate([ref[...] for ref in refs[parts : 2 * parts]], axis=0)
        product = jnp.dot(
            jnp.concatenate([left, right], axis=1),
            jnp.concatenate([first_weight[...], second_weight[...]], axis=0),
            preferred_element_type=jnp.float32,
        )

        @pl.when(pl.program_id(0) == 0)
        def _():
            out_ref[...] = product if earlier is None else product + refs[2 * parts + 2][...]

        @pl.when(pl.program_id(0) > 0)
        def _():
            out_ref[...] += product

    whole = pl.BlockSpec((rows, columns), lambda k, ids: (0, 0))
    in_specs = [
        pl.BlockSpec((part.shape[0], chunk), lambda k, ids: (0, k)) for part in first + second
    ] + [
        pl.BlockSpec((chunk, columns), lambda k, ids: (ids[0] * chunks + k, 0)),
        pl.BlockSpec((chunk, columns), lambda k, ids: (ids[1] * chunks + k, 0)),
    ]
    operands = first + second + [weight, weight]
    if earlier is not None:
        in_specs.append(whole)
        operands.append(earlier)
    return pl.pallas_call(
        kernel,
        out_shape=jax.ShapeDtypeStruct((rows, columns), jnp.float32),
        grid_spec=pltpu.PrefetchScalarGridSpec(
            num_scalar_prefetch=1, grid=(chunks,), in_specs=in_specs, out_specs=whole
        ),
        compiler_params=pltpu.CompilerParams(vmem_limit_bytes=VMEM_LIMIT),
        cost_estimate=pl.CostEstimate(
            flops=4 * rows * depth * columns,
            bytes_accessed=4 * depth * (rows + columns) + 4 * rows * columns,
            transcendentals=0,
        ),
        name="project",
    )(tensor_ids, *operands)


def add_ranks(starts, tokens, row_adapters, groups, rank, earlier=None, last=False):
    rows, depth = tokens.shape
    width = sum(part.shape[0] for part in groups[0])
    sizes = [len(group) for group in groups]
    flat = [part for group in groups for part in group]

    def kernel(starts_ref, tokens_ref, adapter_ref, *refs):
        out_ref = refs[-1]
        lane = lax.broadcasted_iota(jnp.int32, (rows, width), 1) // rank
        total = jnp.zeros((rows, width), jnp.float32) if earlier is None else refs[-2][...]
        used = 0
        for i, size in enumerate(sizes):
            down = jnp.concatenate([ref[...] for ref in refs[used : used + size]], axis=0)
            used += size
            product = lax.dot_general(
                tokens_ref[...],
                down,
                (((1,), (1,)), ((), ())),
                preferred_element_type=jnp.float32,
            )
            total = total + jnp.where(lane + starts_ref[i] == adapter_ref[...], product, 0.0)
        if last:
            folded = total[:, :128]
            for i in range(1, width // 128):
                folded = folded + total[:, i * 128 : (i + 1) * 128]
            out_ref[...] = folded[:, :rank] + folded[:, rank:]
        else:
            out_ref[...] = total

    out_width = rank if last else width
    operands = [tokens, row_adapters] + flat + ([] if earlier is None else [earlier])
    return pl.pallas_call(
        kernel,
        out_shape=jax.ShapeDtypeStruct((rows, out_width), jnp.float32),
        grid_spec=pltpu.PrefetchScalarGridSpec(
            num_scalar_prefetch=1,
            grid=(1,),
            in_specs=[pl.BlockSpec(op.shape, lambda g, starts: (0, 0)) for op in operands],
            out_specs=pl.BlockSpec((rows, out_width), lambda g, starts: (0, 0)),
        ),
        compiler_params=pltpu.CompilerParams(vmem_limit_bytes=VMEM_LIMIT),
        cost_estimate=pl.CostEstimate(
            flops=2 * rows * depth * width * len(groups),
            bytes_accessed=2 * depth * (rows + width * len(groups)),
            transcendentals=0,
        ),
        name="rank",
    )(starts, *operands)


def part_delta(starts_ref, ranks, held, up_refs, sizes):
    rows, rank = ranks.shape
    width = sum(ref.shape[0] for ref in up_refs[: sizes[0]])
    lane = lax.broadcasted_iota(jnp.int32, (rows, width), 1) // rank
    wide = jnp.concatenate([ranks] * (width // rank), axis=1)
    kept = [
        jnp.where(lane + starts_ref[i] == held, wide, 0.0).astype(jnp.bfloat16)
        for i in range(len(sizes))
    ]
    return jnp.dot(
        jnp.concatenate(kept, axis=1),
        jnp.concatenate([ref[...] for ref in up_refs], axis=0),
        preferred_element_type=jnp.float32,
    )


def early_query(starts, base, ranks, row_adapters, groups):
    rows, columns = base.shape
    sizes = [len(group) for group in groups]
    flat = [part for group in groups for part in group]
    depth = sum(part.shape[0] for part in flat)

    def kernel(starts_ref, base_ref, rank_ref, adapter_ref, *refs):
        delta = part_delta(starts_ref, rank_ref[...], adapter_ref[...], refs[:-1], sizes)
        refs[-1][...] = base_ref[...] + delta.astype(jnp.bfloat16).astype(jnp.float32)

    operands = [base, ranks, row_adapters] + flat
    return pl.pallas_call(
        kernel,
        out_shape=jax.ShapeDtypeStruct((rows, columns), jnp.float32),
        grid_spec=pltpu.PrefetchScalarGridSpec(
            num_scalar_prefetch=1,
            grid=(1,),
            in_specs=[pl.BlockSpec(op.shape, lambda g, starts: (0, 0)) for op in operands],
            out_specs=pl.BlockSpec((rows, columns), lambda g, starts: (0, 0)),
        ),
        compiler_params=pltpu.CompilerParams(vmem_limit_bytes=VMEM_LIMIT),
        cost_estimate=pl.CostEstimate(
            flops=2 * rows * columns * depth,
            bytes_accessed=8 * columns * rows + 2 * columns * depth,
            transcendentals=0,
        ),
        name="delta",
    )(starts, *operands)


def attend(
    scalars, query, ranks, row_adapters, groups, lengths, key_values, fresh_keys, fresh_values
):
    steps, rows, head_size = fresh_keys.shape
    width = query.shape[1]
    heads = width // head_size
    blocks = len(key_values)
    sizes = [len(group) for group in groups]
    ups = [part for group in groups for part in group]
    positions = key_values[0].shape[1] // rows
    bundle = 32
    sub = 4 if 4 * positions % 16 == 0 and heads % 2 == 0 else 16
    slab = max(sub, 8)
    pack = slab // sub
    span = sub * positions
    cached = blocks * span
    fresh = steps * slab
    columns = -(-(cached + fresh) // 128) * 128
    scale = head_size ** (-0.5)

    def kernel(scalars_ref, *refs):
        given_ref, rank_ref, adapter_ref = refs[:3]
        up_refs = refs[3 : 3 + len(ups)]
        length_ref = refs[3 + len(ups)]
        cache_refs = refs[4 + len(ups) : 4 + len(ups) + blocks]
        fresh_key_ref, fresh_value_ref, out_ref, query_ref = refs[4 + len(ups) + blocks :]
        step = pl.program_id(0)

        @pl.when(step == 0)
        def _():
            delta = part_delta(scalars_ref, rank_ref[...], adapter_ref[...], up_refs, sizes)
            rounded = (given_ref[...] + delta.astype(jnp.bfloat16).astype(jnp.float32)).astype(
                jnp.bfloat16
            )
            query_ref[...] = rounded.astype(jnp.float32)

        column = lax.broadcasted_iota(jnp.int32, (slab, columns), 1)
        own = lax.broadcasted_iota(jnp.int32, (slab, columns), 0) % sub
        on_row = (column % span) // positions == own
        place = jnp.full((slab, columns), 1 << 20, jnp.int32)
        for b in range(blocks):
            here = (column >= b * span) & (column < (b + 1) * span)
            place = jnp.where(
                here & on_row, column % positions + scalars_ref[len(sizes) + b] * positions, place
            )
        fresh_step = (column - cached) // slab
        fresh_row = (column - cached) % slab
        is_fresh = (column >= cached) & (column < cached + fresh)
        padding = jnp.zeros((columns - cached - fresh, head_size), jnp.bfloat16)
        ones = jnp.ones((columns, head_size), jnp.bfloat16)
        fresh_key_all = fresh_key_ref[...].astype(jnp.float32)
        fresh_value_all = fresh_value_ref[...].astype(jnp.float32)
        scores, values, seen = [], [], []
        for first in range(0, bundle, slab):
            begin = pl.multiple_of(step * bundle + first, slab)
            slabs = [
                [
                    query_ref[pl.ds(s * rows + begin, slab), h * head_size : (h + 1) * head_size]
                    for h in range(heads)
                ]
                for s in range(steps)
            ]
            new = slice(first, first + slab)
            new_keys = jnp.concatenate(
                [fresh_key_all[t, new] for t in range(steps)], axis=0
            ).astype(jnp.bfloat16)
            new_values = jnp.concatenate(
                [fresh_value_all[t, new] for t in range(steps)], axis=0
            ).astype(jnp.bfloat16)
            length_all = length_ref[new]
            for part in range(pack):
                mine = slice(part * sub, (part + 1) * sub)
                there = slice((first + part * sub) * positions, (first + (part + 1) * sub) * positions)
                queries = jnp.concatenate(
                    [slabs[s][h][mine] for s in range(steps) for h in range(heads)], axis=0
                ).astype(jnp.bfloat16)
                keys = jnp.concatenate(
                    [ref[0, there, :] for ref in cache_refs] + [new_keys, padding], axis=0
                )
                own_values = jnp.concatenate(
                    [ref[1, there, :] for ref in cache_refs] + [new_values, padding], axis=0
                )
                values.append(jnp.concatenate([own_values, ones], axis=1))
                scores.append(
                    lax.dot_general(
                        queries, keys, (((1,), (1,)), ((), ())), preferred_element_type=jnp.float32
                    ).reshape(steps, heads // pack, slab, columns)
                )
                length = jnp.concatenate([length_all[mine]] * pack, axis=0)
                cached_seen = place < length
                fresh_seen = is_fresh & (fresh_row == own + part * sub)
                seen.append(
                    [
                        jnp.where(cached_seen | (fresh_seen & (fresh_step <= s)), 0.0, -1e30)
                        for s in range(steps)
                    ]
                )
        shifted = [
            [score[s] * scale + bias[s][None] for s in range(steps)]
            for score, bias in zip(scores, seen)
        ]
        top = [[jnp.max(part, axis=-1, keepdims=True) for part in parts] for parts in shifted]
        raised = [
            jnp.concatenate(
                [
                    jnp.exp(part - most).reshape(heads // pack * slab, columns)
                    for part, most in zip(parts, tops)
                ],
                axis=0,
            ).astype(jnp.bfloat16)
            for parts, tops in zip(shifted, top)
        ]
        sums = [
            jnp.dot(weights, value, preferred_element_type=jnp.float32)
            for weights, value in zip(raised, values)
        ]
        outputs = [both[:, :head_size] / both[:, head_size:] for both in sums]
        for s in range(steps):
            for h in range(heads):
                start = (s * heads + h) * sub
                out_ref[s, :, h * head_size : (h + 1) * head_size] = jnp.concatenate(
                    [out[start : start + sub] for out in outputs], axis=0
                ).astype(jnp.bfloat16)

    def whole(array):
        return pl.BlockSpec(array.shape, lambda g, scalars: (0,) * array.ndim)

    cache_spec = pl.BlockSpec((2, bundle * positions, head_size), lambda g, scalars: (0, g, 0))
    fresh_spec = pl.BlockSpec((steps, bundle, head_size), lambda g, scalars: (0, g, 0))
    wide_spec = pl.BlockSpec((steps, bundle, width), lambda g, scalars: (0, g, 0))
    first = [query, ranks, row_adapters, *ups]
    return pl.pallas_call(
        kernel,
        out_shape=jax.ShapeDtypeStruct((steps, rows, width), jnp.bfloat16),
        grid_spec=pltpu.PrefetchScalarGridSpec(
            num_scalar_prefetch=1,
            grid=(rows // bundle,),
            in_specs=[whole(op) for op in first]
            + [pl.BlockSpec((bundle, 1), lambda g, scalars: (g, 0))]
            + [cache_spec] * blocks
            + [fresh_spec] * 2,
            out_specs=wide_spec,
            scratch_shapes=[pltpu.VMEM((steps * rows, width), jnp.float32)],
        ),
        compiler_params=pltpu.CompilerParams(vmem_limit_bytes=VMEM_LIMIT),
        cost_estimate=pl.CostEstimate(
            flops=4 * steps * rows * width * sub * (blocks * positions + steps),
            bytes_accessed=4 * steps * rows * width + 4 * blocks * rows * positions * head_size,
            transcendentals=steps * rows * heads * columns,
        ),
        name="attend",
    )(scalars, *first, lengths, *key_values, fresh_keys, fresh_values)


def ring_hop(array, step, owners):
    size = 2 * owners
    device = [place if place < owners else 3 * owners - 1 - place for place in range(size)]
    pairs = [(device[place], device[(place + step) % size]) for place in range(size)]
    return lax.ppermute(array, ("rep", "dp"), pairs)


def gate(array, *others):
    return lax.optimization_barrier((array, others))[0]


def ring_step(before, after, owners):
    return ring_hop(before, 1, owners), ring_hop(after, -1, owners)


def split_rows(before, after):
    rows, columns = before.shape
    cut = rows * 3 // 4

    def kernel(before_ref, after_ref, first_ref, last_ref):
        first_ref[...] = before_ref[...]
        last_ref[...] = after_ref[...]

    return pl.pallas_call(
        kernel,
        out_shape=[
            jax.ShapeDtypeStruct((cut, columns), before.dtype),
            jax.ShapeDtypeStruct((rows - cut, columns), before.dtype),
        ],
        grid=(1,),
        in_specs=[
            pl.BlockSpec((cut, columns), lambda g: (0, 0)),
            pl.BlockSpec((rows - cut, columns), lambda g: (3, 0)),
        ],
        out_specs=[
            pl.BlockSpec((cut, columns), lambda g: (0, 0)),
            pl.BlockSpec((rows - cut, columns), lambda g: (0, 0)),
        ],
        compiler_params=pltpu.CompilerParams(vmem_limit_bytes=VMEM_LIMIT),
        cost_estimate=pl.CostEstimate(
            flops=0, bytes_accessed=4 * rows * columns, transcendentals=0
        ),
        name="split",
    )(before, after)


def body(
    tokens,
    query_weight,
    adapter_down_weight,
    adapter_up_weight,
    cached_key_rows,
    cached_value_rows,
    incoming_key_rows,
    incoming_value_rows,
    cached_length_rows,
    row_adapter_index,
):
    steps, rows, features = tokens.shape
    width = query_weight.shape[1]
    positions, head_size = cached_key_rows.shape[2:]
    count = lax.axis_size("tensor")
    owners = lax.axis_size("dp")
    me = lax.axis_index("tensor")
    owner = lax.axis_index("dp")
    replica = lax.axis_index("rep")
    adapters, _, rank = adapter_down_weight.shape
    half = adapters // 2
    flat_tokens = tokens.reshape(steps * rows, features)

    row_adapters = jnp.tile(row_adapter_index, steps).reshape(steps * rows, 1)

    down_rows = jnp.swapaxes(adapter_down_weight, 1, 2).reshape(adapters * rank, features)
    up_rows = adapter_up_weight.reshape(adapters * rank, width)
    own_down = lax.dynamic_slice_in_dim(down_rows, replica * half * rank, half * rank, axis=0)
    own_up = lax.dynamic_slice_in_dim(up_rows, replica * half * rank, half * rank, axis=0)

    size = 2 * owners
    place = jnp.where(replica == 0, owner, size - 1 - owner)
    start = []
    for step in [0] + [d for k in range(1, owners) for d in (-k, k)] + [owners]:
        other = lax.rem(place + step + size, size)
        start.append(
            jnp.where(other < owners, other * adapters, (size - 1 - other) * adapters + half)
        )
    starts = jnp.stack(start).astype(jnp.int32)

    key_heads = jnp.transpose(cached_key_rows, (1, 0, 2, 3)).reshape(KVH, rows * positions, head_size)
    value_heads = jnp.transpose(cached_value_rows, (1, 0, 2, 3)).reshape(
        KVH, rows * positions, head_size
    )
    both = jnp.stack([key_heads, value_heads], axis=1)

    paired = count == 4
    down = [ring_step(own_down, own_down, owners)]
    if paired:
        ids = jnp.stack([me ^ j for j in range(count)]).astype(jnp.int32)
        far = swap(flat_tokens, 2, count)
        near = swap(flat_tokens, 1, count)
        parcels = lax.optimization_barrier(
            [lax.dynamic_index_in_dim(both, ids[j], 0, keepdims=False) for j in range(count)]
        )
        base = project_pair(ids[:2], [flat_tokens], [near], query_weight)
        waits = {2: [near, parcels, base]}
    else:
        all_tokens = lax.all_gather(flat_tokens, "tensor", axis=1, tiled=True)
        base = jnp.dot(all_tokens, query_weight, preferred_element_type=jnp.float32)
        ids = jnp.arange(count, dtype=jnp.int32)
        gathered = lax.all_to_all(
            jnp.repeat(both, count // KVH, axis=0),
            "tensor",
            split_axis=0,
            concat_axis=0,
            tiled=True,
        )
        key_values = [gathered[b] for b in range(count)]
        waits = {}
    early = 1 + 2 * (owners - 2)
    for k in range(2, owners):
        down.append(ring_step(*gate(down[-1], *waits.get(k, [])), owners))
    groups = [[own_down]] + [[part] for pair in down[: owners - 2] for part in pair]
    ranks = add_ranks(starts[:early], flat_tokens, row_adapters, groups, rank)
    if paired:
        far = gate(far, down[owners - 3])
        far_near = swap(far, 1, count)
        second = swap(gate(parcels[2], far), 2, count)
        third = swap(gate(parcels[3], second), 3, count)
        base = project_pair(ids[2:], [far], [far_near], query_weight, base)
    before, after = gate(down[-1], ranks)
    parts = split_rows(before, after)
    down.append(ring_step(*parts, owners))

    from_after = [ring_hop(gate(own_up, *(down[owners - 3] + (far,) if paired else [])), -1, owners)]
    from_before = [ring_hop(gate(own_up, *parts), 1, owners)]
    if paired:
        first = swap(gate(parcels[1], from_after[0]), 1, count)
        key_values = [parcels[0], first, second, third]
    groups = [[part] for part in down[owners - 2]] + [list(down[owners - 1])]
    ranks = add_ranks(
        starts[early:], flat_tokens, row_adapters, groups, rank, earlier=ranks, last=True
    )
    for k in range(2, owners + 1):
        from_after.append(ring_hop(gate(from_after[-1], *([down[-1], base] if k == 2 else [])), -1, owners))
    bits = [1 << i for i in range((count - 1).bit_length())]
    for k in range(2, owners):
        if k == owners - 1:
            for bit in bits:
                ranks = ranks + swap(ranks, bit, count)
        wait = [ranks] + ([third] if paired and k == owners - 1 else [])
        from_before.append(ring_hop(gate(from_before[-1], *wait), 1, owners))
    up = [part for pair in zip(from_before, from_after) for part in pair] + [from_after[-1]]
    groups = [[own_up]] + [[part] for part in up[: early - 1]]
    query = early_query(starts[:early], base, ranks, row_adapters, groups)
    groups = [[part] for part in up[early - 1 :]]

    kv_head = me * KVH // count
    fresh_keys = lax.dynamic_index_in_dim(incoming_key_rows, kv_head, 2, keepdims=False)
    fresh_values = lax.dynamic_index_in_dim(incoming_value_rows, kv_head, 2, keepdims=False)
    return attend(
        jnp.concatenate([starts[early:], ids]),
        query,
        ranks,
        row_adapters,
        groups,
        cached_length_rows.reshape(rows, 1),
        key_values,
        fresh_keys,
        fresh_values,
    )


def solution(mesh):
    in_specs = (
        P(None, ("rep", "dp"), "tensor"),
        P(None, "tensor"),
        P("dp", "tensor", None),
        P("dp", None, "tensor"),
        P(("rep", "dp"), None, "tensor", None),
        P(("rep", "dp"), None, "tensor", None),
        P(None, ("rep", "dp"), None, None),
        P(None, ("rep", "dp"), None, None),
        P(("rep", "dp")),
        P(("rep", "dp")),
    )
    out_specs = P(None, ("rep", "dp"), "tensor")
    return jax.shard_map(body, mesh=mesh, in_specs=in_specs, out_specs=out_specs, check_vma=False)
```

```python
import jax
import jax.numpy as jnp
from jax import lax
from jax.experimental import pallas as pl
from jax.experimental.pallas import tpu as pltpu
from jax.sharding import PartitionSpec as P

KVH = 4
VMEM_LIMIT = 56 * 1024 * 1024


def swap(array, bit, count):
    return lax.ppermute(array, "tensor", [(i, i ^ bit) for i in range(count)])


def project_pair(tensor_ids, first, second, weight, earlier=None):
    depth = first[0].shape[1]
    rows = sum(part.shape[0] for part in first)
    columns = weight.shape[1]
    chunk = 512
    chunks = depth // chunk
    parts = len(first)

    def kernel(ids_ref, *refs):
        first_weight, second_weight = refs[2 * parts : 2 * parts + 2]
        out_ref = refs[-1]
        left = jnp.concatenate([ref[...] for ref in refs[:parts]], axis=0)
        right = jnp.concatenate([ref[...] for ref in refs[parts : 2 * parts]], axis=0)
        product = jnp.dot(
            jnp.concatenate([left, right], axis=1),
            jnp.concatenate([first_weight[...], second_weight[...]], axis=0),
            preferred_element_type=jnp.float32,
        )

        @pl.when(pl.program_id(0) == 0)
        def _():
            out_ref[...] = product if earlier is None else product + refs[2 * parts + 2][...]

        @pl.when(pl.program_id(0) > 0)
        def _():
            out_ref[...] += product

    whole = pl.BlockSpec((rows, columns), lambda k, ids: (0, 0))
    in_specs = [
        pl.BlockSpec((part.shape[0], chunk), lambda k, ids: (0, k)) for part in first + second
    ] + [
        pl.BlockSpec((chunk, columns), lambda k, ids: (ids[0] * chunks + k, 0)),
        pl.BlockSpec((chunk, columns), lambda k, ids: (ids[1] * chunks + k, 0)),
    ]
    operands = first + second + [weight, weight]
    if earlier is not None:
        in_specs.append(whole)
        operands.append(earlier)
    return pl.pallas_call(
        kernel,
        out_shape=jax.ShapeDtypeStruct((rows, columns), jnp.float32),
        grid_spec=pltpu.PrefetchScalarGridSpec(
            num_scalar_prefetch=1, grid=(chunks,), in_specs=in_specs, out_specs=whole
        ),
        compiler_params=pltpu.CompilerParams(vmem_limit_bytes=VMEM_LIMIT),
        cost_estimate=pl.CostEstimate(
            flops=4 * rows * depth * columns,
            bytes_accessed=4 * depth * (rows + columns) + 4 * rows * columns,
            transcendentals=0,
        ),
        name="project",
    )(tensor_ids, *operands)


def add_ranks(starts, tokens, row_adapters, groups, rank, earlier=None, last=False):
    rows, depth = tokens.shape
    width = sum(part.shape[0] for part in groups[0])
    sizes = [len(group) for group in groups]
    flat = [part for group in groups for part in group]

    def kernel(starts_ref, tokens_ref, adapter_ref, *refs):
        out_ref = refs[-1]
        lane = lax.broadcasted_iota(jnp.int32, (rows, width), 1) // rank
        total = jnp.zeros((rows, width), jnp.float32) if earlier is None else refs[-2][...]
        used = 0
        for i, size in enumerate(sizes):
            down = jnp.concatenate([ref[...] for ref in refs[used : used + size]], axis=0)
            used += size
            product = lax.dot_general(
                tokens_ref[...],
                down,
                (((1,), (1,)), ((), ())),
                preferred_element_type=jnp.float32,
            )
            total = total + jnp.where(lane + starts_ref[i] == adapter_ref[...], product, 0.0)
        if last:
            folded = total[:, :128]
            for i in range(1, width // 128):
                folded = folded + total[:, i * 128 : (i + 1) * 128]
            out_ref[...] = folded[:, :rank] + folded[:, rank:]
        else:
            out_ref[...] = total

    out_width = rank if last else width
    operands = [tokens, row_adapters] + flat + ([] if earlier is None else [earlier])
    return pl.pallas_call(
        kernel,
        out_shape=jax.ShapeDtypeStruct((rows, out_width), jnp.float32),
        grid_spec=pltpu.PrefetchScalarGridSpec(
            num_scalar_prefetch=1,
            grid=(1,),
            in_specs=[pl.BlockSpec(op.shape, lambda g, starts: (0, 0)) for op in operands],
            out_specs=pl.BlockSpec((rows, out_width), lambda g, starts: (0, 0)),
        ),
        compiler_params=pltpu.CompilerParams(vmem_limit_bytes=VMEM_LIMIT),
        cost_estimate=pl.CostEstimate(
            flops=2 * rows * depth * width * len(groups),
            bytes_accessed=2 * depth * (rows + width * len(groups)),
            transcendentals=0,
        ),
        name="rank",
    )(starts, *operands)


def part_delta(starts_ref, ranks, held, up_refs, sizes):
    rows, rank = ranks.shape
    width = sum(ref.shape[0] for ref in up_refs[: sizes[0]])
    lane = lax.broadcasted_iota(jnp.int32, (rows, width), 1) // rank
    wide = jnp.concatenate([ranks] * (width // rank), axis=1)
    kept = [
        jnp.where(lane + starts_ref[i] == held, wide, 0.0).astype(jnp.bfloat16)
        for i in range(len(sizes))
    ]
    return jnp.dot(
        jnp.concatenate(kept, axis=1),
        jnp.concatenate([ref[...] for ref in up_refs], axis=0),
        preferred_element_type=jnp.float32,
    )


def early_query(starts, base, ranks, row_adapters, groups):
    rows, columns = base.shape
    sizes = [len(group) for group in groups]
    flat = [part for group in groups for part in group]
    depth = sum(part.shape[0] for part in flat)

    def kernel(starts_ref, base_ref, rank_ref, adapter_ref, *refs):
        delta = part_delta(starts_ref, rank_ref[...], adapter_ref[...], refs[:-1], sizes)
        refs[-1][...] = base_ref[...] + delta.astype(jnp.bfloat16).astype(jnp.float32)

    operands = [base, ranks, row_adapters] + flat
    return pl.pallas_call(
        kernel,
        out_shape=jax.ShapeDtypeStruct((rows, columns), jnp.float32),
        grid_spec=pltpu.PrefetchScalarGridSpec(
            num_scalar_prefetch=1,
            grid=(1,),
            in_specs=[pl.BlockSpec(op.shape, lambda g, starts: (0, 0)) for op in operands],
            out_specs=pl.BlockSpec((rows, columns), lambda g, starts: (0, 0)),
        ),
        compiler_params=pltpu.CompilerParams(vmem_limit_bytes=VMEM_LIMIT),
        cost_estimate=pl.CostEstimate(
            flops=2 * rows * columns * depth,
            bytes_accessed=8 * columns * rows + 2 * columns * depth,
            transcendentals=0,
        ),
        name="delta",
    )(starts, *operands)


def attend(
    scalars, query, ranks, row_adapters, groups, lengths, key_values, fresh_keys, fresh_values
):
    steps, rows, head_size = fresh_keys.shape
    width = query.shape[1]
    heads = width // head_size
    blocks = len(key_values)
    sizes = [len(group) for group in groups]
    ups = [part for group in groups for part in group]
    positions = key_values[0].shape[1] // rows
    bundle = 64
    sub = 4 if 4 * positions % 16 == 0 and heads % 2 == 0 else 16
    slab = max(sub, 8)
    pack = slab // sub
    span = sub * positions
    cached = blocks * span
    fresh = steps * slab
    columns = -(-(cached + fresh) // 128) * 128
    scale = head_size ** (-0.5)

    def kernel(scalars_ref, *refs):
        given_ref, rank_ref, adapter_ref = refs[:3]
        up_refs = refs[3 : 3 + len(ups)]
        length_ref = refs[3 + len(ups)]
        cache_refs = refs[4 + len(ups) : 4 + len(ups) + blocks]
        fresh_key_ref, fresh_value_ref, out_ref, query_ref = refs[4 + len(ups) + blocks :]
        step = pl.program_id(0)

        @pl.when(step == 0)
        def _():
            delta = part_delta(scalars_ref, rank_ref[...], adapter_ref[...], up_refs, sizes)
            rounded = (given_ref[...] + delta.astype(jnp.bfloat16).astype(jnp.float32)).astype(
                jnp.bfloat16
            )
            query_ref[...] = rounded.astype(jnp.float32)

        column = lax.broadcasted_iota(jnp.int32, (slab, columns), 1)
        own = lax.broadcasted_iota(jnp.int32, (slab, columns), 0) % sub
        on_row = (column % span) // positions == own
        place = jnp.full((slab, columns), 1 << 20, jnp.int32)
        for b in range(blocks):
            here = (column >= b * span) & (column < (b + 1) * span)
            place = jnp.where(
                here & on_row, column % positions + scalars_ref[len(sizes) + b] * positions, place
            )
        fresh_step = (column - cached) // slab
        fresh_row = (column - cached) % slab
        is_fresh = (column >= cached) & (column < cached + fresh)
        padding = jnp.zeros((columns - cached - fresh, head_size), jnp.bfloat16)
        ones = jnp.ones((columns, head_size), jnp.bfloat16)
        fresh_key_all = fresh_key_ref[...].astype(jnp.float32)
        fresh_value_all = fresh_value_ref[...].astype(jnp.float32)
        scores, values, seen = [], [], []
        for first in range(0, bundle, slab):
            begin = pl.multiple_of(step * bundle + first, slab)
            slabs = [
                [
                    query_ref[pl.ds(s * rows + begin, slab), h * head_size : (h + 1) * head_size]
                    for h in range(heads)
                ]
                for s in range(steps)
            ]
            new = slice(first, first + slab)
            new_keys = jnp.concatenate(
                [fresh_key_all[t, new] for t in range(steps)], axis=0
            ).astype(jnp.bfloat16)
            new_values = jnp.concatenate(
                [fresh_value_all[t, new] for t in range(steps)], axis=0
            ).astype(jnp.bfloat16)
            length_all = length_ref[new]
            for part in range(pack):
                mine = slice(part * sub, (part + 1) * sub)
                there = slice((first + part * sub) * positions, (first + (part + 1) * sub) * positions)
                queries = jnp.concatenate(
                    [slabs[s][h][mine] for s in range(steps) for h in range(heads)], axis=0
                ).astype(jnp.bfloat16)
                keys = jnp.concatenate(
                    [ref[0, there, :] for ref in cache_refs] + [new_keys, padding], axis=0
                )
                own_values = jnp.concatenate(
                    [ref[1, there, :] for ref in cache_refs] + [new_values, padding], axis=0
                )
                values.append(jnp.concatenate([own_values, ones], axis=1))
                scores.append(
                    lax.dot_general(
                        queries, keys, (((1,), (1,)), ((), ())), preferred_element_type=jnp.float32
                    ).reshape(steps, heads // pack, slab, columns)
                )
                length = jnp.concatenate([length_all[mine]] * pack, axis=0)
                cached_seen = place < length
                fresh_seen = is_fresh & (fresh_row == own + part * sub)
                seen.append(
                    [
                        jnp.where(cached_seen | (fresh_seen & (fresh_step <= s)), 0.0, -1e30)
                        for s in range(steps)
                    ]
                )
        shifted = [
            [score[s] * scale + bias[s][None] for s in range(steps)]
            for score, bias in zip(scores, seen)
        ]
        top = [[jnp.max(part, axis=-1, keepdims=True) for part in parts] for parts in shifted]
        raised = [
            jnp.concatenate(
                [
                    jnp.exp(part - most).reshape(heads // pack * slab, columns)
                    for part, most in zip(parts, tops)
                ],
                axis=0,
            ).astype(jnp.bfloat16)
            for parts, tops in zip(shifted, top)
        ]
        sums = [
            jnp.dot(weights, value, preferred_element_type=jnp.float32)
            for weights, value in zip(raised, values)
        ]
        outputs = [both[:, :head_size] / both[:, head_size:] for both in sums]
        for s in range(steps):
            for h in range(heads):
                start = (s * heads + h) * sub
                out_ref[s, :, h * head_size : (h + 1) * head_size] = jnp.concatenate(
                    [out[start : start + sub] for out in outputs], axis=0
                ).astype(jnp.bfloat16)

    def whole(array):
        return pl.BlockSpec(array.shape, lambda g, scalars: (0,) * array.ndim)

    cache_spec = pl.BlockSpec((2, bundle * positions, head_size), lambda g, scalars: (0, g, 0))
    fresh_spec = pl.BlockSpec((steps, bundle, head_size), lambda g, scalars: (0, g, 0))
    wide_spec = pl.BlockSpec((steps, bundle, width), lambda g, scalars: (0, g, 0))
    first = [query, ranks, row_adapters, *ups]
    return pl.pallas_call(
        kernel,
        out_shape=jax.ShapeDtypeStruct((steps, rows, width), jnp.bfloat16),
        grid_spec=pltpu.PrefetchScalarGridSpec(
            num_scalar_prefetch=1,
            grid=(rows // bundle,),
            in_specs=[whole(op) for op in first]
            + [pl.BlockSpec((bundle, 1), lambda g, scalars: (g, 0))]
            + [cache_spec] * blocks
            + [fresh_spec] * 2,
            out_specs=wide_spec,
            scratch_shapes=[pltpu.VMEM((steps * rows, width), jnp.float32)],
        ),
        compiler_params=pltpu.CompilerParams(vmem_limit_bytes=VMEM_LIMIT),
        cost_estimate=pl.CostEstimate(
            flops=4 * steps * rows * width * sub * (blocks * positions + steps),
            bytes_accessed=4 * steps * rows * width + 4 * blocks * rows * positions * head_size,
            transcendentals=steps * rows * heads * columns,
        ),
        name="attend",
    )(scalars, *first, lengths, *key_values, fresh_keys, fresh_values)


def ring_hop(array, step, owners):
    size = 2 * owners
    device = [place if place < owners else 3 * owners - 1 - place for place in range(size)]
    pairs = [(device[place], device[(place + step) % size]) for place in range(size)]
    return lax.ppermute(array, ("rep", "dp"), pairs)


def gate(array, *others):
    return lax.optimization_barrier((array, others))[0]


def ring_step(before, after, owners):
    return ring_hop(before, 1, owners), ring_hop(after, -1, owners)


def split_rows(before, after):
    rows, columns = before.shape
    cut = rows * 3 // 4

    def kernel(before_ref, after_ref, first_ref, last_ref):
        first_ref[...] = before_ref[...]
        last_ref[...] = after_ref[...]

    return pl.pallas_call(
        kernel,
        out_shape=[
            jax.ShapeDtypeStruct((cut, columns), before.dtype),
            jax.ShapeDtypeStruct((rows - cut, columns), before.dtype),
        ],
        grid=(1,),
        in_specs=[
            pl.BlockSpec((cut, columns), lambda g: (0, 0)),
            pl.BlockSpec((rows - cut, columns), lambda g: (3, 0)),
        ],
        out_specs=[
            pl.BlockSpec((cut, columns), lambda g: (0, 0)),
            pl.BlockSpec((rows - cut, columns), lambda g: (0, 0)),
        ],
        compiler_params=pltpu.CompilerParams(vmem_limit_bytes=VMEM_LIMIT),
        cost_estimate=pl.CostEstimate(
            flops=0, bytes_accessed=4 * rows * columns, transcendentals=0
        ),
        name="split",
    )(before, after)


def body(
    tokens,
    query_weight,
    adapter_down_weight,
    adapter_up_weight,
    cached_key_rows,
    cached_value_rows,
    incoming_key_rows,
    incoming_value_rows,
    cached_length_rows,
    row_adapter_index,
):
    steps, rows, features = tokens.shape
    width = query_weight.shape[1]
    positions, head_size = cached_key_rows.shape[2:]
    count = lax.axis_size("tensor")
    owners = lax.axis_size("dp")
    me = lax.axis_index("tensor")
    owner = lax.axis_index("dp")
    replica = lax.axis_index("rep")
    adapters, _, rank = adapter_down_weight.shape
    half = adapters // 2
    flat_tokens = tokens.reshape(steps * rows, features)

    row_adapters = jnp.tile(row_adapter_index, steps).reshape(steps * rows, 1)

    down_rows = jnp.swapaxes(adapter_down_weight, 1, 2).reshape(adapters * rank, features)
    up_rows = adapter_up_weight.reshape(adapters * rank, width)
    own_down = lax.dynamic_slice_in_dim(down_rows, replica * half * rank, half * rank, axis=0)
    own_up = lax.dynamic_slice_in_dim(up_rows, replica * half * rank, half * rank, axis=0)

    size = 2 * owners
    place = jnp.where(replica == 0, owner, size - 1 - owner)
    start = []
    for step in [0] + [d for k in range(1, owners) for d in (-k, k)] + [owners]:
        other = lax.rem(place + step + size, size)
        start.append(
            jnp.where(other < owners, other * adapters, (size - 1 - other) * adapters + half)
        )
    starts = jnp.stack(start).astype(jnp.int32)

    key_heads = jnp.transpose(cached_key_rows, (1, 0, 2, 3)).reshape(KVH, rows * positions, head_size)
    value_heads = jnp.transpose(cached_value_rows, (1, 0, 2, 3)).reshape(
        KVH, rows * positions, head_size
    )
    both = jnp.stack([key_heads, value_heads], axis=1)

    paired = count == 4
    down = [ring_step(own_down, own_down, owners)]
    if paired:
        ids = jnp.stack([me ^ j for j in range(count)]).astype(jnp.int32)
        far = swap(flat_tokens, 2, count)
        near = swap(flat_tokens, 1, count)
        parcels = lax.optimization_barrier(
            [lax.dynamic_index_in_dim(both, ids[j], 0, keepdims=False) for j in range(count)]
        )
        base = project_pair(ids[:2], [flat_tokens], [near], query_weight)
        waits = {2: [near, parcels, base]}
    else:
        all_tokens = lax.all_gather(flat_tokens, "tensor", axis=1, tiled=True)
        base = jnp.dot(all_tokens, query_weight, preferred_element_type=jnp.float32)
        ids = jnp.arange(count, dtype=jnp.int32)
        gathered = lax.all_to_all(
            jnp.repeat(both, count // KVH, axis=0),
            "tensor",
            split_axis=0,
            concat_axis=0,
            tiled=True,
        )
        key_values = [gathered[b] for b in range(count)]
        waits = {}
    early = 1 + 2 * (owners - 2)
    for k in range(2, owners):
        down.append(ring_step(*gate(down[-1], *waits.get(k, [])), owners))
    groups = [[own_down]] + [[part] for pair in down[: owners - 2] for part in pair]
    ranks = add_ranks(starts[:early], flat_tokens, row_adapters, groups, rank)
    if paired:
        far = gate(far, down[owners - 3])
        far_near = swap(far, 1, count)
        second = swap(gate(parcels[2], far), 2, count)
        third = swap(gate(parcels[3], second), 3, count)
        base = project_pair(ids[2:], [far], [far_near], query_weight, base)
    before, after = gate(down[-1], ranks)
    parts = split_rows(before, after)
    down.append(ring_step(*parts, owners))

    from_after = [ring_hop(gate(own_up, *(down[owners - 3] + (far,) if paired else [])), -1, owners)]
    from_before = [ring_hop(gate(own_up, *parts), 1, owners)]
    if paired:
        first = swap(gate(parcels[1], from_after[0]), 1, count)
        key_values = [parcels[0], first, second, third]
    groups = [[part] for part in down[owners - 2]] + [list(down[owners - 1])]
    ranks = add_ranks(
        starts[early:], flat_tokens, row_adapters, groups, rank, earlier=ranks, last=True
    )
    for k in range(2, owners + 1):
        from_after.append(ring_hop(gate(from_after[-1], *(down[-1] if k == 2 else [])), -1, owners))
    bits = [1 << i for i in range((count - 1).bit_length())]
    ranks = ranks + swap(ranks, bits[0], count)
    for k in range(2, owners):
        wait = [ranks] + ([third, base] if paired else []) if k == owners - 1 else []
        from_before.append(ring_hop(gate(from_before[-1], *wait), 1, owners))
    for bit in bits[1:]:
        ranks = ranks + swap(ranks, bit, count)
    up = [part for pair in zip(from_before, from_after) for part in pair] + [from_after[-1]]
    groups = [[own_up]] + [[part] for part in up[: early - 1]]
    query = early_query(starts[:early], base, ranks, row_adapters, groups)
    groups = [[part] for part in up[early - 1 :]]

    kv_head = me * KVH // count
    fresh_keys = lax.dynamic_index_in_dim(incoming_key_rows, kv_head, 2, keepdims=False)
    fresh_values = lax.dynamic_index_in_dim(incoming_value_rows, kv_head, 2, keepdims=False)
    return attend(
        jnp.concatenate([starts[early:], ids]),
        query,
        ranks,
        row_adapters,
        groups,
        cached_length_rows.reshape(rows, 1),
        key_values,
        fresh_keys,
        fresh_values,
    )


def solution(mesh):
    in_specs = (
        P(None, ("rep", "dp"), "tensor"),
        P(None, "tensor"),
        P("dp", "tensor", None),
        P("dp", None, "tensor"),
        P(("rep", "dp"), None, "tensor", None),
        P(("rep", "dp"), None, "tensor", None),
        P(None, ("rep", "dp"), None, None),
        P(None, ("rep", "dp"), None, None),
        P(("rep", "dp")),
        P(("rep", "dp")),
    )
    out_specs = P(None, ("rep", "dp"), "tensor")
    return jax.shard_map(body, mesh=mesh, in_specs=in_specs, out_specs=out_specs, check_vma=False)
```
